32 devices in a mesh: rows: 8 (over z, x), sk: 4 (over y, core).
Axes of the slice: x: 2, y: 2, z: 4, core: 2. Of those that a mesh axis runs over, the one named last changes fastest.
Arguments:
- panel: float32 [64, 262144], P(None, ('rows', 'sk')), may hold values from -200 to 200
- signs: int32 [262144], P(('rows', 'sk')), may hold values from -1 to 1
- sample_device: int32 [4096, 1], replicated, may hold values from 0 to 31; in each aligned block of 128 rows (0 to 127, 128 to 255, ...) at most 4 rows name the same one
- sample_offset: int32 [4096], replicated, may hold values from 0 to 8191
Outputs:
- mixed: float32 [64, 262144], P(None, ('rows', 'sk'))
- r_factor: float32 [64, 64], replicated
- whitened: float32 [64, 4096], P(None, ('rows', 'sk'))
The draws below stay inside these ranges and needn't reach their ends.
Inputs may be any that keep to these rules, and one draw needn't show every extreme that they name: `sample_device`: among the sample positions j * 128 to (j + 1) * 128 - 1 of any j, no device number appears more than 4 times, and some block reaches it.
All inputs are finite; a program needn't handle non-finite values.
Results may differ from the reference program's by a relative error of at most 0.0003.
Values sent between devices are 32-bit elements; how exact they have to be, the bound alone decides.
No kernel may reach another device: no remote copies, remote signals or barrier semaphores. Data moves between devices by JAX's collectives and lax.ppermute only.
A program may use at most 64 MiB of HBM per device.

```python
import math
import jax
import jax.numpy as jnp
import numpy as np
from jax import lax

COLS = 64
ROWS_DEV = 8192
S_DEV = 128
CAP = 4
TOTAL_ROWS = 262144
SAMPLES = 4096
N_ROWS = 8
N_SK = 4


def draw_panel(key, part):
    first_key, second_key, third_key = jax.random.split(key, 3)
    base = jnp.clip(jax.random.normal(first_key, (COLS, TOTAL_ROWS), jnp.float32), -6.0, 6.0)
    shared = 0.6
    row_scale = jnp.exp(jax.random.uniform(second_key, (1, TOTAL_ROWS), jnp.float32) * math.log(10.0))
    col_scale = jnp.exp(jax.random.uniform(third_key, (COLS, 1), jnp.float32) * math.log(10.0))
    return (base + shared * base[:1, :]) * row_scale * col_scale * 0.125


def draw_signs(key, part):
    return (2 * jax.random.randint(key, (TOTAL_ROWS,), 0, 2) - 1).astype(jnp.int32)


def with_ends(array, rng, smallest, largest):
    longest = array.shape.index(max(array.shape))
    spots = []
    for shift in (0, 1):
        where = [jax.random.randint(jax.random.fold_in(rng, axis), (), 0, length) for axis, length in enumerate(array.shape)]
        where[longest] = (where[longest] + shift) % array.shape[longest]
        spots.append(tuple(where))
    return array.at[spots[0]].set(smallest).at[spots[1]].set(largest)


def shared_out(stream_key, own, number, rows, amount, top, limit, lean):
    sequence = jax.random.permutation(stream_key, amount)
    heavy_load, usual = load_shares(amount, rows * top, limit, lean, True), load_shares(amount, rows * top, limit, lean, False)
    places = jnp.arange(amount)

    def named(lengths, rotation):
        used = int((lengths > 0).sum())
        fixed = max(1, used // 4)
        shifted = fixed + (places - fixed + rotation * (used - fixed)) % max(1, amount - fixed)
        return jnp.zeros((amount,), jnp.int32).at[sequence[jnp.where(places < fixed, places, shifted)]].set(jnp.asarray(lengths, jnp.int32))

    lengths = jnp.where(number % 4 == 0, named(heavy_load, number // 4), named(usual, number - number // 4 - 1))
    mixed = jax.random.permutation(jax.random.fold_in(own, 3), amount)
    giver, sink = mixed[0:amount // 2 * 2:2], mixed[1:amount // 2 * 2:2]
    slack = jnp.minimum(lengths[giver] - 1, limit - lengths[sink]) // 2
    slack = jnp.where((giver == sequence[0]) | (sink == sequence[0]) | (lengths[sink] == 0), 0, jnp.maximum(slack, 0))
    shifted = jax.random.randint(jax.random.fold_in(own, 4), (amount // 2,), 0, 1 << 20) % (slack + 1)
    lengths = lengths.at[giver].add(-shifted).at[sink].add(shifted)
    labels = jnp.searchsorted(jnp.cumsum(lengths), jnp.arange(rows * top), side="right").astype(jnp.int32)
    grid = labels.reshape(top, rows).T
    grid = grid[jax.random.permutation(jax.random.fold_in(own, 1), rows)]
    rotation = jax.random.randint(jax.random.fold_in(own, 2), (rows, 1), 0, top)
    return jnp.take_along_axis(grid, (jnp.arange(top)[None, :] + rotation) % top, axis=1)


def load_shares(amount, total, reach, slope, full):
    loads = [(1 << 20) // math.isqrt(grade ** slope) + 1 for grade in range(1, amount + 1)]
    largest = reach if full else min(reach, max(-(-total // amount), total * loads[0] // sum(loads)))
    least = 1 if total - largest >= amount - 1 else 0
    counts, surplus = [largest] + [least] * (amount - 1), total - largest - least * (amount - 1)
    while surplus > 0:
        candidates = [i for i in range(1, amount) if counts[i] < largest] or [i for i in range(1, amount) if counts[i] < reach]
        whole, remaining = sum([loads[i] for i in candidates]), surplus
        for i in candidates:
            addition = min(reach - counts[i], max(1, remaining * loads[i] // whole), surplus)
            counts[i] = counts[i] + addition
            surplus = surplus - addition
    return np.array(counts)


def setup_inputs(seed: int = 0) -> dict:
    arg_keys = jax.random.split(jax.random.key(seed), 5)
    panel = draw_panel(jax.random.fold_in(arg_keys[4], 71), 0)
    signs = draw_signs(jax.random.fold_in(arg_keys[4], 71), 0)
    sample_device_keys = jax.random.split(jax.random.fold_in(arg_keys[2], 1), SAMPLES // S_DEV)
    sample_device_turns = jax.random.permutation(jax.random.fold_in(arg_keys[2], 3), SAMPLES // S_DEV)
    sample_device = jax.vmap(lambda own, number: shared_out(jax.random.fold_in(arg_keys[2], 2), own, number, S_DEV, N_ROWS * N_SK, 1, CAP, 2))(sample_device_keys, sample_device_turns).reshape((SAMPLES, 1))
    sample_offset = with_ends(jax.random.randint(arg_keys[3], (SAMPLES,), 0, ROWS_DEV), jax.random.fold_in(arg_keys[3], 1), 0, ROWS_DEV - 1).astype(jnp.int32)
    return dict(panel=panel, signs=signs, sample_device=sample_device, sample_offset=sample_offset)


def hadamard_table(order_size):
    left_ids = jnp.arange(order_size, dtype=jnp.int32)[:, None]
    right_ids = jnp.arange(order_size, dtype=jnp.int32)[None, :]
    common = jnp.bitwise_and(left_ids, right_ids)
    parity = jnp.zeros((order_size, order_size), jnp.int32)
    for bit_number in range(max(order_size.bit_length() - 1, 1)):
        parity = parity + jnp.bitwise_and(jnp.right_shift(common, bit_number), 1)
    return jnp.where(parity % 2 == 0, 1.0, -1.0).astype(jnp.float32)

def householder_r(matrix):
    rows_count, cols_count = matrix.shape
    position = jnp.arange(rows_count, dtype=jnp.int32)

    def reflect(j, current):
        column = lax.dynamic_slice_in_dim(current, j, 1, 1)[:, 0]
        column = jnp.where(position >= j, column, jnp.float32(0.0))
        pivot_value = column[j]
        length = jnp.sqrt(jnp.sum(column * column))
        signed = jnp.where(pivot_value >= 0, jnp.float32(1.0), jnp.float32(-1.0))
        vector = column + signed * length * (position == j).astype(jnp.float32)
        denominator = jnp.sum(vector * vector)
        projection = jnp.dot(vector, current, precision=lax.Precision.HIGHEST)
        return current - vector[:, None] * projection[None, :] * (2.0 / denominator)
    reduced = lax.fori_loop(0, cols_count, reflect, matrix)
    upper = jnp.triu(reduced[:cols_count])
    diag_signs = jnp.where(jnp.diagonal(upper) >= 0, jnp.float32(1.0), jnp.float32(-1.0))
    return upper * diag_signs[:, None]

def forward_solve(upper, values):
    lower = upper.T
    order_size = lower.shape[0]

    def step_row(i, solved):
        row_coef = lax.dynamic_slice_in_dim(lower, i, 1, 0)
        partial_sum = jnp.dot(row_coef, solved, precision=lax.Precision.HIGHEST)
        target = lax.dynamic_slice_in_dim(values, i, 1, 0)
        pivot = lax.dynamic_slice_in_dim(row_coef[0], i, 1, 0)
        new_row = (target - partial_sum) / pivot[0]
        return lax.dynamic_update_slice_in_dim(solved, new_row, i, 0)
    return lax.fori_loop(0, order_size, step_row, jnp.zeros(values.shape, jnp.float32))

def reference(panel, signs, sample_device, sample_offset):
    blocks = N_ROWS * N_SK
    inner = ROWS_DEV // 128
    flipped = panel * signs.astype(jnp.float32)[None, :]
    cube = flipped.reshape(COLS, blocks, inner, 128)
    high = lax.Precision.HIGHEST
    cube = jnp.einsum('cpab,qp->cqab', cube, hadamard_table(blocks), precision=high)
    cube = jnp.einsum('cpab,ea->cpeb', cube, hadamard_table(inner), precision=high)
    cube = jnp.einsum('cpab,db->cpad', cube, hadamard_table(128), precision=high)
    mixed = cube.reshape(COLS, TOTAL_ROWS) * (1.0 / math.sqrt(TOTAL_ROWS))
    global_rows = (sample_device[:, 0] * ROWS_DEV + sample_offset).astype(jnp.int32)
    picked = jnp.take(mixed, global_rows, axis=1)
    sketch = picked * (1.0 / math.sqrt(SAMPLES))
    r_factor = householder_r(sketch.T)
    whitened = forward_solve(r_factor, picked)
    return (mixed, r_factor, whitened)
```

```python
import functools
import math

import jax
import jax.numpy as jnp
import numpy as np
from jax import lax
from jax.experimental import pallas as pl
from jax.experimental.pallas import tpu as pltpu
from jax.sharding import PartitionSpec as P

AXES = ("rows", "sk")
LANES = 128
GROUP = 8
SLICES = 6


def hadamard_np(order_size):
    table = np.ones((1, 1), np.float32)
    while table.shape[0] < order_size:
        table = np.block([[table, table], [table, -table]])
    return table


def mix_kernel(scale, panel_ref, signs_ref, table_ref, out_ref):
    rows = panel_ref.shape[1]
    inner = rows // LANES
    flipped = panel_ref[...] * (signs_ref[...].astype(jnp.float32) * scale)
    stacked = jnp.concatenate(
        [flipped[:, a * LANES : (a + 1) * LANES] for a in range(inner)], axis=0
    )
    table = table_ref[...]
    total = None
    rest = stacked
    for piece in range(3):
        part = rest.astype(jnp.bfloat16)
        term = jnp.dot(part, table, preferred_element_type=jnp.float32)
        total = term if total is None else total + term
        if piece < 2:
            rest = rest - part.astype(jnp.float32)
    blocks = [total[a * GROUP : (a + 1) * GROUP] for a in range(inner)]
    span = 1
    while span < inner:
        for a in range(inner):
            if a & span == 0:
                left, right = blocks[a], blocks[a + span]
                blocks[a], blocks[a + span] = left + right, left - right
        span *= 2
    for a in range(inner):
        out_ref[:, a * LANES : (a + 1) * LANES] = blocks[a]


def local_mix(panel, signs_row, table, scale, first, count):
    rows = panel.shape[1]
    return pl.pallas_call(
        functools.partial(mix_kernel, scale),
        grid=(count // GROUP,),
        in_specs=[
            pl.BlockSpec((GROUP, rows), lambda i: (first // GROUP + i, 0)),
            pl.BlockSpec((1, rows), lambda i: (0, 0)),
            pl.BlockSpec((LANES, LANES), lambda i: (0, 0)),
        ],
        out_specs=pl.BlockSpec((GROUP, rows), lambda i: (i, 0)),
        out_shape=jax.ShapeDtypeStruct((count, rows), jnp.float32),
        compiler_params=pltpu.CompilerParams(vmem_limit_bytes=32 << 20),
        cost_estimate=pl.CostEstimate(
            flops=count * rows * 800, bytes_accessed=count * rows * 8, transcendentals=0
        ),
    )(panel, signs_row, table)


def terms_kernel(bits, half, code_ref, me_ref, *refs):
    chunk_refs, out_ref, table_ref = refs[:-2], refs[-2], refs[-1]
    rows = chunk_refs[0].shape[1]
    me = me_ref[0]

    def transpose_block(a, carry):
        start = pl.multiple_of(a * LANES, LANES)
        tile = jnp.concatenate([ref[:, pl.ds(start, LANES)] for ref in chunk_refs], axis=0)
        turned = jnp.concatenate([tile, tile], axis=0).T
        table_ref[pl.ds(start, LANES), :] = turned
        table_ref[pl.ds(rows + start, LANES), :] = -turned
        return carry

    lax.fori_loop(0, rows // LANES, transpose_block, 0)
    first_half = lax.broadcasted_iota(jnp.int32, (1, LANES), 1) < LANES // 2

    def gather_block(r, carry):
        mask = jnp.int32(0)
        for bit in range(bits):
            mask = mask | (((r >> bit) & 1) << (bits - 1 - bit))
        source = (me ^ mask) * (2 * half)
        target = pl.multiple_of(r * half, half)
        for j in range(half):
            upper = table_ref[pl.ds(code_ref[source + j], 1), :]
            lower = table_ref[pl.ds(code_ref[source + half + j], 1), :]
            out_ref[pl.ds(target + j, 1), :] = jnp.where(first_half, upper, lower)
        return carry

    lax.fori_loop(0, 1 << bits, gather_block, 0)


def sampled_terms(chunks, code, me, bits, half):
    rows = chunks[0].shape[1]
    count = half << bits
    return pl.pallas_call(
        functools.partial(terms_kernel, bits, half),
        in_specs=[pl.BlockSpec(memory_space=pltpu.SMEM)] * 2
        + [pl.BlockSpec(memory_space=pltpu.VMEM)] * len(chunks),
        out_specs=pl.BlockSpec(memory_space=pltpu.VMEM),
        out_shape=jax.ShapeDtypeStruct((count, LANES), jnp.float32),
        scratch_shapes=[pltpu.VMEM((2 * rows, LANES), jnp.float32)],
        compiler_params=pltpu.CompilerParams(vmem_limit_bytes=40 << 20),
        cost_estimate=pl.CostEstimate(
            flops=count * LANES * 40, bytes_accessed=24 << 20, transcendentals=0
        ),
    )(code, me, *chunks)


def two_sum(a, b):
    total = a + b
    part = total - a
    return total, (a - (total - part)) + (b - part)


def quick_sum(a, b):
    total = a + b
    return total, b - (total - a)


def pair_add(a, b):
    total, error = two_sum(a[0], b[0])
    return quick_sum(total, error + (a[1] + b[1]))


def halves(a):
    scaled = a * 4097.0
    high = scaled - (scaled - a)
    return high, a - high


def product(a, b, a_parts, b_parts):
    whole = a * b
    error = (a_parts[0] * b_parts[0] - whole) + a_parts[0] * b_parts[1]
    error = (error + a_parts[1] * b_parts[0]) + a_parts[1] * b_parts[1]
    return whole, error


def gram_kernel(scale, terms_ref, picked_ref, gram_ref):
    cols = picked_ref.shape[0]
    turned = terms_ref[...].T
    picked = jnp.concatenate([turned[:cols], turned[cols:]], axis=1)
    picked_ref[...] = picked
    rest = picked * scale
    shift = jnp.max(jnp.abs(rest), axis=1, keepdims=True) * float(1 << 17)
    parts = []
    for _ in range(SLICES):
        part = (rest + shift) - shift
        rest = rest - part
        shift = shift * (1.0 / 64.0)
        parts.append(part.astype(jnp.bfloat16))
    total = None
    for level in range(SLICES):
        left = jnp.concatenate(parts[: level + 1], axis=1)
        right = jnp.concatenate(parts[: level + 1][::-1], axis=1)
        term = lax.dot_general(
            left, right, (((1,), (1,)), ((), ())), preferred_element_type=jnp.float32
        )
        if total is None:
            total = (term, jnp.zeros_like(term))
        else:
            high, error = two_sum(total[0], term)
            total = (high, total[1] + error)
    high, low = quick_sum(*total)
    gram_ref[...] = jnp.concatenate([high, low], axis=1)


def own_gram(terms, cols, per_device, scale):
    return pl.pallas_call(
        functools.partial(gram_kernel, scale),
        out_shape=(
            jax.ShapeDtypeStruct((cols, per_device), jnp.float32),
            jax.ShapeDtypeStruct((cols, 2 * cols), jnp.float32),
        ),
    )(terms)


def tree_sum(values):
    while len(values) > 1:
        values = [pair_add(values[i], values[i + 1]) for i in range(0, len(values), 2)]
    return values[0]


def split_pair(packed):
    cols = packed.shape[0]
    return packed[:, :cols], packed[:, cols:]


def gram_sum_kernel(*refs):
    high, low = tree_sum([split_pair(ref[...]) for ref in refs[:-1]])
    refs[-1][...] = jnp.concatenate([high, low], axis=1)


def gram_sum(grams):
    return pl.pallas_call(
        gram_sum_kernel, out_shape=jax.ShapeDtypeStruct(grams[0].shape, jnp.float32)
    )(*grams)


def factor_kernel(picked_ref, *refs):
    gram_refs, (r_ref, white_ref) = refs[:-2], refs[-2:]
    cols = r_ref.shape[0]
    high, low = tree_sum([split_pair(ref[...]) for ref in gram_refs])
    row_id = lax.broadcasted_iota(jnp.int32, (cols, cols), 0)
    lane_id = lax.broadcasted_iota(jnp.int32, (cols, cols), 1)
    unit = (row_id == lane_id).astype(jnp.float32)
    wide_high = jnp.concatenate([high, unit], axis=1)
    wide_low = jnp.concatenate([low, jnp.zeros_like(unit)], axis=1)
    tiles = cols // 8
    shape = (8, 2 * cols)
    rows = [
        (wide_high[t * 8 : (t + 1) * 8], wide_low[t * 8 : (t + 1) * 8])
        for t in range(tiles)
    ]
    sub_id = lax.broadcasted_iota(jnp.int32, shape, 0)
    for j in range(cols - 1):
        tile, sub = divmod(j, 8)
        row = [jnp.broadcast_to(v[sub : sub + 1], shape) for v in rows[tile]]
        pivot = [jnp.broadcast_to(v[sub : sub + 1, j : j + 1], shape) for v in rows[tile]]
        first = 1.0 / pivot[0]
        first_parts = halves(first)
        whole, error = product(pivot[0], first, halves(pivot[0]), first_parts)
        gap = ((1.0 - whole) - error) - pivot[1] * first
        inverse = quick_sum(first, first * gap)
        whole, error = product(row[0], inverse[0], halves(row[0]), halves(inverse[0]))
        scaled = quick_sum(whole, error + (row[0] * inverse[1] + row[1] * inverse[0]))
        scaled_parts = halves(scaled[0])
        for t in range(tile, tiles):
            if t == tile and sub == 7:
                continue
            high, low = rows[t]
            column = [jnp.broadcast_to(v[:, j : j + 1], shape) for v in rows[t]]
            if t == tile:
                column = [jnp.where(sub_id > sub, v, 0.0) for v in column]
            whole, error = product(column[0], scaled[0], halves(column[0]), scaled_parts)
            error = error + (column[0] * scaled[1] + column[1] * scaled[0])
            total, missed = two_sum(high, -whole)
            rows[t] = quick_sum(total, missed + (low - error))
    wide_high = jnp.concatenate([v[0] for v in rows], axis=0)
    wide_low = jnp.concatenate([v[1] for v in rows], axis=0)
    wide_row = lax.broadcasted_iota(jnp.int32, wide_high.shape, 0)
    wide_lane = lax.broadcasted_iota(jnp.int32, wide_high.shape, 1)
    diagonal = jnp.sum(jnp.where(wide_row == wide_lane, wide_high, 0.0), axis=1, keepdims=True)
    root = jnp.sqrt(diagonal)
    wide = (wide_high + wide_low) / root
    r_ref[...] = jnp.where(lane_id >= row_id, wide[:, :cols], 0.0)
    white_ref[...] = jnp.dot(
        wide[:, cols:],
        picked_ref[...],
        precision=lax.Precision.HIGHEST,
        preferred_element_type=jnp.float32,
    )


def factor_and_solve(picked, grams):
    cols = picked.shape[0]
    return pl.pallas_call(
        factor_kernel,
        out_shape=(
            jax.ShapeDtypeStruct((cols, cols), jnp.float32),
            jax.ShapeDtypeStruct(picked.shape, jnp.float32),
        ),
        cost_estimate=pl.CostEstimate(
            flops=20_000_000, bytes_accessed=1 << 18, transcendentals=0
        ),
    )(picked, *grams)


def xor_permute(value, mask, device_count):
    return lax.ppermute(value, AXES, [(i, i ^ mask) for i in range(device_count)])


def in_groups(masks, size):
    return [masks[i : i + size] for i in range(0, len(masks), size)]


def combined(masks, q):
    mask = 0
    for bit, value in enumerate(masks):
        if (q >> bit) & 1:
            mask |= value
    return mask


def local(panel, signs, sample_device, sample_offset):
    device_count = lax.axis_size(AXES)
    me = lax.axis_index(AXES).astype(jnp.int32)
    bits = device_count.bit_length() - 1
    cols, rows = panel.shape
    samples = sample_offset.shape[0]
    per_device = samples // device_count
    half = per_device // 2
    masks = [1 << bit for bit in range(bits)]

    table = jnp.asarray(hadamard_np(LANES), jnp.bfloat16)
    signs_row = signs.reshape(1, rows)
    scale = 1.0 / math.sqrt(rows * device_count)

    parts = 4
    width = cols // parts
    chunks = [
        local_mix(panel, signs_row, table, scale, part * width, width) for part in range(parts)
    ]

    far = masks[::-1]
    swapped = list(masks)
    if bits > 2:
        swapped[1], swapped[2] = swapped[2], swapped[1]
    orders = [far, swapped[::-1], masks, swapped]

    def own_sign(mask):
        return jnp.where((me & mask) == 0, jnp.float32(1.0), jnp.float32(-1.0))

    done = []
    for chunk, order in zip(chunks, orders):
        value = chunk
        for mask in order:
            other = xor_permute(value, mask, device_count)
            value = other + own_sign(mask) * value
        done.append(value)
    mixed = jnp.concatenate(done, axis=0)

    common = me & sample_device[:, 0]
    odd = lax.population_count(common) & 1
    code = sample_offset + odd * rows
    total = sampled_terms(chunks, code, me.reshape(1), bits, half)
    for group in in_groups(masks, 2):
        block = total.shape[0] >> len(group)
        mine = total[:block]
        for q in range(1, 1 << len(group)):
            mask = combined(group[::-1], q)
            mine = mine + xor_permute(total[q * block : (q + 1) * block], mask, device_count)
        total = mine

    picked, gram = own_gram(total, cols, per_device, 1.0 / math.sqrt(samples))
    groups = in_groups(far, 2)
    if len(groups) > 1 and len(groups[-1]) == 1:
        groups = groups[:-2] + [groups[-2] + groups[-1]]
    for number, group in enumerate(groups):
        received = [gram] + [
            xor_permute(gram, combined(group, q), device_count) for q in range(1, 1 << len(group))
        ]
        if number < len(groups) - 1:
            gram = gram_sum(received)
    r_factor, whitened = factor_and_solve(picked, received)
    return (mixed, r_factor, whitened)


def solution(mesh):
    return jax.shard_map(
        local,
        mesh=mesh,
        in_specs=(P(None, AXES), P(AXES), P(), P()),
        out_specs=(P(None, AXES), P(), P(None, AXES)),
        check_vma=False,
    )
```

```python
import functools
import math

import jax
import jax.numpy as jnp
import numpy as np
from jax import lax
from jax.experimental import pallas as pl
from jax.experimental.pallas import tpu as pltpu
from jax.sharding import PartitionSpec as P

AXES = ("rows", "sk")
LANES = 128
GROUP = 8
SLICES = 6


def hadamard_np(order_size):
    table = np.ones((1, 1), np.float32)
    while table.shape[0] < order_size:
        table = np.block([[table, table], [table, -table]])
    return table


def mix_kernel(scale, panel_ref, signs_ref, table_ref, out_ref):
    rows = panel_ref.shape[1]
    inner = rows // LANES
    flipped = panel_ref[...] * (signs_ref[...].astype(jnp.float32) * scale)
    stacked = jnp.concatenate(
        [flipped[:, a * LANES : (a + 1) * LANES] for a in range(inner)], axis=0
    )
    table = table_ref[...]
    total = None
    rest = stacked
    for piece in range(3):
        part = rest.astype(jnp.bfloat16)
        term = jnp.dot(part, table, preferred_element_type=jnp.float32)
        total = term if total is None else total + term
        if piece < 2:
            rest = rest - part.astype(jnp.float32)
    blocks = [total[a * GROUP : (a + 1) * GROUP] for a in range(inner)]
    span = 1
    while span < inner:
        for a in range(inner):
            if a & span == 0:
                left, right = blocks[a], blocks[a + span]
                blocks[a], blocks[a + span] = left + right, left - right
        span *= 2
    for a in range(inner):
        out_ref[:, a * LANES : (a + 1) * LANES] = blocks[a]


def local_mix(panel, signs_row, table, scale, first, count):
    rows = panel.shape[1]
    return pl.pallas_call(
        functools.partial(mix_kernel, scale),
        grid=(count // GROUP,),
        in_specs=[
            pl.BlockSpec((GROUP, rows), lambda i: (first // GROUP + i, 0)),
            pl.BlockSpec((1, rows), lambda i: (0, 0)),
            pl.BlockSpec((LANES, LANES), lambda i: (0, 0)),
        ],
        out_specs=pl.BlockSpec((GROUP, rows), lambda i: (i, 0)),
        out_shape=jax.ShapeDtypeStruct((count, rows), jnp.float32),
        compiler_params=pltpu.CompilerParams(vmem_limit_bytes=32 << 20),
        cost_estimate=pl.CostEstimate(
            flops=count * rows * 800, bytes_accessed=count * rows * 8, transcendentals=0
        ),
    )(panel, signs_row, table)


def terms_kernel(bits, half, code_ref, me_ref, *refs):
    chunk_refs, out_ref, table_ref = refs[:-2], refs[-2], refs[-1]
    rows = chunk_refs[0].shape[1]
    me = me_ref[0]

    def transpose_block(a, carry):
        start = pl.multiple_of(a * LANES, LANES)
        tile = jnp.concatenate([ref[:, pl.ds(start, LANES)] for ref in chunk_refs], axis=0)
        turned = jnp.concatenate([tile, tile], axis=0).T
        table_ref[pl.ds(start, LANES), :] = turned
        table_ref[pl.ds(rows + start, LANES), :] = -turned
        return carry

    lax.fori_loop(0, rows // LANES, transpose_block, 0)
    first_half = lax.broadcasted_iota(jnp.int32, (1, LANES), 1) < LANES // 2

    def gather_block(r, carry):
        mask = jnp.int32(0)
        for bit in range(bits):
            mask = mask | (((r >> bit) & 1) << (bits - 1 - bit))
        source = (me ^ mask) * (2 * half)
        target = pl.multiple_of(r * half, half)
        for j in range(half):
            upper = table_ref[pl.ds(code_ref[source + j], 1), :]
            lower = table_ref[pl.ds(code_ref[source + half + j], 1), :]
            out_ref[pl.ds(target + j, 1), :] = jnp.where(first_half, upper, lower)
        return carry

    lax.fori_loop(0, 1 << bits, gather_block, 0)


def sampled_terms(chunks, code, me, bits, half):
    rows = chunks[0].shape[1]
    count = half << bits
    return pl.pallas_call(
        functools.partial(terms_kernel, bits, half),
        in_specs=[pl.BlockSpec(memory_space=pltpu.SMEM)] * 2
        + [pl.BlockSpec(memory_space=pltpu.VMEM)] * len(chunks),
        out_specs=pl.BlockSpec(memory_space=pltpu.VMEM),
        out_shape=jax.ShapeDtypeStruct((count, LANES), jnp.float32),
        scratch_shapes=[pltpu.VMEM((2 * rows, LANES), jnp.float32)],
        compiler_params=pltpu.CompilerParams(vmem_limit_bytes=40 << 20),
        cost_estimate=pl.CostEstimate(
            flops=count * LANES * 40, bytes_accessed=24 << 20, transcendentals=0
        ),
    )(code, me, *chunks)


def two_sum(a, b):
    total = a + b
    part = total - a
    return total, (a - (total - part)) + (b - part)


def quick_sum(a, b):
    total = a + b
    return total, b - (total - a)


def pair_add(a, b):
    total, error = two_sum(a[0], b[0])
    return quick_sum(total, error + (a[1] + b[1]))


def halves(a):
    scaled = a * 4097.0
    high = scaled - (scaled - a)
    return high, a - high


def product(a, b, a_parts, b_parts):
    whole = a * b
    error = (a_parts[0] * b_parts[0] - whole) + a_parts[0] * b_parts[1]
    error = (error + a_parts[1] * b_parts[0]) + a_parts[1] * b_parts[1]
    return whole, error


def gram_kernel(scale, terms_ref, picked_ref, gram_ref):
    cols = picked_ref.shape[0]
    turned = terms_ref[...].T
    picked = jnp.concatenate([turned[:cols], turned[cols:]], axis=1)
    picked_ref[...] = picked
    rest = picked * scale
    shift = jnp.max(jnp.abs(rest), axis=1, keepdims=True) * float(1 << 17)
    parts = []
    for _ in range(SLICES):
        part = (rest + shift) - shift
        rest = rest - part
        shift = shift * (1.0 / 64.0)
        parts.append(part.astype(jnp.bfloat16))
    total = None
    for level in range(SLICES):
        left = jnp.concatenate(parts[: level + 1], axis=1)
        right = jnp.concatenate(parts[: level + 1][::-1], axis=1)
        term = lax.dot_general(
            left, right, (((1,), (1,)), ((), ())), preferred_element_type=jnp.float32
        )
        if total is None:
            total = (term, jnp.zeros_like(term))
        else:
            high, error = two_sum(total[0], term)
            total = (high, total[1] + error)
    high, low = quick_sum(*total)
    gram_ref[...] = jnp.concatenate([high, low], axis=1)


def own_gram(terms, cols, per_device, scale):
    return pl.pallas_call(
        functools.partial(gram_kernel, scale),
        out_shape=(
            jax.ShapeDtypeStruct((cols, per_device), jnp.float32),
            jax.ShapeDtypeStruct((cols, 2 * cols), jnp.float32),
        ),
    )(terms)


def tree_sum(values):
    while len(values) > 1:
        values = [pair_add(values[i], values[i + 1]) for i in range(0, len(values), 2)]
    return values[0]


def split_pair(packed):
    cols = packed.shape[0]
    return packed[:, :cols], packed[:, cols:]


def gram_sum_kernel(*refs):
    high, low = tree_sum([split_pair(ref[...]) for ref in refs[:-1]])
    refs[-1][...] = jnp.concatenate([high, low], axis=1)


def gram_sum(grams):
    return pl.pallas_call(
        gram_sum_kernel, out_shape=jax.ShapeDtypeStruct(grams[0].shape, jnp.float32)
    )(*grams)


def factor_kernel(picked_ref, *refs):
    gram_refs, (r_ref, white_ref) = refs[:-2], refs[-2:]
    cols = r_ref.shape[0]
    high, low = tree_sum([split_pair(ref[...]) for ref in gram_refs])
    row_id = lax.broadcasted_iota(jnp.int32, (cols, cols), 0)
    lane_id = lax.broadcasted_iota(jnp.int32, (cols, cols), 1)
    unit = (row_id == lane_id).astype(jnp.float32)
    wide_high = jnp.concatenate([high, unit], axis=1)
    wide_low = jnp.concatenate([low, jnp.zeros_like(unit)], axis=1)
    tiles = cols // 8
    shape = (8, 2 * cols)
    rows = [
        (wide_high[t * 8 : (t + 1) * 8], wide_low[t * 8 : (t + 1) * 8])
        for t in range(tiles)
    ]
    sub_id = lax.broadcasted_iota(jnp.int32, shape, 0)
    for j in range(cols - 1):
        tile, sub = divmod(j, 8)
        row = [jnp.broadcast_to(v[sub : sub + 1], shape) for v in rows[tile]]
        pivot = [jnp.broadcast_to(v[sub : sub + 1, j : j + 1], shape) for v in rows[tile]]
        first = 1.0 / pivot[0]
        first_parts = halves(first)
        whole, error = product(pivot[0], first, halves(pivot[0]), first_parts)
        gap = ((1.0 - whole) - error) - pivot[1] * first
        inverse = quick_sum(first, first * gap)
        whole, error = product(row[0], inverse[0], halves(row[0]), halves(inverse[0]))
        scaled = quick_sum(whole, error + (row[0] * inverse[1] + row[1] * inverse[0]))
        scaled_parts = halves(scaled[0])
        for t in range(tile, tiles):
            if t == tile and sub == 7:
                continue
            high, low = rows[t]
            column = [jnp.broadcast_to(v[:, j : j + 1], shape) for v in rows[t]]
            if t == tile:
                column = [jnp.where(sub_id > sub, v, 0.0) for v in column]
            whole, error = product(column[0], scaled[0], halves(column[0]), scaled_parts)
            error = error + (column[0] * scaled[1] + column[1] * scaled[0])
            total, missed = two_sum(high, -whole)
            rows[t] = quick_sum(total, missed + (low - error))
    wide_high = jnp.concatenate([v[0] for v in rows], axis=0)
    wide_low = jnp.concatenate([v[1] for v in rows], axis=0)
    wide_row = lax.broadcasted_iota(jnp.int32, wide_high.shape, 0)
    wide_lane = lax.broadcasted_iota(jnp.int32, wide_high.shape, 1)
    diagonal = jnp.sum(jnp.where(wide_row == wide_lane, wide_high, 0.0), axis=1, keepdims=True)
    root = jnp.sqrt(diagonal)
    wide = (wide_high + wide_low) / root
    r_ref[...] = jnp.where(lane_id >= row_id, wide[:, :cols], 0.0)
    white_ref[...] = jnp.dot(
        wide[:, cols:],
        picked_ref[...],
        precision=lax.Precision.HIGHEST,
        preferred_element_type=jnp.float32,
    )


def factor_and_solve(picked, grams):
    cols = picked.shape[0]
    return pl.pallas_call(
        factor_kernel,
        out_shape=(
            jax.ShapeDtypeStruct((cols, cols), jnp.float32),
            jax.ShapeDtypeStruct(picked.shape, jnp.float32),
        ),
        cost_estimate=pl.CostEstimate(
            flops=20_000_000, bytes_accessed=1 << 18, transcendentals=0
        ),
    )(picked, *grams)


def xor_permute(value, mask, device_count):
    return lax.ppermute(value, AXES, [(i, i ^ mask) for i in range(device_count)])


def in_groups(masks, size=2):
    odd = len(masks) % size
    groups = [masks[:odd]] if odd else []
    return groups + [masks[i : i + size] for i in range(odd, len(masks), size)]


def idle_kernel(*refs):
    del refs


def gate(values, tokens):
    count = len(values)
    return pl.pallas_call(
        idle_kernel,
        in_specs=[pl.BlockSpec(memory_space=pl.ANY)] * (count + len(tokens)),
        out_specs=tuple([pl.BlockSpec(memory_space=pl.ANY)] * count),
        out_shape=tuple(jax.ShapeDtypeStruct(v.shape, v.dtype) for v in values),
        input_output_aliases={i: i for i in range(count)},
    )(*values, *tokens)


def combined(masks, q):
    mask = 0
    for bit, value in enumerate(masks):
        if (q >> bit) & 1:
            mask |= value
    return mask


def local(panel, signs, sample_device, sample_offset):
    device_count = lax.axis_size(AXES)
    me = lax.axis_index(AXES).astype(jnp.int32)
    bits = device_count.bit_length() - 1
    cols, rows = panel.shape
    samples = sample_offset.shape[0]
    per_device = samples // device_count
    half = per_device // 2
    masks = [1 << bit for bit in range(bits)]

    table = jnp.asarray(hadamard_np(LANES), jnp.bfloat16)
    signs_row = signs.reshape(1, rows)
    scale = 1.0 / math.sqrt(rows * device_count)

    parts = cols // GROUP
    chunks = [
        local_mix(panel, signs_row, table, scale, part * GROUP, GROUP) for part in range(parts)
    ]

    def own_sign(mask):
        return jnp.where((me & mask) == 0, jnp.float32(1.0), jnp.float32(-1.0))

    def exchange(value, order):
        for mask in order:
            other = xor_permute(value, mask, device_count)
            value = other + own_sign(mask) * value
        return value

    def sampled_path():
        common = me & sample_device[:, 0]
        odd = lax.population_count(common) & 1
        code = sample_offset + odd * rows
        total = yield sampled_terms(chunks, code, me.reshape(1), bits, half)
        for number, group in enumerate(in_groups(masks)):
            block = total.shape[0] >> len(group)
            mine = total[:block]
            for q in range(1, 1 << len(group)):
                mask = combined(group[::-1], q)
                sent = total[q * block : (q + 1) * block]
                mine = mine + xor_permute(sent, mask, device_count)
            if number < len(in_groups(masks)) - 1:
                mine = yield mine
            total = mine
        picked, gram = own_gram(total, cols, per_device, 1.0 / math.sqrt(samples))
        groups = in_groups(masks)[::-1]
        for number, group in enumerate(groups):
            gram = yield gram
            received = [gram] + [
                xor_permute(gram, combined(group, q), device_count)
                for q in range(1, 1 << len(group))
            ]
            gram = gram_sum(received)
        gram = yield gram
        yield factor_and_solve(picked, [gram])

    top, near = masks[-1], masks[:-1]
    sets = [near[i * len(near) // 4 : (i + 1) * len(near) // 4] for i in range(4)]
    after = [sets[2], sets[0], sets[1], sets[3]]
    before = [sets[3], sets[1], sets[0], sets[2]]
    path = sampled_path()
    pending = None
    values = list(chunks)
    late = [[]]
    for phase in range(parts):
        if phase > 0:
            tokens = [values[phase - 1]] + late[phase - 1]
            held = [values[phase]] if pending is None else [values[phase], pending]
            gated = gate(held, tokens)
            values[phase] = gated[0]
            pending = gated[1] if pending is not None else None
        start = values[phase - 1] if phase > 0 else None
        late.append([])
        moved = []
        for part in range(parts):
            if part < parts // 2:
                step, order = phase - part - 1, after
            else:
                step, order = phase - part + parts // 2, before
            if 0 <= step < len(order):
                moved.append((part, order[step]))
        if phase > 0 and moved:
            free = [part for part, _ in moved if part != phase - 1]
            if free:
                for part, value in zip(free, gate([values[part] for part in free], [start])):
                    values[part] = value
        for part, order in moved:
            values[part] = exchange(values[part], order)
            if part < parts // 2:
                late[-1].append(values[part])
        values[phase] = exchange(values[phase], [top])
        pending = next(path) if phase == 0 else path.send(pending)
    while True:
        try:
            pending = path.send(pending)
        except StopIteration:
            break
    r_factor, whitened = pending
    mixed = jnp.concatenate(values, axis=0)
    return (mixed, r_factor, whitened)


def solution(mesh):
    return jax.shard_map(
        local,
        mesh=mesh,
        in_specs=(P(None, AXES), P(AXES), P(), P()),
        out_specs=(P(None, AXES), P(), P(None, AXES)),
        check_vma=False,
    )
```

```python
import functools
import math

import jax
import jax.numpy as jnp
import numpy as np
from jax import lax
from jax.experimental import pallas as pl
from jax.experimental.pallas import tpu as pltpu
from jax.sharding import PartitionSpec as P

AXES = ("rows", "sk")
LANES = 128
GROUP = 8
SLICES = 6


def hadamard_np(order_size):
    table = np.ones((1, 1), np.float32)
    while table.shape[0] < order_size:
        table = np.block([[table, table], [table, -table]])
    return table


def in_hbm(value):
    return pltpu.with_memory_space_constraint(value, pltpu.HBM)


def mix_kernel(scale, panel_ref, signs_ref, table_ref, out_ref):
    rows = panel_ref.shape[1]
    inner = rows // LANES
    flipped = panel_ref[...] * (signs_ref[...].astype(jnp.float32) * scale)
    stacked = jnp.concatenate(
        [flipped[:, a * LANES : (a + 1) * LANES] for a in range(inner)], axis=0
    )
    table = table_ref[...]
    total = None
    rest = stacked
    for piece in range(3):
        part = rest.astype(jnp.bfloat16)
        term = jnp.dot(part, table, preferred_element_type=jnp.float32)
        total = term if total is None else total + term
        if piece < 2:
            rest = rest - part.astype(jnp.float32)
    blocks = [total[a * GROUP : (a + 1) * GROUP] for a in range(inner)]
    span = 1
    while span < inner:
        for a in range(inner):
            if a & span == 0:
                left, right = blocks[a], blocks[a + span]
                blocks[a], blocks[a + span] = left + right, left - right
        span *= 2
    peers, _, width = out_ref.shape
    step = min(width, LANES)
    for start in range(0, rows, step):
        block = blocks[start // LANES][:, start % LANES : start % LANES + step]
        out_ref[start // width, :, start % width : start % width + step] = block


def local_mix(panel, signs_row, table, scale, peers):
    cols, rows = panel.shape
    width = rows // peers
    return pl.pallas_call(
        functools.partial(mix_kernel, scale),
        grid=(cols // GROUP,),
        in_specs=[
            pl.BlockSpec((GROUP, rows), lambda i: (i, 0)),
            pl.BlockSpec((1, rows), lambda i: (0, 0)),
            pl.BlockSpec((LANES, LANES), lambda i: (0, 0)),
        ],
        out_specs=pl.BlockSpec((peers, GROUP, width), lambda i: (0, i, 0)),
        out_shape=pltpu.HBM((peers, cols, width), jnp.float32),
        compiler_params=pltpu.CompilerParams(vmem_limit_bytes=32 << 20),
    )(in_hbm(panel), signs_row, table)


def across_kernel(in_ref, out_ref):
    peers = in_ref.shape[0]
    step = min(in_ref.shape[2], LANES)
    for lane in range(0, in_ref.shape[2], step):
        blocks = [in_ref[p, :, lane : lane + step] for p in range(peers)]
        span = 1
        while span < peers:
            for p in range(peers):
                if p & span == 0:
                    left, right = blocks[p], blocks[p + span]
                    blocks[p], blocks[p + span] = left + right, left - right
            span *= 2
        for p in range(peers):
            out_ref[p, :, lane : lane + step] = blocks[p]


def mix_across(received):
    peers, cols, width = received.shape
    spec = pl.BlockSpec((peers, GROUP, width), lambda i: (0, i, 0))
    return pl.pallas_call(
        across_kernel,
        grid=(cols // GROUP,),
        in_specs=[spec],
        out_specs=spec,
        out_shape=pltpu.HBM(received.shape, jnp.float32),
        compiler_params=pltpu.CompilerParams(vmem_limit_bytes=32 << 20),
    )(in_hbm(received))


def lay_out_kernel(in_ref, out_ref):
    peers, _, width = in_ref.shape
    for p in range(peers):
        out_ref[:, p * width : (p + 1) * width] = in_ref[p]


def lay_out(received):
    peers, cols, width = received.shape
    return pl.pallas_call(
        lay_out_kernel,
        grid=(cols // GROUP,),
        in_specs=[pl.BlockSpec((peers, GROUP, width), lambda i: (0, i, 0))],
        out_specs=pl.BlockSpec((GROUP, peers * width), lambda i: (i, 0)),
        out_shape=jax.ShapeDtypeStruct((cols, peers * width), jnp.float32),
        compiler_params=pltpu.CompilerParams(vmem_limit_bytes=32 << 20),
    )(in_hbm(received))


def terms_kernel(bits, half, code_ref, me_ref, far_ref, out_ref, mix_ref, table_ref, done_sem):
    peers, _, width = mix_ref.shape
    pieces = [
        pltpu.make_async_copy(far_ref.at[part], mix_ref.at[part], done_sem.at[number])
        for number, part in enumerate([pl.ds(0, peers // 2), pl.ds(peers // 2, peers // 2)])
    ]
    for piece in pieces:
        piece.start()
    rows = peers * width
    me = me_ref[0]

    span = max(1, LANES // width)

    def transpose_block(number, carry):
        p = number * span
        for lane in range(0, max(width, LANES), LANES):
            start = pl.multiple_of(p * width + lane, LANES)
            tile = jnp.concatenate(
                [mix_ref[p + i, :, lane : lane + min(width, LANES)] for i in range(span)], axis=1
            )
            turned = jnp.concatenate([tile, tile], axis=0).T
            table_ref[pl.ds(start, LANES), :] = turned
            table_ref[pl.ds(rows + start, LANES), :] = -turned
        return carry

    for number, piece in enumerate(pieces):
        piece.wait()
        count = peers // 2 // span
        lax.fori_loop(number * count, (number + 1) * count, transpose_block, 0)
    first_half = lax.broadcasted_iota(jnp.int32, (1, LANES), 1) < LANES // 2

    def gather_block(r, carry):
        mask = jnp.int32(0)
        for bit in range(bits):
            mask = mask | (((r >> bit) & 1) << (bits - 1 - bit))
        source = (me ^ mask) * (2 * half)
        target = pl.multiple_of(r * half, half)
        for j in range(half):
            upper = table_ref[pl.ds(code_ref[source + j], 1), :]
            lower = table_ref[pl.ds(code_ref[source + half + j], 1), :]
            out_ref[pl.ds(target + j, 1), :] = jnp.where(first_half, upper, lower)
        return carry

    lax.fori_loop(0, 1 << bits, gather_block, 0)


def sampled_terms(mix, code, me, bits, half):
    rows = mix.shape[0] * mix.shape[2]
    count = half << bits
    return pl.pallas_call(
        functools.partial(terms_kernel, bits, half),
        in_specs=[pl.BlockSpec(memory_space=pltpu.SMEM)] * 2
        + [pl.BlockSpec(memory_space=pltpu.HBM)],
        out_specs=pl.BlockSpec(memory_space=pltpu.VMEM),
        out_shape=jax.ShapeDtypeStruct((count, LANES), jnp.float32),
        scratch_shapes=[
            pltpu.VMEM(mix.shape, jnp.float32),
            pltpu.VMEM((2 * rows, LANES), jnp.float32),
            pltpu.SemaphoreType.DMA((2,)),
        ],
        compiler_params=pltpu.CompilerParams(vmem_limit_bytes=40 << 20),
        cost_estimate=pl.CostEstimate(
            flops=count * LANES * 40, bytes_accessed=24 << 20, transcendentals=0
        ),
    )(code, me, in_hbm(mix))


def two_sum(a, b):
    total = a + b
    part = total - a
    return total, (a - (total - part)) + (b - part)


def quick_sum(a, b):
    total = a + b
    return total, b - (total - a)


def pair_add(a, b):
    total, error = two_sum(a[0], b[0])
    return quick_sum(total, error + (a[1] + b[1]))


def halves(a):
    scaled = a * 4097.0
    high = scaled - (scaled - a)
    return high, a - high


def product(a, b, a_parts, b_parts):
    whole = a * b
    error = (a_parts[0] * b_parts[0] - whole) + a_parts[0] * b_parts[1]
    error = (error + a_parts[1] * b_parts[0]) + a_parts[1] * b_parts[1]
    return whole, error


def gram_kernel(scale, terms_ref, picked_ref, gram_ref):
    cols = picked_ref.shape[0]
    turned = terms_ref[...].T
    picked = jnp.concatenate([turned[:cols], turned[cols:]], axis=1)
    picked_ref[...] = picked
    rest = picked * scale
    shift = jnp.max(jnp.abs(rest), axis=1, keepdims=True) * float(1 << 17)
    parts = []
    for _ in range(SLICES):
        part = (rest + shift) - shift
        rest = rest - part
        shift = shift * (1.0 / 64.0)
        parts.append(part.astype(jnp.bfloat16))
    total = None
    for level in range(SLICES):
        left = jnp.concatenate(parts[: level + 1], axis=1)
        right = jnp.concatenate(parts[: level + 1][::-1], axis=1)
        term = lax.dot_general(
            left, right, (((1,), (1,)), ((), ())), preferred_element_type=jnp.float32
        )
        if total is None:
            total = (term, jnp.zeros_like(term))
        else:
            high, error = two_sum(total[0], term)
            total = (high, total[1] + error)
    high, low = quick_sum(*total)
    gram_ref[...] = jnp.concatenate([high, low], axis=1)


def own_gram(terms, cols, per_device, scale):
    return pl.pallas_call(
        functools.partial(gram_kernel, scale),
        out_shape=(
            jax.ShapeDtypeStruct((cols, per_device), jnp.float32),
            jax.ShapeDtypeStruct((cols, 2 * cols), jnp.float32),
        ),
    )(terms)


def tree_sum(values):
    while len(values) > 1:
        values = [pair_add(values[i], values[i + 1]) for i in range(0, len(values), 2)]
    return values[0]


def split_pair(packed):
    cols = packed.shape[0]
    return packed[:, :cols], packed[:, cols:]


def gram_sum_kernel(*refs):
    high, low = tree_sum([split_pair(ref[...]) for ref in refs[:-1]])
    refs[-1][...] = jnp.concatenate([high, low], axis=1)


def gram_sum(grams):
    return pl.pallas_call(
        gram_sum_kernel, out_shape=jax.ShapeDtypeStruct(grams[0].shape, jnp.float32)
    )(*grams)


def factor_kernel(picked_ref, *refs):
    gram_refs, (r_ref, white_ref) = refs[:-2], refs[-2:]
    cols = r_ref.shape[0]
    high, low = tree_sum([split_pair(ref[...]) for ref in gram_refs])
    row_id = lax.broadcasted_iota(jnp.int32, (cols, cols), 0)
    lane_id = lax.broadcasted_iota(jnp.int32, (cols, cols), 1)
    unit = (row_id == lane_id).astype(jnp.float32)
    wide_high = jnp.concatenate([high, unit], axis=1)
    wide_low = jnp.concatenate([low, jnp.zeros_like(unit)], axis=1)
    tiles = cols // 8
    shape = (8, 2 * cols)
    rows = [
        (wide_high[t * 8 : (t + 1) * 8], wide_low[t * 8 : (t + 1) * 8])
        for t in range(tiles)
    ]
    sub_id = lax.broadcasted_iota(jnp.int32, shape, 0)
    for j in range(cols - 1):
        tile, sub = divmod(j, 8)
        row = [jnp.broadcast_to(v[sub : sub + 1], shape) for v in rows[tile]]
        pivot = [jnp.broadcast_to(v[sub : sub + 1, j : j + 1], shape) for v in rows[tile]]
        first = 1.0 / pivot[0]
        first_parts = halves(first)
        whole, error = product(pivot[0], first, halves(pivot[0]), first_parts)
        gap = ((1.0 - whole) - error) - pivot[1] * first
        inverse = quick_sum(first, first * gap)
        whole, error = product(row[0], inverse[0], halves(row[0]), halves(inverse[0]))
        scaled = quick_sum(whole, error + (row[0] * inverse[1] + row[1] * inverse[0]))
        scaled_parts = halves(scaled[0])
        for t in range(tile, tiles):
            if t == tile and sub == 7:
                continue
            high, low = rows[t]
            column = [jnp.broadcast_to(v[:, j : j + 1], shape) for v in rows[t]]
            if t == tile:
                column = [jnp.where(sub_id > sub, v, 0.0) for v in column]
            whole, error = product(column[0], scaled[0], halves(column[0]), scaled_parts)
            error = error + (column[0] * scaled[1] + column[1] * scaled[0])
            total, missed = two_sum(high, -whole)
            rows[t] = quick_sum(total, missed + (low - error))
    wide_high = jnp.concatenate([v[0] for v in rows], axis=0)
    wide_low = jnp.concatenate([v[1] for v in rows], axis=0)
    wide_row = lax.broadcasted_iota(jnp.int32, wide_high.shape, 0)
    wide_lane = lax.broadcasted_iota(jnp.int32, wide_high.shape, 1)
    diagonal = jnp.sum(jnp.where(wide_row == wide_lane, wide_high, 0.0), axis=1, keepdims=True)
    root = jnp.sqrt(diagonal)
    wide = (wide_high + wide_low) / root
    r_ref[...] = jnp.where(lane_id >= row_id, wide[:, :cols], 0.0)
    white_ref[...] = jnp.dot(
        wide[:, cols:],
        picked_ref[...],
        precision=lax.Precision.HIGHEST,
        preferred_element_type=jnp.float32,
    )


def factor_and_solve(picked, grams):
    cols = picked.shape[0]
    return pl.pallas_call(
        factor_kernel,
        out_shape=(
            jax.ShapeDtypeStruct((cols, cols), jnp.float32),
            jax.ShapeDtypeStruct(picked.shape, jnp.float32),
        ),
        cost_estimate=pl.CostEstimate(
            flops=20_000_000, bytes_accessed=1 << 18, transcendentals=0
        ),
    )(picked, *grams)


def xor_permute(value, mask, device_count):
    return lax.ppermute(value, AXES, [(i, i ^ mask) for i in range(device_count)])


def in_groups(masks, size=2):
    odd = len(masks) % size
    groups = [masks[:odd]] if odd else []
    return groups + [masks[i : i + size] for i in range(odd, len(masks), size)]


def combined(masks, q):
    mask = 0
    for bit, value in enumerate(masks):
        if (q >> bit) & 1:
            mask |= value
    return mask


def local(panel, signs, sample_device, sample_offset):
    device_count = lax.axis_size(AXES)
    me = lax.axis_index(AXES).astype(jnp.int32)
    bits = device_count.bit_length() - 1
    cols, rows = panel.shape
    samples = sample_offset.shape[0]
    per_device = samples // device_count
    half = per_device // 2
    masks = [1 << bit for bit in range(bits)]

    table = jnp.asarray(hadamard_np(LANES), jnp.bfloat16)
    signs_row = signs.reshape(1, rows)
    scale = 1.0 / math.sqrt(rows * device_count)

    mix = local_mix(panel, signs_row, table, scale, device_count)

    def swap(value):
        return lax.all_to_all(value, AXES, split_axis=0, concat_axis=0, tiled=True)

    mixed = lay_out(swap(mix_across(swap(mix))))

    common = me & sample_device[:, 0]
    odd = lax.population_count(common) & 1
    code = sample_offset + odd * rows
    total = sampled_terms(mix, code, me.reshape(1), bits, half)
    for group in in_groups(masks):
        block = total.shape[0] >> len(group)
        mine = total[:block]
        for q in range(1, 1 << len(group)):
            mask = combined(group[::-1], q)
            sent = total[q * block : (q + 1) * block]
            mine = mine + xor_permute(sent, mask, device_count)
        total = mine
    picked, gram = own_gram(total, cols, per_device, 1.0 / math.sqrt(samples))
    groups = in_groups(masks)[::-1]
    for number, group in enumerate(groups):
        received = [gram] + [
            xor_permute(gram, combined(group, q), device_count) for q in range(1, 1 << len(group))
        ]
        if number < len(groups) - 1:
            gram = gram_sum(received)
    r_factor, whitened = factor_and_solve(picked, received)
    return (mixed, r_factor, whitened)


def solution(mesh):
    return jax.shard_map(
        local,
        mesh=mesh,
        in_specs=(P(None, AXES), P(AXES), P(), P()),
        out_specs=(P(None, AXES), P(), P(None, AXES)),
        check_vma=False,
    )
```

```python
import functools
import math

import jax
import jax.numpy as jnp
import numpy as np
from jax import lax
from jax.experimental import pallas as pl
from jax.experimental.pallas import tpu as pltpu
from jax.sharding import PartitionSpec as P

AXES = ("rows", "sk")
LANES = 128
GROUP = 16
SLICES = 6


def hadamard_table(order_size):
    shape = (order_size, order_size)
    common = lax.broadcasted_iota(jnp.int32, shape, 0) & lax.broadcasted_iota(jnp.int32, shape, 1)
    for distance in (4, 2, 1):
        common = common ^ (common >> distance)
    return (1 - 2 * (common & 1)).astype(jnp.float32).astype(jnp.bfloat16)


def in_hbm(value):
    return pltpu.with_memory_space_constraint(value, pltpu.HBM)


def mix_kernel(scale, panel_ref, signs_ref, out_ref):
    cols, rows = panel_ref.shape
    inner = rows // LANES
    width = out_ref.shape[2]
    step = min(width, LANES)
    table = hadamard_table(LANES)
    signs = signs_ref[...].astype(jnp.float32) * scale
    for first in range(0, cols, 8):
        flipped = panel_ref[first : first + 8, :] * signs
        stacked = jnp.concatenate(
            [flipped[:, a * LANES : (a + 1) * LANES] for a in range(inner)], axis=0
        )
        total = None
        rest = stacked
        for piece in range(3):
            part = rest.astype(jnp.bfloat16)
            term = jnp.dot(part, table, preferred_element_type=jnp.float32)
            total = term if total is None else total + term
            if piece < 2:
                rest = rest - part.astype(jnp.float32)
        blocks = [total[a * 8 : (a + 1) * 8] for a in range(inner)]
        span = 1
        while span < inner:
            for a in range(inner):
                if a & span == 0:
                    left, right = blocks[a], blocks[a + span]
                    blocks[a], blocks[a + span] = left + right, left - right
            span *= 2
        for start in range(0, rows, step):
            block = blocks[start // LANES][:, start % LANES : start % LANES + step]
            out_ref[start // width, first : first + 8, start % width : start % width + step] = block


def local_mix(panel, signs_row, scale, peers):
    cols, rows = panel.shape
    width = rows // peers
    return pl.pallas_call(
        functools.partial(mix_kernel, scale),
        grid=(cols // GROUP,),
        in_specs=[
            pl.BlockSpec((GROUP, rows), lambda i: (i, 0)),
            pl.BlockSpec((1, rows), lambda i: (0, 0)),
        ],
        out_specs=pl.BlockSpec((peers, GROUP, width), lambda i: (0, i, 0)),
        out_shape=pltpu.HBM((peers, cols, width), jnp.float32),
        compiler_params=pltpu.CompilerParams(vmem_limit_bytes=32 << 20),
    )(in_hbm(panel), in_hbm(signs_row))


def across_kernel(in_ref, out_ref):
    peers = in_ref.shape[0]
    step = min(in_ref.shape[2], LANES)
    for lane in range(0, in_ref.shape[2], step):
        for first in range(0, in_ref.shape[1], 8):
            columns = pl.ds(first, 8)
            blocks = [in_ref[p, columns, lane : lane + step] for p in range(peers)]
            span = 1
            while span < peers:
                for p in range(peers):
                    if p & span == 0:
                        left, right = blocks[p], blocks[p + span]
                        blocks[p], blocks[p + span] = left + right, left - right
                span *= 2
            for p in range(peers):
                out_ref[p, columns, lane : lane + step] = blocks[p]


def mix_across(received):
    peers, cols, width = received.shape
    spec = pl.BlockSpec((peers, GROUP, width), lambda i: (0, i, 0))
    return pl.pallas_call(
        across_kernel,
        grid=(cols // GROUP,),
        in_specs=[spec],
        out_specs=spec,
        out_shape=pltpu.HBM(received.shape, jnp.float32),
        compiler_params=pltpu.CompilerParams(vmem_limit_bytes=32 << 20),
    )(in_hbm(received))


def lay_out_kernel(in_ref, out_ref):
    peers, _, width = in_ref.shape
    for p in range(peers):
        out_ref[:, p * width : (p + 1) * width] = in_ref[p]


def lay_out(received):
    peers, cols, width = received.shape
    return pl.pallas_call(
        lay_out_kernel,
        grid=(cols // GROUP,),
        in_specs=[pl.BlockSpec((peers, GROUP, width), lambda i: (0, i, 0))],
        out_specs=pl.BlockSpec((GROUP, peers * width), lambda i: (i, 0)),
        out_shape=jax.ShapeDtypeStruct((cols, peers * width), jnp.float32),
        compiler_params=pltpu.CompilerParams(vmem_limit_bytes=32 << 20),
    )(in_hbm(received))


def terms_kernel(bits, half, code_ref, me_ref, far_ref, out_ref, mix_ref, table_ref, done_sem):
    peers, _, width = mix_ref.shape
    pieces = [
        pltpu.make_async_copy(far_ref.at[part], mix_ref.at[part], done_sem.at[number])
        for number, part in enumerate([pl.ds(0, peers // 2), pl.ds(peers // 2, peers // 2)])
    ]
    for piece in pieces:
        piece.start()
    rows = peers * width
    me = me_ref[0]

    span = max(1, LANES // width)

    def transpose_block(number, carry):
        p = number * span
        for lane in range(0, max(width, LANES), LANES):
            start = pl.multiple_of(p * width + lane, LANES)
            tile = jnp.concatenate(
                [mix_ref[p + i, :, lane : lane + min(width, LANES)] for i in range(span)], axis=1
            )
            turned = jnp.concatenate([tile, tile], axis=0).T
            table_ref[pl.ds(start, LANES), :] = turned
            table_ref[pl.ds(rows + start, LANES), :] = -turned
        return carry

    for number, piece in enumerate(pieces):
        piece.wait()
        count = peers // 2 // span
        lax.fori_loop(number * count, (number + 1) * count, transpose_block, 0)
    first_half = lax.broadcasted_iota(jnp.int32, (1, LANES), 1) < LANES // 2

    def gather_block(r, carry):
        mask = jnp.int32(0)
        for bit in range(bits):
            mask = mask | (((r >> bit) & 1) << (bits - 1 - bit))
        source = (me ^ mask) * (2 * half)
        target = pl.multiple_of(r * half, half)
        for j in range(half):
            upper = table_ref[pl.ds(code_ref[source + j], 1), :]
            lower = table_ref[pl.ds(code_ref[source + half + j], 1), :]
            out_ref[pl.ds(target + j, 1), :] = jnp.where(first_half, upper, lower)
        return carry

    lax.fori_loop(0, 1 << bits, gather_block, 0)


def sampled_terms(mix, code, me, bits, half):
    rows = mix.shape[0] * mix.shape[2]
    count = half << bits
    return pl.pallas_call(
        functools.partial(terms_kernel, bits, half),
        in_specs=[pl.BlockSpec(memory_space=pltpu.SMEM)] * 2
        + [pl.BlockSpec(memory_space=pltpu.HBM)],
        out_specs=pl.BlockSpec(memory_space=pltpu.VMEM),
        out_shape=jax.ShapeDtypeStruct((count, LANES), jnp.float32),
        scratch_shapes=[
            pltpu.VMEM(mix.shape, jnp.float32),
            pltpu.VMEM((2 * rows, LANES), jnp.float32),
            pltpu.SemaphoreType.DMA((2,)),
        ],
        compiler_params=pltpu.CompilerParams(vmem_limit_bytes=40 << 20),
        cost_estimate=pl.CostEstimate(
            flops=count * LANES * 40, bytes_accessed=24 << 20, transcendentals=0
        ),
    )(code, me, in_hbm(mix))


def two_sum(a, b):
    total = a + b
    part = total - a
    return total, (a - (total - part)) + (b - part)


def quick_sum(a, b):
    total = a + b
    return total, b - (total - a)


def pair_add(a, b):
    total, error = two_sum(a[0], b[0])
    return quick_sum(total, error + (a[1] + b[1]))


def halves(a):
    scaled = a * 4097.0
    high = scaled - (scaled - a)
    return high, a - high


def product(a, b, a_parts, b_parts):
    whole = a * b
    error = (a_parts[0] * b_parts[0] - whole) + a_parts[0] * b_parts[1]
    error = (error + a_parts[1] * b_parts[0]) + a_parts[1] * b_parts[1]
    return whole, error


def gram_kernel(scale, terms_ref, picked_ref, gram_ref):
    cols = picked_ref.shape[0]
    turned = terms_ref[...].T
    picked = jnp.concatenate([turned[:cols], turned[cols:]], axis=1)
    picked_ref[...] = picked
    rest = picked * scale
    shift = jnp.max(jnp.abs(rest), axis=1, keepdims=True) * float(1 << 17)
    parts = []
    for _ in range(SLICES):
        part = (rest + shift) - shift
        rest = rest - part
        shift = shift * (1.0 / 64.0)
        parts.append(part.astype(jnp.bfloat16))
    total = None
    for level in range(SLICES):
        left = jnp.concatenate(parts[: level + 1], axis=1)
        right = jnp.concatenate(parts[: level + 1][::-1], axis=1)
        term = lax.dot_general(
            left, right, (((1,), (1,)), ((), ())), preferred_element_type=jnp.float32
        )
        if total is None:
            total = (term, jnp.zeros_like(term))
        else:
            high, error = two_sum(total[0], term)
            total = (high, total[1] + error)
    high, low = quick_sum(*total)
    gram_ref[...] = jnp.concatenate([high, low], axis=1)


def own_gram(terms, cols, per_device, scale):
    return pl.pallas_call(
        functools.partial(gram_kernel, scale),
        out_shape=(
            jax.ShapeDtypeStruct((cols, per_device), jnp.float32),
            jax.ShapeDtypeStruct((cols, 2 * cols), jnp.float32),
        ),
    )(terms)


def tree_sum(values):
    while len(values) > 1:
        values = [pair_add(values[i], values[i + 1]) for i in range(0, len(values), 2)]
    return values[0]


def split_pair(packed):
    cols = packed.shape[0]
    return packed[:, :cols], packed[:, cols:]


def gram_sum_kernel(*refs):
    high, low = tree_sum([split_pair(ref[...]) for ref in refs[:-1]])
    refs[-1][...] = jnp.concatenate([high, low], axis=1)


def gram_sum(grams):
    return pl.pallas_call(
        gram_sum_kernel, out_shape=jax.ShapeDtypeStruct(grams[0].shape, jnp.float32)
    )(*grams)


def factor_kernel(picked_ref, *refs):
    gram_refs, (r_ref, white_ref) = refs[:-2], refs[-2:]
    cols = r_ref.shape[0]
    high, low = tree_sum([split_pair(ref[...]) for ref in gram_refs])
    row_id = lax.broadcasted_iota(jnp.int32, (cols, cols), 0)
    lane_id = lax.broadcasted_iota(jnp.int32, (cols, cols), 1)
    unit = (row_id == lane_id).astype(jnp.float32)
    wide_high = jnp.concatenate([high, unit], axis=1)
    wide_low = jnp.concatenate([low, jnp.zeros_like(unit)], axis=1)
    tiles = cols // 8
    shape = (8, 2 * cols)
    rows = [
        (wide_high[t * 8 : (t + 1) * 8], wide_low[t * 8 : (t + 1) * 8])
        for t in range(tiles)
    ]
    sub_id = lax.broadcasted_iota(jnp.int32, shape, 0)
    for j in range(cols - 1):
        tile, sub = divmod(j, 8)
        row = [jnp.broadcast_to(v[sub : sub + 1], shape) for v in rows[tile]]
        pivot = [jnp.broadcast_to(v[sub : sub + 1, j : j + 1], shape) for v in rows[tile]]
        first = 1.0 / pivot[0]
        first_parts = halves(first)
        whole, error = product(pivot[0], first, halves(pivot[0]), first_parts)
        gap = ((1.0 - whole) - error) - pivot[1] * first
        inverse = quick_sum(first, first * gap)
        whole, error = product(row[0], inverse[0], halves(row[0]), halves(inverse[0]))
        scaled = quick_sum(whole, error + (row[0] * inverse[1] + row[1] * inverse[0]))
        scaled_parts = halves(scaled[0])
        for t in range(tile, tiles):
            if t == tile and sub == 7:
                continue
            high, low = rows[t]
            column = [jnp.broadcast_to(v[:, j : j + 1], shape) for v in rows[t]]
            if t == tile:
                column = [jnp.where(sub_id > sub, v, 0.0) for v in column]
            whole, error = product(column[0], scaled[0], halves(column[0]), scaled_parts)
            error = error + (column[0] * scaled[1] + column[1] * scaled[0])
            total, missed = two_sum(high, -whole)
            rows[t] = quick_sum(total, missed + (low - error))
    wide_high = jnp.concatenate([v[0] for v in rows], axis=0)
    wide_low = jnp.concatenate([v[1] for v in rows], axis=0)
    wide_row = lax.broadcasted_iota(jnp.int32, wide_high.shape, 0)
    wide_lane = lax.broadcasted_iota(jnp.int32, wide_high.shape, 1)
    diagonal = jnp.sum(jnp.where(wide_row == wide_lane, wide_high, 0.0), axis=1, keepdims=True)
    root = jnp.sqrt(diagonal)
    wide = (wide_high + wide_low) / root
    r_ref[...] = jnp.where(lane_id >= row_id, wide[:, :cols], 0.0)
    white_ref[...] = jnp.dot(
        wide[:, cols:],
        picked_ref[...],
        precision=lax.Precision.HIGHEST,
        preferred_element_type=jnp.float32,
    )


def factor_and_solve(picked, grams):
    cols = picked.shape[0]
    return pl.pallas_call(
        factor_kernel,
        out_shape=(
            jax.ShapeDtypeStruct((cols, cols), jnp.float32),
            jax.ShapeDtypeStruct(picked.shape, jnp.float32),
        ),
        cost_estimate=pl.CostEstimate(
            flops=20_000_000, bytes_accessed=1 << 18, transcendentals=0
        ),
    )(picked, *grams)


def xor_permute(value, mask, device_count):
    return lax.ppermute(value, AXES, [(i, i ^ mask) for i in range(device_count)])


def in_groups(masks, size=2):
    odd = len(masks) % size
    groups = [masks[:odd]] if odd else []
    return groups + [masks[i : i + size] for i in range(odd, len(masks), size)]


def idle_kernel(*refs):
    del refs


def gate(value, *tokens):
    spec = pl.BlockSpec(memory_space=pltpu.HBM)
    return pl.pallas_call(
        idle_kernel,
        in_specs=[spec] + [pl.BlockSpec(memory_space=pl.ANY)] * len(tokens),
        out_specs=spec,
        out_shape=pltpu.HBM(value.shape, value.dtype),
        input_output_aliases={0: 0},
    )(value, *tokens)


def combined(masks, q):
    mask = 0
    for bit, value in enumerate(masks):
        if (q >> bit) & 1:
            mask |= value
    return mask


def local(panel, signs, sample_device, sample_offset):
    device_count = lax.axis_size(AXES)
    me = lax.axis_index(AXES).astype(jnp.int32)
    bits = device_count.bit_length() - 1
    cols, rows = panel.shape
    samples = sample_offset.shape[0]
    per_device = samples // device_count
    half = per_device // 2
    masks = [1 << bit for bit in range(bits)]

    signs_row = signs.reshape(1, rows)
    scale = 1.0 / math.sqrt(rows * device_count)

    mix = local_mix(panel, signs_row, scale, device_count)

    def swap(value):
        return lax.all_to_all(value, AXES, split_axis=0, concat_axis=0, tiled=True)

    across = mix_across(swap(mix))

    common = me & sample_device[:, 0]
    odd = lax.population_count(common) & 1
    code = sample_offset + odd * rows
    total = sampled_terms(mix, code, me.reshape(1), bits, half)
    for group in in_groups(masks):
        block = total.shape[0] >> len(group)
        mine = total[:block]
        for q in range(1, 1 << len(group)):
            mask = combined(group[::-1], q)
            sent = total[q * block : (q + 1) * block]
            mine = mine + xor_permute(sent, mask, device_count)
        total = mine
    picked, gram = own_gram(total, cols, per_device, 1.0 / math.sqrt(samples))
    groups = in_groups(masks)[::-1]
    for number, group in enumerate(groups):
        received = [gram] + [
            xor_permute(gram, combined(group, q), device_count) for q in range(1, 1 << len(group))
        ]
        if number < len(groups) - 1:
            gram = gram_sum(received)
        if number == 0:
            mixed = lay_out(swap(gate(across, gram)))
    r_factor, whitened = factor_and_solve(picked, received)
    return (mixed, r_factor, whitened)


def solution(mesh):
    return jax.shard_map(
        local,
        mesh=mesh,
        in_specs=(P(None, AXES), P(AXES), P(), P()),
        out_specs=(P(None, AXES), P(), P(None, AXES)),
        check_vma=False,
    )
```

```python
import functools
import math

import jax
import jax.numpy as jnp
import numpy as np
from jax import lax
from jax.experimental import pallas as pl
from jax.experimental.pallas import tpu as pltpu
from jax.sharding import PartitionSpec as P

AXES = ("rows", "sk")
LANES = 128
GROUP = 16
SLICES = 6
IN_VMEM = pl.BlockSpec(memory_space=pltpu.VMEM)


def hadamard_table(order_size):
    shape = (order_size, order_size)
    common = lax.broadcasted_iota(jnp.int32, shape, 0) & lax.broadcasted_iota(jnp.int32, shape, 1)
    for distance in (4, 2, 1):
        common = common ^ (common >> distance)
    return (1 - 2 * (common & 1)).astype(jnp.float32).astype(jnp.bfloat16)


def in_hbm(value):
    return pltpu.with_memory_space_constraint(value, pltpu.HBM)


def mix_kernel(scale, panel_ref, signs_ref, out_ref):
    cols, rows = panel_ref.shape
    inner = rows // LANES
    width = out_ref.shape[2]
    step = min(width, LANES)
    table = hadamard_table(LANES)
    signs = signs_ref[...].astype(jnp.float32) * scale
    for first in range(0, cols, 8):
        flipped = panel_ref[first : first + 8, :] * signs
        stacked = jnp.concatenate(
            [flipped[:, a * LANES : (a + 1) * LANES] for a in range(inner)], axis=0
        )
        total = None
        rest = stacked
        for piece in range(3):
            part = rest.astype(jnp.bfloat16)
            term = jnp.dot(part, table, preferred_element_type=jnp.float32)
            total = term if total is None else total + term
            if piece < 2:
                rest = rest - part.astype(jnp.float32)
        blocks = [total[a * 8 : (a + 1) * 8] for a in range(inner)]
        span = 1
        while span < inner:
            for a in range(inner):
                if a & span == 0:
                    left, right = blocks[a], blocks[a + span]
                    blocks[a], blocks[a + span] = left + right, left - right
            span *= 2
        for start in range(0, rows, step):
            block = blocks[start // LANES][:, start % LANES : start % LANES + step]
            out_ref[start // width, first : first + 8, start % width : start % width + step] = block


def local_mix(panel, signs_row, scale, peers):
    cols, rows = panel.shape
    width = rows // peers
    return pl.pallas_call(
        functools.partial(mix_kernel, scale),
        grid=(cols // GROUP,),
        in_specs=[
            pl.BlockSpec((GROUP, rows), lambda i: (i, 0)),
            pl.BlockSpec((1, rows), lambda i: (0, 0)),
        ],
        out_specs=pl.BlockSpec((peers, GROUP, width), lambda i: (0, i, 0)),
        out_shape=pltpu.HBM((peers, cols, width), jnp.float32),
        compiler_params=pltpu.CompilerParams(vmem_limit_bytes=32 << 20),
    )(in_hbm(panel), in_hbm(signs_row))


def across_kernel(in_ref, token_ref, out_ref):
    del token_ref
    peers = in_ref.shape[0]
    step = min(in_ref.shape[2], LANES)
    for lane in range(0, in_ref.shape[2], step):
        for first in range(0, in_ref.shape[1], 8):
            columns = pl.ds(first, 8)
            blocks = [in_ref[p, columns, lane : lane + step] for p in range(peers)]
            span = 1
            while span < peers:
                for p in range(peers):
                    if p & span == 0:
                        left, right = blocks[p], blocks[p + span]
                        blocks[p], blocks[p + span] = left + right, left - right
                span *= 2
            for p in range(peers):
                out_ref[p, columns, lane : lane + step] = blocks[p]


def mix_across(received, token):
    peers, cols, width = received.shape
    spec = pl.BlockSpec((peers, GROUP, width), lambda i: (0, i, 0))
    return pl.pallas_call(
        across_kernel,
        grid=(cols // GROUP,),
        in_specs=[spec, pl.BlockSpec(token.shape, lambda i: (0, 0))],
        out_specs=spec,
        out_shape=pltpu.HBM(received.shape, jnp.float32),
        compiler_params=pltpu.CompilerParams(vmem_limit_bytes=32 << 20),
    )(received, token)


def lay_out_kernel(in_ref, out_ref):
    peers, _, width = in_ref.shape
    for p in range(peers):
        out_ref[:, p * width : (p + 1) * width] = in_ref[p]


def lay_out(received):
    peers, cols, width = received.shape
    return pl.pallas_call(
        lay_out_kernel,
        grid=(cols // GROUP,),
        in_specs=[pl.BlockSpec((peers, GROUP, width), lambda i: (0, i, 0))],
        out_specs=pl.BlockSpec((GROUP, peers * width), lambda i: (i, 0)),
        out_shape=jax.ShapeDtypeStruct((cols, peers * width), jnp.float32),
        compiler_params=pltpu.CompilerParams(vmem_limit_bytes=32 << 20),
    )(received)


def terms_kernel(bits, half, code_ref, me_ref, far_ref, out_ref, mix_ref, table_ref, done_sem):
    peers, _, width = mix_ref.shape
    pieces = [
        pltpu.make_async_copy(far_ref.at[part], mix_ref.at[part], done_sem.at[number])
        for number, part in enumerate([pl.ds(0, peers // 2), pl.ds(peers // 2, peers // 2)])
    ]
    for piece in pieces:
        piece.start()
    rows = peers * width
    me = me_ref[0]

    span = max(1, LANES // width)

    def transpose_block(number, carry):
        p = number * span
        for lane in range(0, max(width, LANES), LANES):
            start = pl.multiple_of(p * width + lane, LANES)
            tile = jnp.concatenate(
                [mix_ref[p + i, :, lane : lane + min(width, LANES)] for i in range(span)], axis=1
            )
            turned = jnp.concatenate([tile, tile], axis=0).T
            table_ref[pl.ds(start, LANES), :] = turned
            table_ref[pl.ds(rows + start, LANES), :] = -turned
        return carry

    for number, piece in enumerate(pieces):
        piece.wait()
        count = peers // 2 // span
        lax.fori_loop(number * count, (number + 1) * count, transpose_block, 0)
    first_half = lax.broadcasted_iota(jnp.int32, (1, LANES), 1) < LANES // 2

    def gather_block(r, carry):
        mask = jnp.int32(0)
        for bit in range(bits):
            mask = mask | (((r >> bit) & 1) << (bits - 1 - bit))
        source = (me ^ mask) * (2 * half)
        target = pl.multiple_of(r * half, half)
        for j in range(half):
            upper = table_ref[pl.ds(code_ref[source + j], 1), :]
            lower = table_ref[pl.ds(code_ref[source + half + j], 1), :]
            out_ref[pl.ds(target + j, 1), :] = jnp.where(first_half, upper, lower)
        return carry

    lax.fori_loop(0, 1 << bits, gather_block, 0)


def sampled_terms(mix, code, me, bits, half):
    rows = mix.shape[0] * mix.shape[2]
    count = half << bits
    return pl.pallas_call(
        functools.partial(terms_kernel, bits, half),
        in_specs=[pl.BlockSpec(memory_space=pltpu.SMEM)] * 2
        + [pl.BlockSpec(memory_space=pltpu.HBM)],
        out_specs=pl.BlockSpec(memory_space=pltpu.VMEM),
        out_shape=jax.ShapeDtypeStruct((count, LANES), jnp.float32),
        scratch_shapes=[
            pltpu.VMEM(mix.shape, jnp.float32),
            pltpu.VMEM((2 * rows, LANES), jnp.float32),
            pltpu.SemaphoreType.DMA((2,)),
        ],
        compiler_params=pltpu.CompilerParams(vmem_limit_bytes=40 << 20),
        cost_estimate=pl.CostEstimate(
            flops=count * LANES * 40, bytes_accessed=24 << 20, transcendentals=0
        ),
    )(code, me, in_hbm(mix))


def two_sum(a, b):
    total = a + b
    part = total - a
    return total, (a - (total - part)) + (b - part)


def quick_sum(a, b):
    total = a + b
    return total, b - (total - a)


def pair_add(a, b):
    total, error = two_sum(a[0], b[0])
    return quick_sum(total, error + (a[1] + b[1]))


def halves(a):
    scaled = a * 4097.0
    high = scaled - (scaled - a)
    return high, a - high


def product(a, b, a_parts, b_parts):
    whole = a * b
    error = (a_parts[0] * b_parts[0] - whole) + a_parts[0] * b_parts[1]
    error = (error + a_parts[1] * b_parts[0]) + a_parts[1] * b_parts[1]
    return whole, error


def gram_kernel(scale, terms_ref, picked_ref, gram_ref):
    cols = picked_ref.shape[0]
    turned = terms_ref[...].T
    picked = jnp.concatenate([turned[:cols], turned[cols:]], axis=1)
    picked_ref[...] = picked
    rest = picked * scale
    shift = jnp.max(jnp.abs(rest), axis=1, keepdims=True) * float(1 << 17)
    parts = []
    for _ in range(SLICES):
        part = (rest + shift) - shift
        rest = rest - part
        shift = shift * (1.0 / 64.0)
        parts.append(part.astype(jnp.bfloat16))
    total = None
    for level in range(SLICES):
        left = jnp.concatenate(parts[: level + 1], axis=1)
        right = jnp.concatenate(parts[: level + 1][::-1], axis=1)
        term = lax.dot_general(
            left, right, (((1,), (1,)), ((), ())), preferred_element_type=jnp.float32
        )
        if total is None:
            total = (term, jnp.zeros_like(term))
        else:
            high, error = two_sum(total[0], term)
            total = (high, total[1] + error)
    high, low = quick_sum(*total)
    gram_ref[...] = jnp.concatenate([high, low], axis=1)


def own_gram(terms, cols, per_device, scale):
    return pl.pallas_call(
        functools.partial(gram_kernel, scale),
        in_specs=[IN_VMEM],
        out_specs=(IN_VMEM, IN_VMEM),
        out_shape=(
            jax.ShapeDtypeStruct((cols, per_device), jnp.float32),
            jax.ShapeDtypeStruct((cols, 2 * cols), jnp.float32),
        ),
    )(terms)


def tree_sum(values):
    while len(values) > 1:
        values = [pair_add(values[i], values[i + 1]) for i in range(0, len(values), 2)]
    return values[0]


def split_pair(packed):
    cols = packed.shape[0]
    return packed[:, :cols], packed[:, cols:]


def gram_sum_kernel(count, *refs):
    high, low = tree_sum([split_pair(ref[...]) for ref in refs[:count]])
    refs[-1][...] = jnp.concatenate([high, low], axis=1)


def gram_sum(grams, *through):
    count = len(grams)
    in_place = pl.BlockSpec(memory_space=pltpu.HBM)
    return pl.pallas_call(
        functools.partial(gram_sum_kernel, count),
        in_specs=[IN_VMEM] * count + [in_place] * len(through),
        out_specs=tuple([in_place] * len(through) + [IN_VMEM]),
        out_shape=tuple(
            [pltpu.HBM(v.shape, v.dtype) for v in through]
            + [jax.ShapeDtypeStruct(grams[0].shape, jnp.float32)]
        ),
        input_output_aliases={count + i: i for i in range(len(through))},
    )(*grams, *through)


def factor_kernel(picked_ref, *refs):
    gram_refs, (r_ref, white_ref) = refs[:-2], refs[-2:]
    cols = r_ref.shape[0]
    high, low = tree_sum([split_pair(ref[...]) for ref in gram_refs])
    row_id = lax.broadcasted_iota(jnp.int32, (cols, cols), 0)
    lane_id = lax.broadcasted_iota(jnp.int32, (cols, cols), 1)
    unit = (row_id == lane_id).astype(jnp.float32)
    wide_high = jnp.concatenate([high, unit], axis=1)
    wide_low = jnp.concatenate([low, jnp.zeros_like(unit)], axis=1)
    tiles = cols // 8
    shape = (8, 2 * cols)
    rows = [
        (wide_high[t * 8 : (t + 1) * 8], wide_low[t * 8 : (t + 1) * 8])
        for t in range(tiles)
    ]
    sub_id = lax.broadcasted_iota(jnp.int32, shape, 0)
    for j in range(cols - 1):
        tile, sub = divmod(j, 8)
        row = [jnp.broadcast_to(v[sub : sub + 1], shape) for v in rows[tile]]
        pivot = [jnp.broadcast_to(v[sub : sub + 1, j : j + 1], shape) for v in rows[tile]]
        first = 1.0 / pivot[0]
        first_parts = halves(first)
        whole, error = product(pivot[0], first, halves(pivot[0]), first_parts)
        gap = ((1.0 - whole) - error) - pivot[1] * first
        inverse = quick_sum(first, first * gap)
        whole, error = product(row[0], inverse[0], halves(row[0]), halves(inverse[0]))
        scaled = quick_sum(whole, error + (row[0] * inverse[1] + row[1] * inverse[0]))
        scaled_parts = halves(scaled[0])
        for t in range(tile, tiles):
            if t == tile and sub == 7:
                continue
            high, low = rows[t]
            column = [jnp.broadcast_to(v[:, j : j + 1], shape) for v in rows[t]]
            if t == tile:
                column = [jnp.where(sub_id > sub, v, 0.0) for v in column]
            whole, error = product(column[0], scaled[0], halves(column[0]), scaled_parts)
            error = error + (column[0] * scaled[1] + column[1] * scaled[0])
            total, missed = two_sum(high, -whole)
            rows[t] = quick_sum(total, missed + (low - error))
    wide_high = jnp.concatenate([v[0] for v in rows], axis=0)
    wide_low = jnp.concatenate([v[1] for v in rows], axis=0)
    wide_row = lax.broadcasted_iota(jnp.int32, wide_high.shape, 0)
    wide_lane = lax.broadcasted_iota(jnp.int32, wide_high.shape, 1)
    diagonal = jnp.sum(jnp.where(wide_row == wide_lane, wide_high, 0.0), axis=1, keepdims=True)
    root = jnp.sqrt(diagonal)
    wide = (wide_high + wide_low) / root
    r_ref[...] = jnp.where(lane_id >= row_id, wide[:, :cols], 0.0)
    white_ref[...] = jnp.dot(
        wide[:, cols:],
        picked_ref[...],
        precision=lax.Precision.HIGHEST,
        preferred_element_type=jnp.float32,
    )


def factor_and_solve(picked, grams):
    cols = picked.shape[0]
    return pl.pallas_call(
        factor_kernel,
        in_specs=[IN_VMEM] * (1 + len(grams)),
        out_specs=(IN_VMEM, IN_VMEM),
        out_shape=(
            jax.ShapeDtypeStruct((cols, cols), jnp.float32),
            jax.ShapeDtypeStruct(picked.shape, jnp.float32),
        ),
        cost_estimate=pl.CostEstimate(
            flops=20_000_000, bytes_accessed=1 << 18, transcendentals=0
        ),
    )(picked, *grams)


def xor_permute(value, mask, device_count):
    return lax.ppermute(value, AXES, [(i, i ^ mask) for i in range(device_count)])


def in_groups(masks, size=2):
    odd = len(masks) % size
    groups = [masks[:odd]] if odd else []
    return groups + [masks[i : i + size] for i in range(odd, len(masks), size)]


def combined(masks, q):
    mask = 0
    for bit, value in enumerate(masks):
        if (q >> bit) & 1:
            mask |= value
    return mask


def local(panel, signs, sample_device, sample_offset):
    device_count = lax.axis_size(AXES)
    me = lax.axis_index(AXES).astype(jnp.int32)
    bits = device_count.bit_length() - 1
    cols, rows = panel.shape
    samples = sample_offset.shape[0]
    per_device = samples // device_count
    half = per_device // 2
    masks = [1 << bit for bit in range(bits)]

    signs_row = signs.reshape(1, rows)
    scale = 1.0 / math.sqrt(rows * device_count)

    mix = local_mix(panel, signs_row, scale, device_count)

    def swap(value):
        return lax.all_to_all(value, AXES, split_axis=0, concat_axis=0, tiled=True)

    received_mix = swap(mix)

    common = me & sample_device[:, 0]
    odd = lax.population_count(common) & 1
    code = sample_offset + odd * rows
    total = sampled_terms(mix, code, me.reshape(1), bits, half)
    for group in in_groups(masks):
        block = total.shape[0] >> len(group)
        mine = total[:block]
        for q in range(1, 1 << len(group)):
            mask = combined(group[::-1], q)
            sent = total[q * block : (q + 1) * block]
            mine = mine + xor_permute(sent, mask, device_count)
        total = mine
    picked, gram = own_gram(total, cols, per_device, 1.0 / math.sqrt(samples))
    across = mix_across(received_mix, gram)
    groups = in_groups(masks)[::-1]
    for number, group in enumerate(groups):
        received = [gram] + [
            xor_permute(gram, combined(group, q), device_count) for q in range(1, 1 << len(group))
        ]
        if number == 0:
            across, gram = gram_sum(received, across)
            mixed = lay_out(swap(across))
        elif number < len(groups) - 1:
            (gram,) = gram_sum(received)
    r_factor, whitened = factor_and_solve(picked, received)
    return (mixed, r_factor, whitened)


def solution(mesh):
    return jax.shard_map(
        local,
        mesh=mesh,
        in_specs=(P(None, AXES), P(AXES), P(), P()),
        out_specs=(P(None, AXES), P(), P(None, AXES)),
        check_vma=False,
    )
```

```python
import functools
import math

import jax
import jax.numpy as jnp
from jax import lax
from jax.experimental import pallas as pl
from jax.experimental.pallas import tpu as pltpu
from jax.sharding import Mesh
from jax.sharding import PartitionSpec as P

AXES = ("far", "near")
LANES = 128
GROUP = 16
SLICES = 6


def hadamard_table(order_size):
    shape = (order_size, order_size)
    common = lax.broadcasted_iota(jnp.int32, shape, 0) & lax.broadcasted_iota(jnp.int32, shape, 1)
    for distance in (4, 2, 1):
        common = common ^ (common >> distance)
    return (1 - 2 * (common & 1)).astype(jnp.float32).astype(jnp.bfloat16)


def whole(value):
    return pl.BlockSpec(value.shape, lambda i: (0,) * len(value.shape))


def corner(value):
    lead = (1,) * (len(value.shape) - 2)
    return pl.BlockSpec(lead + (8, LANES), lambda i: (0,) * len(value.shape))


def in_hbm(value):
    return pltpu.with_memory_space_constraint(value, pltpu.HBM)


def mix_kernel(scale, panel_ref, signs_ref, *out_refs):
    cols, rows = panel_ref.shape
    inner = rows // LANES
    peers, _, width = out_refs[0].shape
    step = min(width, LANES)
    table = hadamard_table(LANES)
    signs = signs_ref[...].astype(jnp.float32) * scale
    for first in range(0, cols, 8):
        flipped = panel_ref[first : first + 8, :] * signs
        stacked = jnp.concatenate(
            [flipped[:, a * LANES : (a + 1) * LANES] for a in range(inner)], axis=0
        )
        total = None
        rest = stacked
        for piece in range(3):
            part = rest.astype(jnp.bfloat16)
            term = jnp.dot(part, table, preferred_element_type=jnp.float32)
            total = term if total is None else total + term
            if piece < 2:
                rest = rest - part.astype(jnp.float32)
        blocks = [total[a * 8 : (a + 1) * 8] for a in range(inner)]
        span = 1
        while span < inner:
            for a in range(inner):
                if a & span == 0:
                    left, right = blocks[a], blocks[a + span]
                    blocks[a], blocks[a + span] = left + right, left - right
            span *= 2
        for start in range(0, rows, step):
            block = blocks[start // LANES][:, start % LANES : start % LANES + step]
            piece, peer = divmod(start // width, peers)
            lane = start % width
            out_refs[piece][peer, first : first + 8, lane : lane + step] = block


def local_mix(panel, signs_row, scale, peers, first, count, pieces):
    rows = panel.shape[1]
    width = rows // peers
    share = peers // pieces
    return pl.pallas_call(
        functools.partial(mix_kernel, scale),
        grid=(count // GROUP,),
        in_specs=[
            pl.BlockSpec((GROUP, rows), lambda i: (first // GROUP + i, 0)),
            pl.BlockSpec((1, rows), lambda i: (0, 0)),
        ],
        out_specs=(pl.BlockSpec((share, GROUP, width), lambda i: (0, i, 0)),) * pieces,
        out_shape=(pltpu.HBM((share, count, width), jnp.float32),) * pieces,
        compiler_params=pltpu.CompilerParams(vmem_limit_bytes=32 << 20),
    )(in_hbm(panel), in_hbm(signs_row))


def across_kernel(in_ref, *refs):
    out_ref = refs[-1]
    peers = in_ref.shape[0]
    step = min(in_ref.shape[2], LANES)
    for lane in range(0, in_ref.shape[2], step):
        for first in range(0, in_ref.shape[1], 8):
            columns = pl.ds(first, 8)
            blocks = [in_ref[p, columns, lane : lane + step] for p in range(peers)]
            span = 1
            while span < peers:
                for p in range(peers):
                    if p & span == 0:
                        left, right = blocks[p], blocks[p + span]
                        blocks[p], blocks[p + span] = left + right, left - right
                span *= 2
            for p in range(peers):
                out_ref[p, columns, lane : lane + step] = blocks[p]


def mix_across(received, *tokens):
    peers, cols, width = received.shape
    spec = pl.BlockSpec((peers, GROUP, width), lambda i: (0, i, 0))
    return pl.pallas_call(
        across_kernel,
        grid=(cols // GROUP,),
        in_specs=[spec] + [corner(token) for token in tokens],
        out_specs=spec,
        out_shape=pltpu.HBM(received.shape, jnp.float32),
        compiler_params=pltpu.CompilerParams(vmem_limit_bytes=32 << 20),
    )(received, *tokens)


def far_sign(me_ref, device_count):
    return jnp.where(me_ref[0] < device_count // 2, jnp.float32(1.0), jnp.float32(-1.0))


def far_kernel(device_count, me_ref, *refs):
    sign = far_sign(me_ref, device_count)
    own, other, out_ref = refs[:2], refs[2:4], refs[-1]
    share = own[0].shape[0]
    for piece in range(2):
        for p in range(share):
            out_ref[piece * share + p] = other[piece][p] + sign * own[piece][p]


def mix_far(me, own, other, device_count, token):
    share, cols, width = own[0].shape
    half = pl.BlockSpec((share, GROUP, width), lambda i: (0, i, 0))
    return pl.pallas_call(
        functools.partial(far_kernel, device_count),
        grid=(cols // GROUP,),
        in_specs=[pl.BlockSpec(memory_space=pltpu.SMEM)] + [half] * 4 + [corner(token)],
        out_specs=pl.BlockSpec((2 * share, GROUP, width), lambda i: (0, i, 0)),
        out_shape=pltpu.HBM((2 * share, cols, width), jnp.float32),
        compiler_params=pltpu.CompilerParams(vmem_limit_bytes=32 << 20),
    )(me, *own, *other, token)


def first_half_kernel(in_ref, out_ref):
    peers, _, width = in_ref.shape
    for p in range(peers):
        out_ref[:, p * width : (p + 1) * width] = in_ref[p]


def first_half(received, cols):
    peers, count, width = received.shape
    return pl.pallas_call(
        first_half_kernel,
        grid=(count // GROUP,),
        in_specs=[pl.BlockSpec((peers, GROUP, width), lambda i: (0, i, 0))],
        out_specs=pl.BlockSpec((GROUP, peers * width), lambda i: (i, 0)),
        out_shape=pltpu.HBM((cols, peers * width), jnp.float32),
        compiler_params=pltpu.CompilerParams(vmem_limit_bytes=32 << 20),
    )(received)


def second_half_kernel(device_count, me_ref, own_ref, low_ref, high_ref, whole_ref, out_ref):
    del whole_ref
    sign = far_sign(me_ref, device_count)
    share, _, width = low_ref.shape
    for p in range(2 * share):
        other = low_ref[p] if p < share else high_ref[p - share]
        out_ref[:, p * width : (p + 1) * width] = other + sign * own_ref[p]


def second_half(me, own, other, mixed, device_count):
    peers, count, width = own.shape
    skipped = (mixed.shape[0] - count) // GROUP
    half = pl.BlockSpec((peers // 2, GROUP, width), lambda i: (0, i, 0))
    return pl.pallas_call(
        functools.partial(second_half_kernel, device_count),
        grid=(count // GROUP,),
        in_specs=[
            pl.BlockSpec(memory_space=pltpu.SMEM),
            pl.BlockSpec((peers, GROUP, width), lambda i: (0, i, 0)),
            half,
            half,
            pl.BlockSpec(memory_space=pltpu.HBM),
        ],
        out_specs=pl.BlockSpec((GROUP, peers * width), lambda i: (skipped + i, 0)),
        out_shape=pltpu.HBM(mixed.shape, jnp.float32),
        input_output_aliases={4: 0},
        compiler_params=pltpu.CompilerParams(vmem_limit_bytes=32 << 20),
    )(me, own, *other, mixed)


def terms_kernel(bits, half, code_ref, me_ref, *refs):
    far_refs, (out_ref, mix_ref, table_ref, done_sem) = refs[:3], refs[3:]
    peers, _, width = mix_ref.shape
    rows = peers * width
    me = me_ref[0]
    share = peers // 2
    cols = far_refs[0].shape[1]
    pieces = [
        (far_refs[0], pl.ds(0, share), pl.ds(0, cols)),
        (far_refs[1], pl.ds(share, share), pl.ds(0, cols)),
        (far_refs[2], pl.ds(0, peers), pl.ds(cols, cols)),
    ]
    copies = [
        pltpu.make_async_copy(ref, mix_ref.at[part, columns], done_sem.at[number])
        for number, (ref, part, columns) in enumerate(pieces)
    ]
    for copy in copies:
        copy.start()

    def transpose_block(p, carry):
        for lane in range(0, width, LANES):
            start = pl.multiple_of(p * width + lane, LANES)
            tile = mix_ref[p, :, lane : lane + LANES]
            turned = jnp.concatenate([tile, tile], axis=0).T
            table_ref[pl.ds(start, LANES), :] = turned
            table_ref[pl.ds(rows + start, LANES), :] = -turned
        return carry

    for copy in copies:
        copy.wait()
    lax.fori_loop(0, peers, transpose_block, 0)
    first_lanes = lax.broadcasted_iota(jnp.int32, (1, LANES), 1) < LANES // 2

    def gather_block(r, carry):
        mask = jnp.int32(0)
        for bit in range(bits):
            mask = mask | (((r >> bit) & 1) << (bits - 1 - bit))
        source = (me ^ mask) * (2 * half)
        target = pl.multiple_of(r * half, half)
        for j in range(half):
            upper = table_ref[pl.ds(code_ref[source + j], 1), :]
            lower = table_ref[pl.ds(code_ref[source + half + j], 1), :]
            out_ref[pl.ds(target + j, 1), :] = jnp.where(first_lanes, upper, lower)
        return carry

    lax.fori_loop(0, 1 << bits, gather_block, 0)


def sampled_terms(pieces, code, me, bits, half):
    share, cols, width = pieces[0].shape
    peers = 2 * share
    return pl.pallas_call(
        functools.partial(terms_kernel, bits, half),
        in_specs=[pl.BlockSpec(memory_space=pltpu.SMEM)] * 2
        + [pl.BlockSpec(memory_space=pltpu.HBM)] * len(pieces),
        out_specs=pl.BlockSpec(memory_space=pltpu.VMEM),
        out_shape=jax.ShapeDtypeStruct((half << bits, LANES), jnp.float32),
        scratch_shapes=[
            pltpu.VMEM((peers, 2 * cols, width), jnp.float32),
            pltpu.VMEM((2 * peers * width, LANES), jnp.float32),
            pltpu.SemaphoreType.DMA((len(pieces),)),
        ],
        compiler_params=pltpu.CompilerParams(vmem_limit_bytes=40 << 20),
    )(code, me, *[in_hbm(piece) for piece in pieces])


def add_terms_kernel(count, own_ref, *refs):
    out_ref = refs[-1]
    first = 0
    for ref in refs[:count]:
        size = ref.shape[0]
        rows = pl.ds(first, size)
        out_ref[rows, :] = own_ref[rows, :] + ref[...]
        first += size


def add_terms(total, received, *tokens):
    block = sum(piece.shape[0] for piece in received)
    return pl.pallas_call(
        functools.partial(add_terms_kernel, len(received)),
        grid=(1,),
        in_specs=[pl.BlockSpec((block, LANES), lambda i: (0, 0))]
        + [whole(piece) for piece in received]
        + [corner(token) for token in tokens],
        out_specs=pl.BlockSpec((block, LANES), lambda i: (0, 0)),
        out_shape=jax.ShapeDtypeStruct((block, LANES), jnp.float32),
        compiler_params=pltpu.CompilerParams(vmem_limit_bytes=32 << 20),
    )(total, *received, *tokens)


def two_sum(a, b):
    total = a + b
    part = total - a
    return total, (a - (total - part)) + (b - part)


def quick_sum(a, b):
    total = a + b
    return total, b - (total - a)


def pair_add(a, b):
    total, error = two_sum(a[0], b[0])
    return quick_sum(total, error + (a[1] + b[1]))


def halves(a):
    scaled = a * 4097.0
    high = scaled - (scaled - a)
    return high, a - high


def product(a, b, a_parts, b_parts):
    whole = a * b
    error = (a_parts[0] * b_parts[0] - whole) + a_parts[0] * b_parts[1]
    error = (error + a_parts[1] * b_parts[0]) + a_parts[1] * b_parts[1]
    return whole, error


def gram_kernel(scale, terms_ref, picked_ref, gram_ref):
    cols = picked_ref.shape[0]
    turned = terms_ref[...].T
    picked = jnp.concatenate([turned[:cols], turned[cols:]], axis=1)
    picked_ref[...] = picked
    rest = picked * scale
    shift = jnp.max(jnp.abs(rest), axis=1, keepdims=True) * float(1 << 17)
    parts = []
    for _ in range(SLICES):
        part = (rest + shift) - shift
        rest = rest - part
        shift = shift * (1.0 / 64.0)
        parts.append(part.astype(jnp.bfloat16))
    total = None
    for level in range(SLICES):
        left = jnp.concatenate(parts[: level + 1], axis=1)
        right = jnp.concatenate(parts[: level + 1][::-1], axis=1)
        term = lax.dot_general(
            left, right, (((1,), (1,)), ((), ())), preferred_element_type=jnp.float32
        )
        if total is None:
            total = (term, jnp.zeros_like(term))
        else:
            high, error = two_sum(total[0], term)
            total = (high, total[1] + error)
    high, low = quick_sum(*total)
    gram_ref[...] = jnp.concatenate([high, low], axis=1)


def own_gram(terms, cols, per_device, scale):
    return pl.pallas_call(
        functools.partial(gram_kernel, scale),
        grid=(1,),
        in_specs=[whole(terms)],
        out_specs=(
            pl.BlockSpec((cols, per_device), lambda i: (0, 0)),
            pl.BlockSpec((cols, 2 * cols), lambda i: (0, 0)),
        ),
        out_shape=(
            jax.ShapeDtypeStruct((cols, per_device), jnp.float32),
            jax.ShapeDtypeStruct((cols, 2 * cols), jnp.float32),
        ),
    )(terms)


def tree_sum(values):
    while len(values) > 1:
        values = [pair_add(values[i], values[i + 1]) for i in range(0, len(values), 2)]
    return values[0]


def split_pair(packed):
    cols = packed.shape[0]
    return packed[:, :cols], packed[:, cols:]


def gram_sum_kernel(*refs):
    high, low = tree_sum([split_pair(ref[...]) for ref in refs[:-1]])
    refs[-1][...] = jnp.concatenate([high, low], axis=1)


def gram_sum(grams):
    return pl.pallas_call(
        gram_sum_kernel,
        grid=(1,),
        in_specs=[whole(gram) for gram in grams],
        out_specs=whole(grams[0]),
        out_shape=jax.ShapeDtypeStruct(grams[0].shape, jnp.float32),
    )(*grams)


def factor_kernel(picked_ref, *refs):
    gram_refs, (r_ref, white_ref) = refs[:-2], refs[-2:]
    cols = r_ref.shape[0]
    high, low = tree_sum([split_pair(ref[...]) for ref in gram_refs])
    row_id = lax.broadcasted_iota(jnp.int32, (cols, cols), 0)
    lane_id = lax.broadcasted_iota(jnp.int32, (cols, cols), 1)
    unit = (row_id == lane_id).astype(jnp.float32)
    wide_high = jnp.concatenate([high, unit], axis=1)
    wide_low = jnp.concatenate([low, jnp.zeros_like(unit)], axis=1)
    tiles = cols // 8
    shape = (8, 2 * cols)
    rows = [
        (wide_high[t * 8 : (t + 1) * 8], wide_low[t * 8 : (t + 1) * 8])
        for t in range(tiles)
    ]
    sub_id = lax.broadcasted_iota(jnp.int32, shape, 0)
    for j in range(cols - 1):
        tile, sub = divmod(j, 8)
        row = [jnp.broadcast_to(v[sub : sub + 1], shape) for v in rows[tile]]
        pivot = [jnp.broadcast_to(v[sub : sub + 1, j : j + 1], shape) for v in rows[tile]]
        first = 1.0 / pivot[0]
        first_parts = halves(first)
        whole, error = product(pivot[0], first, halves(pivot[0]), first_parts)
        gap = ((1.0 - whole) - error) - pivot[1] * first
        inverse = quick_sum(first, first * gap)
        whole, error = product(row[0], inverse[0], halves(row[0]), halves(inverse[0]))
        scaled = quick_sum(whole, error + (row[0] * inverse[1] + row[1] * inverse[0]))
        scaled_parts = halves(scaled[0])
        for t in range(tile, tiles):
            if t == tile and sub == 7:
                continue
            high, low = rows[t]
            column = [jnp.broadcast_to(v[:, j : j + 1], shape) for v in rows[t]]
            if t == tile:
                column = [jnp.where(sub_id > sub, v, 0.0) for v in column]
            whole, error = product(column[0], scaled[0], halves(column[0]), scaled_parts)
            error = error + (column[0] * scaled[1] + column[1] * scaled[0])
            total, missed = two_sum(high, -whole)
            rows[t] = quick_sum(total, missed + (low - error))
    wide_high = jnp.concatenate([v[0] for v in rows], axis=0)
    wide_low = jnp.concatenate([v[1] for v in rows], axis=0)
    wide_row = lax.broadcasted_iota(jnp.int32, wide_high.shape, 0)
    wide_lane = lax.broadcasted_iota(jnp.int32, wide_high.shape, 1)
    diagonal = jnp.sum(jnp.where(wide_row == wide_lane, wide_high, 0.0), axis=1, keepdims=True)
    root = jnp.sqrt(diagonal)
    wide = (wide_high + wide_low) / root
    r_ref[...] = jnp.where(lane_id >= row_id, wide[:, :cols], 0.0)
    white_ref[...] = jnp.dot(
        wide[:, cols:],
        picked_ref[...],
        precision=lax.Precision.HIGHEST,
        preferred_element_type=jnp.float32,
    )


def factor_and_solve(picked, grams):
    cols = picked.shape[0]
    return pl.pallas_call(
        factor_kernel,
        grid=(1,),
        in_specs=[whole(value) for value in (picked, *grams)],
        out_specs=(pl.BlockSpec((cols, cols), lambda i: (0, 0)), whole(picked)),
        out_shape=(
            jax.ShapeDtypeStruct((cols, cols), jnp.float32),
            jax.ShapeDtypeStruct(picked.shape, jnp.float32),
        ),
        cost_estimate=pl.CostEstimate(
            flops=20_000_000, bytes_accessed=1 << 18, transcendentals=0
        ),
    )(picked, *grams)


def xor_permute(value, mask, device_count):
    return lax.ppermute(value, AXES, [(i, i ^ mask) for i in range(device_count)])


def in_groups(masks, size=2):
    odd = len(masks) % size
    groups = [masks[:odd]] if odd else []
    return groups + [masks[i : i + size] for i in range(odd, len(masks), size)]


def combined(masks, q):
    mask = 0
    for bit, value in enumerate(masks):
        if (q >> bit) & 1:
            mask |= value
    return mask


def local(panel, signs, sample_device, sample_offset):
    device_count = lax.axis_size(AXES)
    me = lax.axis_index(AXES).astype(jnp.int32)
    bits = device_count.bit_length() - 1
    cols, rows = panel.shape
    samples = sample_offset.shape[0]
    per_device = samples // device_count
    half = per_device // 2
    masks = [1 << bit for bit in range(bits)]

    signs_row = signs.reshape(1, rows)
    scale = 1.0 / math.sqrt(rows * device_count)
    top = masks[-1]
    peers = device_count // 2
    own_id = me.reshape(1)

    low_a, high_a = local_mix(panel, signs_row, scale, peers, 0, cols // 2, 2)
    (mix_b,) = local_mix(panel, signs_row, scale, peers, cols // 2, cols // 2, 1)
    other_a = [xor_permute(piece, top, device_count) for piece in (low_a, high_a)]

    def swap(value):
        return lax.all_to_all(value, AXES[1], split_axis=0, concat_axis=0, tiled=True)

    common = me & sample_device[:, 0]
    odd = lax.population_count(common) & 1
    code = sample_offset + odd * rows
    total = sampled_terms([low_a, high_a, mix_b], code, own_id, bits, half)
    received_b = swap(mix_b)
    swapped_b = swap(mix_across(received_b, other_a[0], total))
    block = total.shape[0] // 2
    pieces = 2
    sent = [total[block + part * (block // pieces) :][: block // pieces] for part in range(pieces)]
    nearest = [xor_permute(piece, masks[0], device_count) for piece in sent]
    total = add_terms(total, nearest, other_a[0])
    far_ready = None
    groups = in_groups(masks[1:])
    for number, group in enumerate(groups):
        if number == len(groups) - 1:
            far_ready = total
        block = total.shape[0] >> len(group)
        mine = total[:block]
        for q in range(1, 1 << len(group)):
            mask = combined(group[::-1], q)
            sent = total[q * block : (q + 1) * block]
            mine = mine + xor_permute(sent, mask, device_count)
        total = mine
    near_a = mix_far(own_id, (low_a, high_a), other_a, device_count, far_ready)
    other_b = [
        xor_permute(swapped_b[part * (peers // 2) : (part + 1) * (peers // 2)], top, device_count)
        for part in range(2)
    ]
    received_a = swap(near_a)

    picked, gram = own_gram(total, cols, per_device, 1.0 / math.sqrt(samples))
    groups = groups[::-1] + [masks[:1]]
    for number, group in enumerate(groups):
        received = [gram] + [
            xor_permute(gram, combined(group, q), device_count) for q in range(1, 1 << len(group))
        ]
        if number < len(groups) - 1:
            gram = gram_sum(received)
        if number == 0:
            swapped_a = swap(mix_across(received_a, other_b[0], gram))
    r_factor, whitened = factor_and_solve(picked, received)
    mixed = second_half(own_id, swapped_b, other_b, first_half(swapped_a, cols), device_count)
    return (mixed, r_factor, whitened)


def solution(mesh):
    view = Mesh(mesh.devices.reshape(2, -1), AXES)
    return jax.shard_map(
        local,
        mesh=view,
        in_specs=(P(None, AXES), P(AXES), P(), P()),
        out_specs=(P(None, AXES), P(), P(None, AXES)),
        check_vma=False,
    )
```

```python
import functools
import math

import jax
import jax.numpy as jnp
from jax import lax
from jax.experimental import pallas as pl
from jax.experimental.pallas import tpu as pltpu
from jax.sharding import Mesh
from jax.sharding import PartitionSpec as P

AXES = ("far", "near")
LANES = 128
GROUP = 16
SLICES = 6


def hadamard_table(order_size):
    shape = (order_size, order_size)
    common = lax.broadcasted_iota(jnp.int32, shape, 0) & lax.broadcasted_iota(jnp.int32, shape, 1)
    for distance in (4, 2, 1):
        common = common ^ (common >> distance)
    return (1 - 2 * (common & 1)).astype(jnp.float32).astype(jnp.bfloat16)


def whole(value):
    return pl.BlockSpec(value.shape, lambda i: (0,) * len(value.shape))


def corner(value):
    lead = (1,) * (len(value.shape) - 2)
    return pl.BlockSpec(lead + (8, LANES), lambda i: (0,) * len(value.shape))


def in_hbm(value):
    return pltpu.with_memory_space_constraint(value, pltpu.HBM)


def mix_kernel(scale, panel_ref, signs_ref, *out_refs):
    cols, rows = panel_ref.shape
    inner = rows // LANES
    width = out_refs[0].shape[2]
    places = [(ref, peer) for ref in out_refs for peer in range(ref.shape[0])]
    step = min(width, LANES)
    table = hadamard_table(LANES)
    signs = signs_ref[...].astype(jnp.float32) * scale
    for first in range(0, cols, 8):
        flipped = panel_ref[first : first + 8, :] * signs
        stacked = jnp.concatenate(
            [flipped[:, a * LANES : (a + 1) * LANES] for a in range(inner)], axis=0
        )
        total = None
        rest = stacked
        for piece in range(3):
            part = rest.astype(jnp.bfloat16)
            term = jnp.dot(part, table, preferred_element_type=jnp.float32)
            total = term if total is None else total + term
            if piece < 2:
                rest = rest - part.astype(jnp.float32)
        blocks = [total[a * 8 : (a + 1) * 8] for a in range(inner)]
        span = 1
        while span < inner:
            for a in range(inner):
                if a & span == 0:
                    left, right = blocks[a], blocks[a + span]
                    blocks[a], blocks[a + span] = left + right, left - right
            span *= 2
        for start in range(0, rows, step):
            block = blocks[start // LANES][:, start % LANES : start % LANES + step]
            out_ref, peer = places[start // width]
            lane = start % width
            out_ref[peer, first : first + 8, lane : lane + step] = block


def local_mix(panel, signs_row, scale, shares, first, count):
    rows = panel.shape[1]
    width = rows // sum(shares)
    return pl.pallas_call(
        functools.partial(mix_kernel, scale),
        grid=(count // GROUP,),
        in_specs=[
            pl.BlockSpec((GROUP, rows), lambda i: (first // GROUP + i, 0)),
            pl.BlockSpec((1, rows), lambda i: (0, 0)),
        ],
        out_specs=tuple(pl.BlockSpec((n, GROUP, width), lambda i: (0, i, 0)) for n in shares),
        out_shape=tuple(pltpu.HBM((n, count, width), jnp.float32) for n in shares),
        compiler_params=pltpu.CompilerParams(vmem_limit_bytes=32 << 20),
    )(in_hbm(panel), in_hbm(signs_row))


def across_kernel(in_ref, *refs):
    out_ref = refs[-1]
    peers = in_ref.shape[0]
    step = min(in_ref.shape[2], LANES)
    for lane in range(0, in_ref.shape[2], step):
        for first in range(0, in_ref.shape[1], 8):
            columns = pl.ds(first, 8)
            blocks = [in_ref[p, columns, lane : lane + step] for p in range(peers)]
            span = 1
            while span < peers:
                for p in range(peers):
                    if p & span == 0:
                        left, right = blocks[p], blocks[p + span]
                        blocks[p], blocks[p + span] = left + right, left - right
                span *= 2
            for p in range(peers):
                out_ref[p, columns, lane : lane + step] = blocks[p]


def mix_across(received, *tokens):
    peers, cols, width = received.shape
    spec = pl.BlockSpec((peers, GROUP, width), lambda i: (0, i, 0))
    return pl.pallas_call(
        across_kernel,
        grid=(cols // GROUP,),
        in_specs=[spec] + [corner(token) for token in tokens],
        out_specs=spec,
        out_shape=pltpu.HBM(received.shape, jnp.float32),
        compiler_params=pltpu.CompilerParams(vmem_limit_bytes=32 << 20),
    )(received, *tokens)


def far_sign(me_ref, device_count):
    return jnp.where(me_ref[0] < device_count // 2, jnp.float32(1.0), jnp.float32(-1.0))


def far_kernel(device_count, me_ref, *refs):
    sign = far_sign(me_ref, device_count)
    own, other, out_ref = refs[:2], refs[2:4], refs[-1]
    peer = 0
    for piece in range(2):
        for p in range(own[piece].shape[0]):
            out_ref[peer] = other[piece][p] + sign * own[piece][p]
            peer += 1


def mix_far(me, own, other, device_count, token):
    peers = own[0].shape[0] + own[1].shape[0]
    _, cols, width = own[0].shape
    pieces = [*own, *other]
    specs = [pl.BlockSpec((v.shape[0], GROUP, width), lambda i: (0, i, 0)) for v in pieces]
    return pl.pallas_call(
        functools.partial(far_kernel, device_count),
        grid=(cols // GROUP,),
        in_specs=[pl.BlockSpec(memory_space=pltpu.SMEM)] + specs + [corner(token)],
        out_specs=pl.BlockSpec((peers, GROUP, width), lambda i: (0, i, 0)),
        out_shape=pltpu.HBM((peers, cols, width), jnp.float32),
        compiler_params=pltpu.CompilerParams(vmem_limit_bytes=32 << 20),
    )(me, *pieces, token)


def idle_kernel(*refs):
    del refs


def gate(value, *tokens):
    in_place = pl.BlockSpec(memory_space=pltpu.HBM)
    return pl.pallas_call(
        idle_kernel,
        grid=(1,),
        in_specs=[in_place] + [corner(token) for token in tokens],
        out_specs=in_place,
        out_shape=pltpu.HBM(value.shape, value.dtype),
        input_output_aliases={0: 0},
    )(value, *tokens)


def first_half_kernel(in_ref, out_ref):
    peers, _, width = in_ref.shape
    for p in range(peers):
        out_ref[:, p * width : (p + 1) * width] = in_ref[p]


def first_half(received, cols):
    peers, count, width = received.shape
    return pl.pallas_call(
        first_half_kernel,
        grid=(count // GROUP,),
        in_specs=[pl.BlockSpec((peers, GROUP, width), lambda i: (0, i, 0))],
        out_specs=pl.BlockSpec((GROUP, peers * width), lambda i: (i, 0)),
        out_shape=pltpu.HBM((cols, peers * width), jnp.float32),
        compiler_params=pltpu.CompilerParams(vmem_limit_bytes=32 << 20),
    )(received)


def second_half_kernel(device_count, me_ref, own_ref, other_ref, whole_ref, out_ref):
    del whole_ref
    sign = far_sign(me_ref, device_count)
    peers, _, width = own_ref.shape
    for p in range(peers):
        out_ref[:, p * width : (p + 1) * width] = other_ref[p] + sign * own_ref[p]


def second_half(me, own, other, mixed, device_count):
    peers, count, width = own.shape
    skipped = (mixed.shape[0] - count) // GROUP
    spec = pl.BlockSpec((peers, GROUP, width), lambda i: (0, i, 0))
    return pl.pallas_call(
        functools.partial(second_half_kernel, device_count),
        grid=(count // GROUP,),
        in_specs=[
            pl.BlockSpec(memory_space=pltpu.SMEM),
            spec,
            spec,
            pl.BlockSpec(memory_space=pltpu.HBM),
        ],
        out_specs=pl.BlockSpec((GROUP, peers * width), lambda i: (skipped + i, 0)),
        out_shape=pltpu.HBM(mixed.shape, jnp.float32),
        input_output_aliases={3: 0},
        compiler_params=pltpu.CompilerParams(vmem_limit_bytes=32 << 20),
    )(me, own, other, mixed)


def terms_kernel(bits, half, code_ref, me_ref, *refs):
    far_refs, (out_ref, mix_ref, table_ref, done_sem) = refs[:3], refs[-4:]
    peers, _, width = mix_ref.shape
    rows = peers * width
    me = me_ref[0]
    share, cols, _ = far_refs[0].shape
    pieces = [
        (far_refs[0], pl.ds(0, share), pl.ds(0, cols)),
        (far_refs[1], pl.ds(share, peers - share), pl.ds(0, cols)),
        (far_refs[2], pl.ds(0, peers), pl.ds(cols, cols)),
    ]
    copies = [
        pltpu.make_async_copy(ref, mix_ref.at[part, columns], done_sem.at[number])
        for number, (ref, part, columns) in enumerate(pieces)
    ]
    for copy in copies:
        copy.start()

    def transpose_block(p, carry):
        for lane in range(0, width, LANES):
            start = pl.multiple_of(p * width + lane, LANES)
            tile = mix_ref[p, :, lane : lane + LANES]
            turned = jnp.concatenate([tile, tile], axis=0).T
            table_ref[pl.ds(start, LANES), :] = turned
            table_ref[pl.ds(rows + start, LANES), :] = -turned
        return carry

    for copy in copies:
        copy.wait()
    lax.fori_loop(0, peers, transpose_block, 0)
    first_lanes = lax.broadcasted_iota(jnp.int32, (1, LANES), 1) < LANES // 2

    def gather_block(r, carry):
        mask = jnp.int32(0)
        for bit in range(bits):
            mask = mask | (((r >> bit) & 1) << (bits - 1 - bit))
        source = (me ^ mask) * (2 * half)
        target = pl.multiple_of(r * half, half)
        for j in range(half):
            upper = table_ref[pl.ds(code_ref[source + j], 1), :]
            lower = table_ref[pl.ds(code_ref[source + half + j], 1), :]
            out_ref[pl.ds(target + j, 1), :] = jnp.where(first_lanes, upper, lower)
        return carry

    lax.fori_loop(0, 1 << bits, gather_block, 0)


def sampled_terms(pieces, code, me, bits, half):
    peers, cols, width = pieces[-1].shape
    count = half << bits
    return pl.pallas_call(
        functools.partial(terms_kernel, bits, half),
        grid=(1,),
        in_specs=[pl.BlockSpec(memory_space=pltpu.SMEM)] * 2
        + [pl.BlockSpec(memory_space=pltpu.HBM)] * len(pieces),
        out_specs=pl.BlockSpec((count, LANES), lambda i: (0, 0)),
        out_shape=jax.ShapeDtypeStruct((count, LANES), jnp.float32),
        scratch_shapes=[
            pltpu.VMEM((peers, 2 * cols, width), jnp.float32),
            pltpu.VMEM((2 * peers * width, LANES), jnp.float32),
            pltpu.SemaphoreType.DMA((len(pieces),)),
        ],
        compiler_params=pltpu.CompilerParams(vmem_limit_bytes=40 << 20),
    )(code, me, *[in_hbm(piece) for piece in pieces])


def sum_terms_kernel(count, *refs):
    total = refs[0][...]
    for ref in refs[1:count]:
        total = total + ref[...]
    refs[-1][...] = total


def sum_terms(total, received, *tokens):
    return pl.pallas_call(
        functools.partial(sum_terms_kernel, 1 + len(received)),
        grid=(1,),
        in_specs=[whole(received[0])] * (1 + len(received)) + [corner(token) for token in tokens],
        out_specs=whole(received[0]),
        out_shape=jax.ShapeDtypeStruct(received[0].shape, jnp.float32),
        compiler_params=pltpu.CompilerParams(vmem_limit_bytes=32 << 20),
    )(total, *received, *tokens)


def add_terms_kernel(count, own_ref, *refs):
    out_ref = refs[-1]
    first = 0
    for ref in refs[:count]:
        size = ref.shape[0]
        rows = pl.ds(first, size)
        out_ref[rows, :] = own_ref[rows, :] + ref[...]
        first += size


def add_terms(total, received, *tokens):
    block = sum(piece.shape[0] for piece in received)
    return pl.pallas_call(
        functools.partial(add_terms_kernel, len(received)),
        grid=(1,),
        in_specs=[pl.BlockSpec((block, LANES), lambda i: (0, 0))]
        + [whole(piece) for piece in received]
        + [corner(token) for token in tokens],
        out_specs=pl.BlockSpec((block, LANES), lambda i: (0, 0)),
        out_shape=jax.ShapeDtypeStruct((block, LANES), jnp.float32),
        compiler_params=pltpu.CompilerParams(vmem_limit_bytes=32 << 20),
    )(total, *received, *tokens)


def two_sum(a, b):
    total = a + b
    part = total - a
    return total, (a - (total - part)) + (b - part)


def quick_sum(a, b):
    total = a + b
    return total, b - (total - a)


def pair_add(a, b):
    total, error = two_sum(a[0], b[0])
    return quick_sum(total, error + (a[1] + b[1]))


def halves(a):
    scaled = a * 4097.0
    high = scaled - (scaled - a)
    return high, a - high


def product(a, b, a_parts, b_parts):
    whole = a * b
    error = (a_parts[0] * b_parts[0] - whole) + a_parts[0] * b_parts[1]
    error = (error + a_parts[1] * b_parts[0]) + a_parts[1] * b_parts[1]
    return whole, error


def gram_kernel(scale, terms_ref, picked_ref, gram_ref):
    cols = picked_ref.shape[0]
    turned = terms_ref[...].T
    picked = jnp.concatenate([turned[:cols], turned[cols:]], axis=1)
    picked_ref[...] = picked
    rest = picked * scale
    shift = jnp.max(jnp.abs(rest), axis=1, keepdims=True) * float(1 << 17)
    parts = []
    for _ in range(SLICES):
        part = (rest + shift) - shift
        rest = rest - part
        shift = shift * (1.0 / 64.0)
        parts.append(part.astype(jnp.bfloat16))
    total = None
    for level in range(SLICES):
        left = jnp.concatenate(parts[: level + 1], axis=1)
        right = jnp.concatenate(parts[: level + 1][::-1], axis=1)
        term = lax.dot_general(
            left, right, (((1,), (1,)), ((), ())), preferred_element_type=jnp.float32
        )
        if total is None:
            total = (term, jnp.zeros_like(term))
        else:
            high, error = two_sum(total[0], term)
            total = (high, total[1] + error)
    high, low = quick_sum(*total)
    gram_ref[...] = jnp.concatenate([high, low], axis=1)


def own_gram(terms, cols, per_device, scale):
    return pl.pallas_call(
        functools.partial(gram_kernel, scale),
        grid=(1,),
        in_specs=[whole(terms)],
        out_specs=(
            pl.BlockSpec((cols, per_device), lambda i: (0, 0)),
            pl.BlockSpec((cols, 2 * cols), lambda i: (0, 0)),
        ),
        out_shape=(
            jax.ShapeDtypeStruct((cols, per_device), jnp.float32),
            jax.ShapeDtypeStruct((cols, 2 * cols), jnp.float32),
        ),
    )(terms)


def tree_sum(values):
    while len(values) > 1:
        values = [pair_add(values[i], values[i + 1]) for i in range(0, len(values), 2)]
    return values[0]


def split_pair(packed):
    cols = packed.shape[0]
    return packed[:, :cols], packed[:, cols:]


def gram_sum_kernel(count, *refs):
    high, low = tree_sum([split_pair(ref[...]) for ref in refs[:count]])
    refs[-1][...] = jnp.concatenate([high, low], axis=1)


def gram_sum(grams, *tokens):
    return pl.pallas_call(
        functools.partial(gram_sum_kernel, len(grams)),
        grid=(1,),
        in_specs=[whole(gram) for gram in grams] + [corner(token) for token in tokens],
        out_specs=whole(grams[0]),
        out_shape=jax.ShapeDtypeStruct(grams[0].shape, jnp.float32),
    )(*grams, *tokens)


def factor_kernel(picked_ref, *refs):
    gram_refs, (r_ref, white_ref) = refs[:-2], refs[-2:]
    cols = r_ref.shape[0]
    high, low = tree_sum([split_pair(ref[...]) for ref in gram_refs])
    row_id = lax.broadcasted_iota(jnp.int32, (cols, cols), 0)
    lane_id = lax.broadcasted_iota(jnp.int32, (cols, cols), 1)
    unit = (row_id == lane_id).astype(jnp.float32)
    wide_high = jnp.concatenate([high, unit], axis=1)
    wide_low = jnp.concatenate([low, jnp.zeros_like(unit)], axis=1)
    tiles = cols // 8
    shape = (8, 2 * cols)
    rows = [
        (wide_high[t * 8 : (t + 1) * 8], wide_low[t * 8 : (t + 1) * 8])
        for t in range(tiles)
    ]
    sub_id = lax.broadcasted_iota(jnp.int32, shape, 0)
    for j in range(cols - 1):
        tile, sub = divmod(j, 8)
        row = [jnp.broadcast_to(v[sub : sub + 1], shape) for v in rows[tile]]
        pivot = [jnp.broadcast_to(v[sub : sub + 1, j : j + 1], shape) for v in rows[tile]]
        first = 1.0 / pivot[0]
        first_parts = halves(first)
        whole, error = product(pivot[0], first, halves(pivot[0]), first_parts)
        gap = ((1.0 - whole) - error) - pivot[1] * first
        inverse = quick_sum(first, first * gap)
        whole, error = product(row[0], inverse[0], halves(row[0]), halves(inverse[0]))
        scaled = quick_sum(whole, error + (row[0] * inverse[1] + row[1] * inverse[0]))
        scaled_parts = halves(scaled[0])
        for t in range(tile, tiles):
            if t == tile and sub == 7:
                continue
            high, low = rows[t]
            column = [jnp.broadcast_to(v[:, j : j + 1], shape) for v in rows[t]]
            if t == tile:
                column = [jnp.where(sub_id > sub, v, 0.0) for v in column]
            whole, error = product(column[0], scaled[0], halves(column[0]), scaled_parts)
            error = error + (column[0] * scaled[1] + column[1] * scaled[0])
            total, missed = two_sum(high, -whole)
            rows[t] = quick_sum(total, missed + (low - error))
    wide_high = jnp.concatenate([v[0] for v in rows], axis=0)
    wide_low = jnp.concatenate([v[1] for v in rows], axis=0)
    wide_row = lax.broadcasted_iota(jnp.int32, wide_high.shape, 0)
    wide_lane = lax.broadcasted_iota(jnp.int32, wide_high.shape, 1)
    diagonal = jnp.sum(jnp.where(wide_row == wide_lane, wide_high, 0.0), axis=1, keepdims=True)
    root = jnp.sqrt(diagonal)
    wide = (wide_high + wide_low) / root
    r_ref[...] = jnp.where(lane_id >= row_id, wide[:, :cols], 0.0)
    white_ref[...] = jnp.dot(
        wide[:, cols:],
        picked_ref[...],
        precision=lax.Precision.HIGHEST,
        preferred_element_type=jnp.float32,
    )


def factor_and_solve(picked, grams):
    cols = picked.shape[0]
    return pl.pallas_call(
        factor_kernel,
        grid=(1,),
        in_specs=[whole(value) for value in (picked, *grams)],
        out_specs=(pl.BlockSpec((cols, cols), lambda i: (0, 0)), whole(picked)),
        out_shape=(
            jax.ShapeDtypeStruct((cols, cols), jnp.float32),
            jax.ShapeDtypeStruct(picked.shape, jnp.float32),
        ),
        cost_estimate=pl.CostEstimate(
            flops=20_000_000, bytes_accessed=1 << 18, transcendentals=0
        ),
    )(picked, *grams)


def xor_permute(value, mask, device_count):
    return lax.ppermute(value, AXES, [(i, i ^ mask) for i in range(device_count)])


def in_groups(masks, size=2):
    odd = len(masks) % size
    groups = [masks[:odd]] if odd else []
    return groups + [masks[i : i + size] for i in range(odd, len(masks), size)]


def combined(masks, q):
    mask = 0
    for bit, value in enumerate(masks):
        if (q >> bit) & 1:
            mask |= value
    return mask


def local(panel, signs, sample_device, sample_offset):
    device_count = lax.axis_size(AXES)
    me = lax.axis_index(AXES).astype(jnp.int32)
    bits = device_count.bit_length() - 1
    cols, rows = panel.shape
    samples = sample_offset.shape[0]
    per_device = samples // device_count
    half = per_device // 2
    masks = [1 << bit for bit in range(bits)]

    signs_row = signs.reshape(1, rows)
    scale = 1.0 / math.sqrt(rows * device_count)
    top = masks[-1]
    peers = device_count // 2
    own_id = me.reshape(1)

    shares = (peers // 2, peers // 2)
    piece_a = local_mix(panel, signs_row, scale, shares, 0, cols // 2)
    (mix_b,) = local_mix(panel, signs_row, scale, (peers,), cols // 2, cols // 2)
    other_a = [xor_permute(piece, top, device_count) for piece in piece_a]

    def swap(value):
        return lax.all_to_all(value, AXES[1], split_axis=0, concat_axis=0, tiled=True)

    common = me & sample_device[:, 0]
    odd = lax.population_count(common) & 1
    code = sample_offset + odd * rows
    total = sampled_terms([*piece_a, mix_b], code, own_id, bits, half)
    received_b = swap(gate(mix_b, total))
    swapped_b = swap(mix_across(received_b))
    block = total.shape[0] // 2
    pieces = 2
    sent = [total[block + part * (block // pieces) :][: block // pieces] for part in range(pieces)]
    nearest = [xor_permute(piece, masks[0], device_count) for piece in sent]
    total = add_terms(total, nearest, other_a[0])
    far_ready = None
    groups = in_groups(masks[1:])
    for number, group in enumerate(groups):
        if number == len(groups) - 1:
            far_ready = total
        block = total.shape[0] >> len(group)
        received = []
        for q in range(1, 1 << len(group)):
            mask = combined(group[::-1], q)
            sent = total[q * block : (q + 1) * block]
            received.append(xor_permute(sent, mask, device_count))
        total = sum_terms(total, received, *([other_a[1]] if number == 0 else []))
    near_a = mix_far(own_id, piece_a, other_a, device_count, far_ready)
    received_a = swap(near_a)

    picked, gram = own_gram(total, cols, per_device, 1.0 / math.sqrt(samples))
    groups = groups[::-1] + [masks[:1]]
    for number, group in enumerate(groups):
        received = [gram] + [
            xor_permute(gram, combined(group, q), device_count) for q in range(1, 1 << len(group))
        ]
        if number < len(groups) - 1:
            gram = gram_sum(received, *([near_a] if number == 0 else []))
        if number == 0:
            swapped_a = swap(mix_across(received_a, gram))
            swapped_b = gate(swapped_b, gram)
            other_b = xor_permute(swapped_b, top, device_count)
    r_factor, whitened = factor_and_solve(picked, received)
    mixed = second_half(own_id, swapped_b, other_b, first_half(swapped_a, cols), device_count)
    return (mixed, r_factor, whitened)


def solution(mesh):
    view = Mesh(mesh.devices.reshape(2, -1), AXES)
    return jax.shard_map(
        local,
        mesh=view,
        in_specs=(P(None, AXES), P(AXES), P(), P()),
        out_specs=(P(None, AXES), P(), P(None, AXES)),
        check_vma=False,
    )
```

```python
import functools
import math

import jax
import jax.numpy as jnp
from jax import lax
from jax.experimental import pallas as pl
from jax.experimental.pallas import tpu as pltpu
from jax.sharding import Mesh
from jax.sharding import PartitionSpec as P

AXES = ("far", "near")
LANES = 128
GROUP = 16
SLICES = 6


def hadamard_table(order_size):
    shape = (order_size, order_size)
    common = lax.broadcasted_iota(jnp.int32, shape, 0) & lax.broadcasted_iota(jnp.int32, shape, 1)
    for distance in (4, 2, 1):
        common = common ^ (common >> distance)
    return (1 - 2 * (common & 1)).astype(jnp.float32).astype(jnp.bfloat16)


def whole(value):
    return pl.BlockSpec(value.shape, lambda i: (0,) * len(value.shape))


def corner(value):
    lead = (1,) * (len(value.shape) - 2)
    return pl.BlockSpec(lead + (8, LANES), lambda i: (0,) * len(value.shape))


def in_hbm(value):
    return pltpu.with_memory_space_constraint(value, pltpu.HBM)


def mix_kernel(scale, panel_ref, signs_ref, *out_refs):
    cols, rows = panel_ref.shape
    inner = rows // LANES
    width = out_refs[0].shape[2]
    places = [(ref, peer) for ref in out_refs for peer in range(ref.shape[0])]
    step = min(width, LANES)
    table = hadamard_table(LANES)
    signs = signs_ref[...].astype(jnp.float32) * scale
    for first in range(0, cols, 8):
        flipped = panel_ref[first : first + 8, :] * signs
        stacked = jnp.concatenate(
            [flipped[:, a * LANES : (a + 1) * LANES] for a in range(inner)], axis=0
        )
        total = None
        rest = stacked
        for piece in range(3):
            part = rest.astype(jnp.bfloat16)
            term = jnp.dot(part, table, preferred_element_type=jnp.float32)
            total = term if total is None else total + term
            if piece < 2:
                rest = rest - part.astype(jnp.float32)
        blocks = [total[a * 8 : (a + 1) * 8] for a in range(inner)]
        span = 1
        while span < inner:
            for a in range(inner):
                if a & span == 0:
                    left, right = blocks[a], blocks[a + span]
                    blocks[a], blocks[a + span] = left + right, left - right
            span *= 2
        for start in range(0, rows, step):
            block = blocks[start // LANES][:, start % LANES : start % LANES + step]
            out_ref, peer = places[start // width]
            lane = start % width
            out_ref[peer, first : first + 8, lane : lane + step] = block


def local_mix(panel, signs_row, scale, shares, first, count):
    rows = panel.shape[1]
    width = rows // sum(shares)
    return pl.pallas_call(
        functools.partial(mix_kernel, scale),
        grid=(count // GROUP,),
        in_specs=[
            pl.BlockSpec((GROUP, rows), lambda i: (first // GROUP + i, 0)),
            pl.BlockSpec((1, rows), lambda i: (0, 0)),
        ],
        out_specs=tuple(pl.BlockSpec((n, GROUP, width), lambda i: (0, i, 0)) for n in shares),
        out_shape=tuple(pltpu.HBM((n, count, width), jnp.float32) for n in shares),
        compiler_params=pltpu.CompilerParams(vmem_limit_bytes=32 << 20),
    )(in_hbm(panel), in_hbm(signs_row))


def across_kernel(in_ref, *refs):
    out_ref = refs[-1]
    peers = in_ref.shape[0]
    step = min(in_ref.shape[2], LANES)
    for lane in range(0, in_ref.shape[2], step):
        for first in range(0, in_ref.shape[1], 8):
            columns = pl.ds(first, 8)
            blocks = [in_ref[p, columns, lane : lane + step] for p in range(peers)]
            span = 1
            while span < peers:
                for p in range(peers):
                    if p & span == 0:
                        left, right = blocks[p], blocks[p + span]
                        blocks[p], blocks[p + span] = left + right, left - right
                span *= 2
            for p in range(peers):
                out_ref[p, columns, lane : lane + step] = blocks[p]


def mix_across(received, *tokens):
    peers, cols, width = received.shape
    spec = pl.BlockSpec((peers, GROUP, width), lambda i: (0, i, 0))
    return pl.pallas_call(
        across_kernel,
        grid=(cols // GROUP,),
        in_specs=[spec] + [corner(token) for token in tokens],
        out_specs=spec,
        out_shape=pltpu.HBM(received.shape, jnp.float32),
        compiler_params=pltpu.CompilerParams(vmem_limit_bytes=32 << 20),
    )(received, *tokens)


def far_sign(me_ref, device_count):
    return jnp.where(me_ref[0] < device_count // 2, jnp.float32(1.0), jnp.float32(-1.0))


def far_kernel(device_count, me_ref, *refs):
    sign = far_sign(me_ref, device_count)
    own, other, out_ref = refs[:2], refs[2:4], refs[-1]
    peer = 0
    for piece in range(2):
        for p in range(own[piece].shape[0]):
            out_ref[peer] = other[piece][p] + sign * own[piece][p]
            peer += 1


def mix_far(me, own, other, device_count, token):
    peers = own[0].shape[0] + own[1].shape[0]
    _, cols, width = own[0].shape
    pieces = [*own, *other]
    specs = [pl.BlockSpec((v.shape[0], GROUP, width), lambda i: (0, i, 0)) for v in pieces]
    return pl.pallas_call(
        functools.partial(far_kernel, device_count),
        grid=(cols // GROUP,),
        in_specs=[pl.BlockSpec(memory_space=pltpu.SMEM)] + specs + [corner(token)],
        out_specs=pl.BlockSpec((peers, GROUP, width), lambda i: (0, i, 0)),
        out_shape=pltpu.HBM((peers, cols, width), jnp.float32),
        compiler_params=pltpu.CompilerParams(vmem_limit_bytes=32 << 20),
    )(me, *pieces, token)


def take_kernel(in_ref, *refs):
    refs[-1][...] = in_ref[...]


def take_half(value, part, *tokens):
    peers, cols, width = value.shape
    return pl.pallas_call(
        take_kernel,
        grid=(cols // GROUP,),
        in_specs=[pl.BlockSpec((peers // 2, GROUP, width), lambda i: (part, i, 0))]
        + [corner(token) for token in tokens],
        out_specs=pl.BlockSpec((peers // 2, GROUP, width), lambda i: (0, i, 0)),
        out_shape=pltpu.HBM((peers // 2, cols, width), jnp.float32),
    )(value, *tokens)


def first_half_kernel(in_ref, out_ref):
    peers, _, width = in_ref.shape
    for p in range(peers):
        out_ref[:, p * width : (p + 1) * width] = in_ref[p]


def first_half(received, cols):
    peers, count, width = received.shape
    return pl.pallas_call(
        first_half_kernel,
        grid=(count // GROUP,),
        in_specs=[pl.BlockSpec((peers, GROUP, width), lambda i: (0, i, 0))],
        out_specs=pl.BlockSpec((GROUP, peers * width), lambda i: (i, 0)),
        out_shape=pltpu.HBM((cols, peers * width), jnp.float32),
        compiler_params=pltpu.CompilerParams(vmem_limit_bytes=32 << 20),
    )(received)


def second_half_kernel(device_count, me_ref, own_ref, low_ref, high_ref, whole_ref, out_ref):
    del whole_ref
    sign = far_sign(me_ref, device_count)
    share, _, width = low_ref.shape
    for p in range(2 * share):
        other = low_ref[p] if p < share else high_ref[p - share]
        out_ref[:, p * width : (p + 1) * width] = other + sign * own_ref[p]


def second_half(me, own, other, mixed, device_count):
    peers, count, width = own.shape
    skipped = (mixed.shape[0] - count) // GROUP
    share = pl.BlockSpec((peers // 2, GROUP, width), lambda i: (0, i, 0))
    return pl.pallas_call(
        functools.partial(second_half_kernel, device_count),
        grid=(count // GROUP,),
        in_specs=[
            pl.BlockSpec(memory_space=pltpu.SMEM),
            pl.BlockSpec((peers, GROUP, width), lambda i: (0, i, 0)),
            share,
            share,
            pl.BlockSpec(memory_space=pltpu.HBM),
        ],
        out_specs=pl.BlockSpec((GROUP, peers * width), lambda i: (skipped + i, 0)),
        out_shape=pltpu.HBM(mixed.shape, jnp.float32),
        input_output_aliases={4: 0},
        compiler_params=pltpu.CompilerParams(vmem_limit_bytes=32 << 20),
    )(me, own, *other, mixed)


def terms_kernel(bits, half, code_ref, me_ref, *refs):
    far_refs, (out_ref, mix_ref, table_ref, done_sem) = refs[:3], refs[-4:]
    peers, _, width = mix_ref.shape
    rows = peers * width
    me = me_ref[0]
    share, cols, _ = far_refs[0].shape
    pieces = [
        (far_refs[0], pl.ds(0, share), pl.ds(0, cols)),
        (far_refs[1], pl.ds(share, peers - share), pl.ds(0, cols)),
        (far_refs[2], pl.ds(0, peers), pl.ds(cols, cols)),
    ]
    copies = [
        pltpu.make_async_copy(ref, mix_ref.at[part, columns], done_sem.at[number])
        for number, (ref, part, columns) in enumerate(pieces)
    ]
    for copy in copies:
        copy.start()

    def transpose_block(p, carry):
        for lane in range(0, width, LANES):
            start = pl.multiple_of(p * width + lane, LANES)
            tile = mix_ref[p, :, lane : lane + LANES]
            turned = jnp.concatenate([tile, tile], axis=0).T
            table_ref[pl.ds(start, LANES), :] = turned
            table_ref[pl.ds(rows + start, LANES), :] = -turned
        return carry

    for copy in copies:
        copy.wait()
    lax.fori_loop(0, peers, transpose_block, 0)
    first_lanes = lax.broadcasted_iota(jnp.int32, (1, LANES), 1) < LANES // 2

    def gather_block(r, carry):
        mask = jnp.int32(0)
        for bit in range(bits):
            mask = mask | (((r >> bit) & 1) << (bits - 1 - bit))
        source = (me ^ mask) * (2 * half)
        target = pl.multiple_of(r * half, half)
        for j in range(half):
            upper = table_ref[pl.ds(code_ref[source + j], 1), :]
            lower = table_ref[pl.ds(code_ref[source + half + j], 1), :]
            out_ref[pl.ds(target + j, 1), :] = jnp.where(first_lanes, upper, lower)
        return carry

    lax.fori_loop(0, 1 << bits, gather_block, 0)


def sampled_terms(pieces, code, me, bits, half):
    peers, cols, width = pieces[-1].shape
    count = half << bits
    return pl.pallas_call(
        functools.partial(terms_kernel, bits, half),
        grid=(1,),
        in_specs=[pl.BlockSpec(memory_space=pltpu.SMEM)] * 2
        + [pl.BlockSpec(memory_space=pltpu.HBM)] * len(pieces),
        out_specs=pl.BlockSpec((count, LANES), lambda i: (0, 0)),
        out_shape=jax.ShapeDtypeStruct((count, LANES), jnp.float32),
        scratch_shapes=[
            pltpu.VMEM((peers, 2 * cols, width), jnp.float32),
            pltpu.VMEM((2 * peers * width, LANES), jnp.float32),
            pltpu.SemaphoreType.DMA((len(pieces),)),
        ],
        compiler_params=pltpu.CompilerParams(vmem_limit_bytes=40 << 20),
    )(code, me, *[in_hbm(piece) for piece in pieces])


def sum_terms_kernel(count, *refs):
    total = refs[0][...]
    for ref in refs[1:count]:
        total = total + ref[...]
    refs[-1][...] = total


def sum_terms(total, received, *tokens):
    return pl.pallas_call(
        functools.partial(sum_terms_kernel, 1 + len(received)),
        grid=(1,),
        in_specs=[whole(received[0])] * (1 + len(received)) + [corner(token) for token in tokens],
        out_specs=whole(received[0]),
        out_shape=jax.ShapeDtypeStruct(received[0].shape, jnp.float32),
        compiler_params=pltpu.CompilerParams(vmem_limit_bytes=32 << 20),
    )(total, *received, *tokens)


def add_terms_kernel(count, own_ref, *refs):
    out_ref = refs[-1]
    first = 0
    for ref in refs[:count]:
        size = ref.shape[0]
        rows = pl.ds(first, size)
        out_ref[rows, :] = own_ref[rows, :] + ref[...]
        first += size


def add_terms(total, received, *tokens):
    block = sum(piece.shape[0] for piece in received)
    return pl.pallas_call(
        functools.partial(add_terms_kernel, len(received)),
        grid=(1,),
        in_specs=[pl.BlockSpec((block, LANES), lambda i: (0, 0))]
        + [whole(piece) for piece in received]
        + [corner(token) for token in tokens],
        out_specs=pl.BlockSpec((block, LANES), lambda i: (0, 0)),
        out_shape=jax.ShapeDtypeStruct((block, LANES), jnp.float32),
        compiler_params=pltpu.CompilerParams(vmem_limit_bytes=32 << 20),
    )(total, *received, *tokens)


def two_sum(a, b):
    total = a + b
    part = total - a
    return total, (a - (total - part)) + (b - part)


def quick_sum(a, b):
    total = a + b
    return total, b - (total - a)


def pair_add(a, b):
    total, error = two_sum(a[0], b[0])
    return quick_sum(total, error + (a[1] + b[1]))


def halves(a):
    scaled = a * 4097.0
    high = scaled - (scaled - a)
    return high, a - high


def product(a, b, a_parts, b_parts):
    whole = a * b
    error = (a_parts[0] * b_parts[0] - whole) + a_parts[0] * b_parts[1]
    error = (error + a_parts[1] * b_parts[0]) + a_parts[1] * b_parts[1]
    return whole, error


def gram_kernel(scale, terms_ref, picked_ref, gram_ref):
    cols = picked_ref.shape[0]
    turned = terms_ref[...].T
    picked = jnp.concatenate([turned[:cols], turned[cols:]], axis=1)
    picked_ref[...] = picked
    rest = picked * scale
    shift = jnp.max(jnp.abs(rest), axis=1, keepdims=True) * float(1 << 17)
    parts = []
    for _ in range(SLICES):
        part = (rest + shift) - shift
        rest = rest - part
        shift = shift * (1.0 / 64.0)
        parts.append(part.astype(jnp.bfloat16))
    total = None
    for level in range(SLICES):
        left = jnp.concatenate(parts[: level + 1], axis=1)
        right = jnp.concatenate(parts[: level + 1][::-1], axis=1)
        term = lax.dot_general(
            left, right, (((1,), (1,)), ((), ())), preferred_element_type=jnp.float32
        )
        if total is None:
            total = (term, jnp.zeros_like(term))
        else:
            high, error = two_sum(total[0], term)
            total = (high, total[1] + error)
    high, low = quick_sum(*total)
    gram_ref[...] = jnp.concatenate([high, low], axis=1)


def own_gram(terms, cols, per_device, scale):
    return pl.pallas_call(
        functools.partial(gram_kernel, scale),
        grid=(1,),
        in_specs=[whole(terms)],
        out_specs=(
            pl.BlockSpec((cols, per_device), lambda i: (0, 0)),
            pl.BlockSpec((cols, 2 * cols), lambda i: (0, 0)),
        ),
        out_shape=(
            jax.ShapeDtypeStruct((cols, per_device), jnp.float32),
            jax.ShapeDtypeStruct((cols, 2 * cols), jnp.float32),
        ),
    )(terms)


def tree_sum(values):
    while len(values) > 1:
        values = [pair_add(values[i], values[i + 1]) for i in range(0, len(values), 2)]
    return values[0]


def split_pair(packed):
    cols = packed.shape[0]
    return packed[:, :cols], packed[:, cols:]


def gram_sum_kernel(count, *refs):
    high, low = tree_sum([split_pair(ref[...]) for ref in refs[:count]])
    refs[-1][...] = jnp.concatenate([high, low], axis=1)


def gram_sum(grams, *tokens):
    return pl.pallas_call(
        functools.partial(gram_sum_kernel, len(grams)),
        grid=(1,),
        in_specs=[whole(gram) for gram in grams] + [corner(token) for token in tokens],
        out_specs=whole(grams[0]),
        out_shape=jax.ShapeDtypeStruct(grams[0].shape, jnp.float32),
    )(*grams, *tokens)


def factor_kernel(picked_ref, *refs):
    gram_refs, (r_ref, white_ref) = refs[:-2], refs[-2:]
    cols = r_ref.shape[0]
    high, low = tree_sum([split_pair(ref[...]) for ref in gram_refs])
    row_id = lax.broadcasted_iota(jnp.int32, (cols, cols), 0)
    lane_id = lax.broadcasted_iota(jnp.int32, (cols, cols), 1)
    unit = (row_id == lane_id).astype(jnp.float32)
    wide_high = jnp.concatenate([high, unit], axis=1)
    wide_low = jnp.concatenate([low, jnp.zeros_like(unit)], axis=1)
    tiles = cols // 8
    shape = (8, 2 * cols)
    rows = [
        (wide_high[t * 8 : (t + 1) * 8], wide_low[t * 8 : (t + 1) * 8])
        for t in range(tiles)
    ]
    sub_id = lax.broadcasted_iota(jnp.int32, shape, 0)
    for j in range(cols - 1):
        tile, sub = divmod(j, 8)
        row = [jnp.broadcast_to(v[sub : sub + 1], shape) for v in rows[tile]]
        pivot = [jnp.broadcast_to(v[sub : sub + 1, j : j + 1], shape) for v in rows[tile]]
        first = 1.0 / pivot[0]
        first_parts = halves(first)
        whole, error = product(pivot[0], first, halves(pivot[0]), first_parts)
        gap = ((1.0 - whole) - error) - pivot[1] * first
        inverse = quick_sum(first, first * gap)
        whole, error = product(row[0], inverse[0], halves(row[0]), halves(inverse[0]))
        scaled = quick_sum(whole, error + (row[0] * inverse[1] + row[1] * inverse[0]))
        scaled_parts = halves(scaled[0])
        for t in range(tile, tiles):
            if t == tile and sub == 7:
                continue
            high, low = rows[t]
            column = [jnp.broadcast_to(v[:, j : j + 1], shape) for v in rows[t]]
            if t == tile:
                column = [jnp.where(sub_id > sub, v, 0.0) for v in column]
            whole, error = product(column[0], scaled[0], halves(column[0]), scaled_parts)
            error = error + (column[0] * scaled[1] + column[1] * scaled[0])
            total, missed = two_sum(high, -whole)
            rows[t] = quick_sum(total, missed + (low - error))
    wide_high = jnp.concatenate([v[0] for v in rows], axis=0)
    wide_low = jnp.concatenate([v[1] for v in rows], axis=0)
    wide_row = lax.broadcasted_iota(jnp.int32, wide_high.shape, 0)
    wide_lane = lax.broadcasted_iota(jnp.int32, wide_high.shape, 1)
    diagonal = jnp.sum(jnp.where(wide_row == wide_lane, wide_high, 0.0), axis=1, keepdims=True)
    root = jnp.sqrt(diagonal)
    wide = (wide_high + wide_low) / root
    r_ref[...] = jnp.where(lane_id >= row_id, wide[:, :cols], 0.0)
    white_ref[...] = jnp.dot(
        wide[:, cols:],
        picked_ref[...],
        precision=lax.Precision.HIGHEST,
        preferred_element_type=jnp.float32,
    )


def factor_and_solve(picked, grams):
    cols = picked.shape[0]
    return pl.pallas_call(
        factor_kernel,
        grid=(1,),
        in_specs=[whole(value) for value in (picked, *grams)],
        out_specs=(pl.BlockSpec((cols, cols), lambda i: (0, 0)), whole(picked)),
        out_shape=(
            jax.ShapeDtypeStruct((cols, cols), jnp.float32),
            jax.ShapeDtypeStruct(picked.shape, jnp.float32),
        ),
        cost_estimate=pl.CostEstimate(
            flops=20_000_000, bytes_accessed=1 << 18, transcendentals=0
        ),
    )(picked, *grams)


def xor_permute(value, mask, device_count):
    return lax.ppermute(value, AXES, [(i, i ^ mask) for i in range(device_count)])


def in_groups(masks, size=2):
    odd = len(masks) % size
    groups = [masks[:odd]] if odd else []
    return groups + [masks[i : i + size] for i in range(odd, len(masks), size)]


def combined(masks, q):
    mask = 0
    for bit, value in enumerate(masks):
        if (q >> bit) & 1:
            mask |= value
    return mask


def local(panel, signs, sample_device, sample_offset):
    device_count = lax.axis_size(AXES)
    me = lax.axis_index(AXES).astype(jnp.int32)
    bits = device_count.bit_length() - 1
    cols, rows = panel.shape
    samples = sample_offset.shape[0]
    per_device = samples // device_count
    half = per_device // 2
    masks = [1 << bit for bit in range(bits)]

    signs_row = signs.reshape(1, rows)
    scale = 1.0 / math.sqrt(rows * device_count)
    top = masks[-1]
    peers = device_count // 2
    own_id = me.reshape(1)

    shares = (peers // 2, peers // 2)
    piece_a = local_mix(panel, signs_row, scale, shares, 0, cols // 2)
    (mix_b,) = local_mix(panel, signs_row, scale, (peers,), cols // 2, cols // 2)
    other_a = [xor_permute(piece, top, device_count) for piece in piece_a]

    def swap(value):
        return lax.all_to_all(value, AXES[1], split_axis=0, concat_axis=0, tiled=True)

    common = me & sample_device[:, 0]
    odd = lax.population_count(common) & 1
    code = sample_offset + odd * rows
    total = sampled_terms([*piece_a, mix_b], code, own_id, bits, half)
    received_b = swap(mix_b)
    across_b = mix_across(received_b, total)
    swapped_b = swap(across_b)
    block = total.shape[0] // 2
    pieces = 2
    sent = [total[block + part * (block // pieces) :][: block // pieces] for part in range(pieces)]
    nearest = [xor_permute(piece, masks[0], device_count) for piece in sent]
    total = add_terms(total, nearest, other_a[0], across_b)
    groups = in_groups(masks[1:])
    for number, group in enumerate(groups):
        block = total.shape[0] >> len(group)
        received = []
        for q in range(1, 1 << len(group)):
            mask = combined(group[::-1], q)
            sent = total[q * block : (q + 1) * block]
            received.append(xor_permute(sent, mask, device_count))
        last = number == len(groups) - 1
        total = sum_terms(total, received, *([other_a[1]] if last else []))
    near_a = mix_far(own_id, piece_a, other_a, device_count, swapped_b)
    received_a = swap(near_a)

    picked, gram = own_gram(total, cols, per_device, 1.0 / math.sqrt(samples))
    low_b = xor_permute(take_half(swapped_b, 0, gram), top, device_count)
    groups = groups[::-1] + [masks[:1]]
    for number, group in enumerate(groups):
        received = [gram] + [
            xor_permute(gram, combined(group, q), device_count) for q in range(1, 1 << len(group))
        ]
        if number < len(groups) - 1:
            gram = gram_sum(received, *([near_a] if number == 0 else []))
        if number == 0:
            swapped_a = swap(mix_across(received_a, gram))
            high_b = xor_permute(take_half(swapped_b, 1, gram, low_b), top, device_count)
    r_factor, whitened = factor_and_solve(picked, received)
    mixed = second_half(
        own_id, swapped_b, (low_b, high_b), first_half(swapped_a, cols), device_count
    )
    return (mixed, r_factor, whitened)


def solution(mesh):
    view = Mesh(mesh.devices.reshape(2, -1), AXES)
    return jax.shard_map(
        local,
        mesh=view,
        in_specs=(P(None, AXES), P(AXES), P(), P()),
        out_specs=(P(None, AXES), P(), P(None, AXES)),
        check_vma=False,
    )
```

```python
import functools
import math

import jax
import jax.numpy as jnp
import numpy as np
from jax import lax
from jax.experimental import pallas as pl
from jax.experimental.pallas import tpu as pltpu
from jax.sharding import PartitionSpec as P

AXES = ("rows", "sk")
LANES = 128
GROUP = 16
SLICES = 6


def hadamard_table(order_size):
    shape = (order_size, order_size)
    common = lax.broadcasted_iota(jnp.int32, shape, 0) & lax.broadcasted_iota(jnp.int32, shape, 1)
    for distance in (4, 2, 1):
        common = common ^ (common >> distance)
    return (1 - 2 * (common & 1)).astype(jnp.float32).astype(jnp.bfloat16)


def whole(value):
    return pl.BlockSpec(value.shape, lambda i: (0,) * len(value.shape))


def in_hbm(value):
    return pltpu.with_memory_space_constraint(value, pltpu.HBM)


def mix_kernel(scale, panel_ref, signs_ref, out_ref):
    cols, rows = panel_ref.shape
    inner = rows // LANES
    width = out_ref.shape[2]
    step = min(width, LANES)
    table = hadamard_table(LANES)
    signs = signs_ref[...].astype(jnp.float32) * scale
    for first in range(0, cols, 8):
        flipped = panel_ref[first : first + 8, :] * signs
        stacked = jnp.concatenate(
            [flipped[:, a * LANES : (a + 1) * LANES] for a in range(inner)], axis=0
        )
        total = None
        rest = stacked
        for piece in range(3):
            part = rest.astype(jnp.bfloat16)
            term = jnp.dot(part, table, preferred_element_type=jnp.float32)
            total = term if total is None else total + term
            if piece < 2:
                rest = rest - part.astype(jnp.float32)
        blocks = [total[a * 8 : (a + 1) * 8] for a in range(inner)]
        span = 1
        while span < inner:
            for a in range(inner):
                if a & span == 0:
                    left, right = blocks[a], blocks[a + span]
                    blocks[a], blocks[a + span] = left + right, left - right
            span *= 2
        for start in range(0, rows, step):
            block = blocks[start // LANES][:, start % LANES : start % LANES + step]
            out_ref[start // width, first : first + 8, start % width : start % width + step] = block


def local_mix(panel, signs_row, scale, peers):
    cols, rows = panel.shape
    width = rows // peers
    return pl.pallas_call(
        functools.partial(mix_kernel, scale),
        grid=(cols // GROUP,),
        in_specs=[
            pl.BlockSpec((GROUP, rows), lambda i: (i, 0)),
            pl.BlockSpec((1, rows), lambda i: (0, 0)),
        ],
        out_specs=pl.BlockSpec((peers, GROUP, width), lambda i: (0, i, 0)),
        out_shape=pltpu.HBM((peers, cols, width), jnp.float32),
        compiler_params=pltpu.CompilerParams(vmem_limit_bytes=32 << 20),
    )(in_hbm(panel), in_hbm(signs_row))


def across_kernel(in_ref, token_ref, out_ref):
    del token_ref
    peers = in_ref.shape[0]
    step = min(in_ref.shape[2], LANES)
    for lane in range(0, in_ref.shape[2], step):
        for first in range(0, in_ref.shape[1], 8):
            columns = pl.ds(first, 8)
            blocks = [in_ref[p, columns, lane : lane + step] for p in range(peers)]
            span = 1
            while span < peers:
                for p in range(peers):
                    if p & span == 0:
                        left, right = blocks[p], blocks[p + span]
                        blocks[p], blocks[p + span] = left + right, left - right
                span *= 2
            for p in range(peers):
                out_ref[p, columns, lane : lane + step] = blocks[p]


def mix_across(received, token):
    peers, cols, width = received.shape
    spec = pl.BlockSpec((peers, GROUP, width), lambda i: (0, i, 0))
    return pl.pallas_call(
        across_kernel,
        grid=(cols // GROUP,),
        in_specs=[spec, pl.BlockSpec((8, LANES), lambda i: (0, 0))],
        out_specs=spec,
        out_shape=pltpu.HBM(received.shape, jnp.float32),
        compiler_params=pltpu.CompilerParams(vmem_limit_bytes=32 << 20),
    )(received, token)


def lay_out_kernel(in_ref, out_ref):
    peers, _, width = in_ref.shape
    for p in range(peers):
        out_ref[:, p * width : (p + 1) * width] = in_ref[p]


def lay_out(received):
    peers, cols, width = received.shape
    return pl.pallas_call(
        lay_out_kernel,
        grid=(cols // GROUP,),
        in_specs=[pl.BlockSpec((peers, GROUP, width), lambda i: (0, i, 0))],
        out_specs=pl.BlockSpec((GROUP, peers * width), lambda i: (i, 0)),
        out_shape=jax.ShapeDtypeStruct((cols, peers * width), jnp.float32),
        compiler_params=pltpu.CompilerParams(vmem_limit_bytes=32 << 20),
    )(received)


def terms_kernel(bits, half, code_ref, me_ref, far_ref, out_ref, mix_ref, table_ref, done_sem):
    peers, _, width = mix_ref.shape
    pieces = [
        pltpu.make_async_copy(far_ref.at[part], mix_ref.at[part], done_sem.at[number])
        for number, part in enumerate([pl.ds(0, peers // 2), pl.ds(peers // 2, peers // 2)])
    ]
    for piece in pieces:
        piece.start()
    rows = peers * width
    me = me_ref[0]

    span = max(1, LANES // width)

    def transpose_block(number, carry):
        p = number * span
        for lane in range(0, max(width, LANES), LANES):
            start = pl.multiple_of(p * width + lane, LANES)
            tile = jnp.concatenate(
                [mix_ref[p + i, :, lane : lane + min(width, LANES)] for i in range(span)], axis=1
            )
            turned = jnp.concatenate([tile, tile], axis=0).T
            table_ref[pl.ds(start, LANES), :] = turned
            table_ref[pl.ds(rows + start, LANES), :] = -turned
        return carry

    for number, piece in enumerate(pieces):
        piece.wait()
        count = peers // 2 // span
        lax.fori_loop(number * count, (number + 1) * count, transpose_block, 0)
    first_half = lax.broadcasted_iota(jnp.int32, (1, LANES), 1) < LANES // 2

    def gather_block(r, carry):
        mask = jnp.int32(0)
        for bit in range(bits):
            mask = mask | (((r >> bit) & 1) << (bits - 1 - bit))
        source = (me ^ mask) * (2 * half)
        target = pl.multiple_of(r * half, half)
        for j in range(half):
            upper = table_ref[pl.ds(code_ref[source + j], 1), :]
            lower = table_ref[pl.ds(code_ref[source + half + j], 1), :]
            out_ref[pl.ds(target + j, 1), :] = jnp.where(first_half, upper, lower)
        return carry

    lax.fori_loop(0, 1 << bits, gather_block, 0)


def sampled_terms(mix, code, me, bits, half):
    rows = mix.shape[0] * mix.shape[2]
    count = half << bits
    return pl.pallas_call(
        functools.partial(terms_kernel, bits, half),
        in_specs=[pl.BlockSpec(memory_space=pltpu.SMEM)] * 2
        + [pl.BlockSpec(memory_space=pltpu.HBM)],
        out_specs=pl.BlockSpec(memory_space=pltpu.VMEM),
        out_shape=jax.ShapeDtypeStruct((count, LANES), jnp.float32),
        scratch_shapes=[
            pltpu.VMEM(mix.shape, jnp.float32),
            pltpu.VMEM((2 * rows, LANES), jnp.float32),
            pltpu.SemaphoreType.DMA((2,)),
        ],
        compiler_params=pltpu.CompilerParams(vmem_limit_bytes=40 << 20),
        cost_estimate=pl.CostEstimate(
            flops=count * LANES * 40, bytes_accessed=24 << 20, transcendentals=0
        ),
    )(code, me, in_hbm(mix))


def two_sum(a, b):
    total = a + b
    part = total - a
    return total, (a - (total - part)) + (b - part)


def quick_sum(a, b):
    total = a + b
    return total, b - (total - a)


def pair_add(a, b):
    total, error = two_sum(a[0], b[0])
    return quick_sum(total, error + (a[1] + b[1]))


def halves(a):
    scaled = a * 4097.0
    high = scaled - (scaled - a)
    return high, a - high


def product(a, b, a_parts, b_parts):
    whole = a * b
    error = (a_parts[0] * b_parts[0] - whole) + a_parts[0] * b_parts[1]
    error = (error + a_parts[1] * b_parts[0]) + a_parts[1] * b_parts[1]
    return whole, error


def gram_kernel(scale, terms_ref, picked_ref, gram_ref):
    cols = picked_ref.shape[0]
    turned = terms_ref[...].T
    picked = jnp.concatenate([turned[:cols], turned[cols:]], axis=1)
    picked_ref[...] = picked
    rest = picked * scale
    shift = jnp.max(jnp.abs(rest), axis=1, keepdims=True) * float(1 << 17)
    parts = []
    for _ in range(SLICES):
        part = (rest + shift) - shift
        rest = rest - part
        shift = shift * (1.0 / 64.0)
        parts.append(part.astype(jnp.bfloat16))
    total = None
    for level in range(SLICES):
        left = jnp.concatenate(parts[: level + 1], axis=1)
        right = jnp.concatenate(parts[: level + 1][::-1], axis=1)
        term = lax.dot_general(
            left, right, (((1,), (1,)), ((), ())), preferred_element_type=jnp.float32
        )
        if total is None:
            total = (term, jnp.zeros_like(term))
        else:
            high, error = two_sum(total[0], term)
            total = (high, total[1] + error)
    high, low = quick_sum(*total)
    gram_ref[...] = jnp.concatenate([high, low], axis=1)


def own_gram(terms, cols, per_device, scale):
    return pl.pallas_call(
        functools.partial(gram_kernel, scale),
        grid=(1,),
        in_specs=[whole(terms)],
        out_specs=(
            pl.BlockSpec((cols, per_device), lambda i: (0, 0)),
            pl.BlockSpec((cols, 2 * cols), lambda i: (0, 0)),
        ),
        out_shape=(
            jax.ShapeDtypeStruct((cols, per_device), jnp.float32),
            jax.ShapeDtypeStruct((cols, 2 * cols), jnp.float32),
        ),
    )(terms)


def tree_sum(values):
    while len(values) > 1:
        values = [pair_add(values[i], values[i + 1]) for i in range(0, len(values), 2)]
    return values[0]


def split_pair(packed):
    cols = packed.shape[0]
    return packed[:, :cols], packed[:, cols:]


def gram_sum_kernel(count, *refs):
    high, low = tree_sum([split_pair(ref[...]) for ref in refs[:count]])
    refs[-1][...] = jnp.concatenate([high, low], axis=1)


def gram_sum(grams, *through):
    count = len(grams)
    in_place = pl.BlockSpec(memory_space=pltpu.HBM)
    return pl.pallas_call(
        functools.partial(gram_sum_kernel, count),
        grid=(1,),
        in_specs=[whole(gram) for gram in grams] + [in_place] * len(through),
        out_specs=tuple([in_place] * len(through) + [whole(grams[0])]),
        out_shape=tuple(
            [pltpu.HBM(v.shape, v.dtype) for v in through]
            + [jax.ShapeDtypeStruct(grams[0].shape, jnp.float32)]
        ),
        input_output_aliases={count + i: i for i in range(len(through))},
    )(*grams, *through)


def factor_kernel(picked_ref, *refs):
    gram_refs, (r_ref, white_ref) = refs[:-2], refs[-2:]
    cols = r_ref.shape[0]
    high, low = tree_sum([split_pair(ref[...]) for ref in gram_refs])
    row_id = lax.broadcasted_iota(jnp.int32, (cols, cols), 0)
    lane_id = lax.broadcasted_iota(jnp.int32, (cols, cols), 1)
    unit = (row_id == lane_id).astype(jnp.float32)
    wide_high = jnp.concatenate([high, unit], axis=1)
    wide_low = jnp.concatenate([low, jnp.zeros_like(unit)], axis=1)
    tiles = cols // 8
    shape = (8, 2 * cols)
    rows = [
        (wide_high[t * 8 : (t + 1) * 8], wide_low[t * 8 : (t + 1) * 8])
        for t in range(tiles)
    ]
    sub_id = lax.broadcasted_iota(jnp.int32, shape, 0)
    for j in range(cols - 1):
        tile, sub = divmod(j, 8)
        row = [jnp.broadcast_to(v[sub : sub + 1], shape) for v in rows[tile]]
        pivot = [jnp.broadcast_to(v[sub : sub + 1, j : j + 1], shape) for v in rows[tile]]
        first = 1.0 / pivot[0]
        first_parts = halves(first)
        whole, error = product(pivot[0], first, halves(pivot[0]), first_parts)
        gap = ((1.0 - whole) - error) - pivot[1] * first
        inverse = quick_sum(first, first * gap)
        whole, error = product(row[0], inverse[0], halves(row[0]), halves(inverse[0]))
        scaled = quick_sum(whole, error + (row[0] * inverse[1] + row[1] * inverse[0]))
        scaled_parts = halves(scaled[0])
        for t in range(tile, tiles):
            if t == tile and sub == 7:
                continue
            high, low = rows[t]
            column = [jnp.broadcast_to(v[:, j : j + 1], shape) for v in rows[t]]
            if t == tile:
                column = [jnp.where(sub_id > sub, v, 0.0) for v in column]
            whole, error = product(column[0], scaled[0], halves(column[0]), scaled_parts)
            error = error + (column[0] * scaled[1] + column[1] * scaled[0])
            total, missed = two_sum(high, -whole)
            rows[t] = quick_sum(total, missed + (low - error))
    wide_high = jnp.concatenate([v[0] for v in rows], axis=0)
    wide_low = jnp.concatenate([v[1] for v in rows], axis=0)
    wide_row = lax.broadcasted_iota(jnp.int32, wide_high.shape, 0)
    wide_lane = lax.broadcasted_iota(jnp.int32, wide_high.shape, 1)
    diagonal = jnp.sum(jnp.where(wide_row == wide_lane, wide_high, 0.0), axis=1, keepdims=True)
    root = jnp.sqrt(diagonal)
    wide = (wide_high + wide_low) / root
    r_ref[...] = jnp.where(lane_id >= row_id, wide[:, :cols], 0.0)
    white_ref[...] = jnp.dot(
        wide[:, cols:],
        picked_ref[...],
        precision=lax.Precision.HIGHEST,
        preferred_element_type=jnp.float32,
    )


def factor_and_solve(picked, grams):
    cols = picked.shape[0]
    return pl.pallas_call(
        factor_kernel,
        grid=(1,),
        in_specs=[whole(value) for value in (picked, *grams)],
        out_specs=(pl.BlockSpec((cols, cols), lambda i: (0, 0)), whole(picked)),
        out_shape=(
            jax.ShapeDtypeStruct((cols, cols), jnp.float32),
            jax.ShapeDtypeStruct(picked.shape, jnp.float32),
        ),
        cost_estimate=pl.CostEstimate(
            flops=20_000_000, bytes_accessed=1 << 18, transcendentals=0
        ),
    )(picked, *grams)


def xor_permute(value, mask, device_count):
    return lax.ppermute(value, AXES, [(i, i ^ mask) for i in range(device_count)])


def in_groups(masks, size=2):
    odd = len(masks) % size
    groups = [masks[:odd]] if odd else []
    return groups + [masks[i : i + size] for i in range(odd, len(masks), size)]


def combined(masks, q):
    mask = 0
    for bit, value in enumerate(masks):
        if (q >> bit) & 1:
            mask |= value
    return mask


def local(panel, signs, sample_device, sample_offset):
    device_count = lax.axis_size(AXES)
    me = lax.axis_index(AXES).astype(jnp.int32)
    bits = device_count.bit_length() - 1
    cols, rows = panel.shape
    samples = sample_offset.shape[0]
    per_device = samples // device_count
    half = per_device // 2
    masks = [1 << bit for bit in range(bits)]

    signs_row = signs.reshape(1, rows)
    scale = 1.0 / math.sqrt(rows * device_count)

    mix = local_mix(panel, signs_row, scale, device_count)

    def swap(value):
        return lax.all_to_all(value, AXES, split_axis=0, concat_axis=0, tiled=True)

    received_mix = swap(mix)

    common = me & sample_device[:, 0]
    odd = lax.population_count(common) & 1
    code = sample_offset + odd * rows
    total = sampled_terms(mix, code, me.reshape(1), bits, half)
    for group in in_groups(masks):
        block = total.shape[0] >> len(group)
        mine = total[:block]
        for q in range(1, 1 << len(group)):
            mask = combined(group[::-1], q)
            sent = total[q * block : (q + 1) * block]
            mine = mine + xor_permute(sent, mask, device_count)
        total = mine
    picked, gram = own_gram(total, cols, per_device, 1.0 / math.sqrt(samples))
    across = mix_across(received_mix, gram)
    groups = in_groups(masks)[::-1]
    for number, group in enumerate(groups):
        received = [gram] + [
            xor_permute(gram, combined(group, q), device_count) for q in range(1, 1 << len(group))
        ]
        if number == 0:
            across, gram = gram_sum(received, across)
            mixed = lay_out(swap(across))
        elif number < len(groups) - 1:
            (gram,) = gram_sum(received)
    r_factor, whitened = factor_and_solve(picked, received)
    return (mixed, r_factor, whitened)


def solution(mesh):
    return jax.shard_map(
        local,
        mesh=mesh,
        in_specs=(P(None, AXES), P(AXES), P(), P()),
        out_specs=(P(None, AXES), P(), P(None, AXES)),
        check_vma=False,
    )
```

```python
import functools
import math

import jax
import jax.numpy as jnp
import numpy as np
from jax import lax
from jax.experimental import pallas as pl
from jax.experimental.pallas import tpu as pltpu
from jax.sharding import PartitionSpec as P

AXES = ("rows", "sk")
LANES = 128
GROUP = 16
SLICES = 6


def hadamard_table(order_size):
    shape = (order_size, order_size)
    common = lax.broadcasted_iota(jnp.int32, shape, 0) & lax.broadcasted_iota(jnp.int32, shape, 1)
    for distance in (4, 2, 1):
        common = common ^ (common >> distance)
    return (1 - 2 * (common & 1)).astype(jnp.float32).astype(jnp.bfloat16)


def whole(value):
    return pl.BlockSpec(value.shape, lambda i: (0,) * len(value.shape))


def in_hbm(value):
    return pltpu.with_memory_space_constraint(value, pltpu.HBM)


def mix_kernel(scale, panel_ref, signs_ref, out_ref):
    cols, rows = panel_ref.shape
    inner = rows // LANES
    width = out_ref.shape[2]
    step = min(width, LANES)
    table = hadamard_table(LANES)
    signs = signs_ref[...].astype(jnp.float32) * scale
    for first in range(0, cols, 8):
        flipped = panel_ref[first : first + 8, :] * signs
        stacked = jnp.concatenate(
            [flipped[:, a * LANES : (a + 1) * LANES] for a in range(inner)], axis=0
        )
        total = None
        rest = stacked
        for piece in range(3):
            part = rest.astype(jnp.bfloat16)
            term = jnp.dot(part, table, preferred_element_type=jnp.float32)
            total = term if total is None else total + term
            if piece < 2:
                rest = rest - part.astype(jnp.float32)
        blocks = [total[a * 8 : (a + 1) * 8] for a in range(inner)]
        span = 1
        while span < inner:
            for a in range(inner):
                if a & span == 0:
                    left, right = blocks[a], blocks[a + span]
                    blocks[a], blocks[a + span] = left + right, left - right
            span *= 2
        for start in range(0, rows, step):
            block = blocks[start // LANES][:, start % LANES : start % LANES + step]
            out_ref[start // width, first : first + 8, start % width : start % width + step] = block


def local_mix(panel, signs_row, scale, peers):
    cols, rows = panel.shape
    width = rows // peers
    return pl.pallas_call(
        functools.partial(mix_kernel, scale),
        grid=(cols // GROUP,),
        in_specs=[
            pl.BlockSpec((GROUP, rows), lambda i: (i, 0)),
            pl.BlockSpec((1, rows), lambda i: (0, 0)),
        ],
        out_specs=pl.BlockSpec((peers, GROUP, width), lambda i: (0, i, 0)),
        out_shape=pltpu.HBM((peers, cols, width), jnp.float32),
        compiler_params=pltpu.CompilerParams(vmem_limit_bytes=32 << 20),
    )(in_hbm(panel), in_hbm(signs_row))


def across_kernel(in_ref, token_ref, out_ref):
    del token_ref
    peers = in_ref.shape[0]
    step = min(in_ref.shape[2], LANES)
    for lane in range(0, in_ref.shape[2], step):
        for first in range(0, in_ref.shape[1], 8):
            columns = pl.ds(first, 8)
            blocks = [in_ref[p, columns, lane : lane + step] for p in range(peers)]
            span = 1
            while span < peers:
                for p in range(peers):
                    if p & span == 0:
                        left, right = blocks[p], blocks[p + span]
                        blocks[p], blocks[p + span] = left + right, left - right
                span *= 2
            for p in range(peers):
                out_ref[p, columns, lane : lane + step] = blocks[p]


def mix_across(received, token):
    peers, cols, width = received.shape
    spec = pl.BlockSpec((peers, GROUP, width), lambda i: (0, i, 0))
    return pl.pallas_call(
        across_kernel,
        grid=(cols // GROUP,),
        in_specs=[spec, pl.BlockSpec((8, LANES), lambda i: (0, 0))],
        out_specs=spec,
        out_shape=pltpu.HBM(received.shape, jnp.float32),
        compiler_params=pltpu.CompilerParams(vmem_limit_bytes=32 << 20),
    )(received, token)


def lay_out_kernel(in_ref, out_ref):
    peers, _, width = in_ref.shape
    for p in range(peers):
        out_ref[:, p * width : (p + 1) * width] = in_ref[p]


def lay_out(received):
    peers, cols, width = received.shape
    return pl.pallas_call(
        lay_out_kernel,
        grid=(cols // GROUP,),
        in_specs=[pl.BlockSpec((peers, GROUP, width), lambda i: (0, i, 0))],
        out_specs=pl.BlockSpec((GROUP, peers * width), lambda i: (i, 0)),
        out_shape=jax.ShapeDtypeStruct((cols, peers * width), jnp.float32),
        compiler_params=pltpu.CompilerParams(vmem_limit_bytes=32 << 20),
    )(received)


def terms_kernel(bits, half, code_ref, me_ref, far_ref, out_ref, mix_ref, table_ref, done_sem):
    peers, _, width = mix_ref.shape
    pieces = [
        pltpu.make_async_copy(far_ref.at[part], mix_ref.at[part], done_sem.at[number])
        for number, part in enumerate([pl.ds(0, peers // 2), pl.ds(peers // 2, peers // 2)])
    ]
    for piece in pieces:
        piece.start()
    rows = peers * width
    me = me_ref[0]

    span = max(1, LANES // width)

    def transpose_block(number, carry):
        p = number * span
        for lane in range(0, max(width, LANES), LANES):
            start = pl.multiple_of(p * width + lane, LANES)
            tile = jnp.concatenate(
                [mix_ref[p + i, :, lane : lane + min(width, LANES)] for i in range(span)], axis=1
            )
            turned = jnp.concatenate([tile, tile], axis=0).T
            table_ref[pl.ds(start, LANES), :] = turned
            table_ref[pl.ds(rows + start, LANES), :] = -turned
        return carry

    for number, piece in enumerate(pieces):
        piece.wait()
        count = peers // 2 // span
        lax.fori_loop(number * count, (number + 1) * count, transpose_block, 0)
    first_half = lax.broadcasted_iota(jnp.int32, (1, LANES), 1) < LANES // 2

    def gather_block(r, carry):
        mask = jnp.int32(0)
        for bit in range(bits):
            mask = mask | (((r >> bit) & 1) << (bits - 1 - bit))
        source = (me ^ mask) * (2 * half)
        target = pl.multiple_of(r * half, half)
        for j in range(half):
            upper = table_ref[pl.ds(code_ref[source + j], 1), :]
            lower = table_ref[pl.ds(code_ref[source + half + j], 1), :]
            out_ref[pl.ds(target + j, 1), :] = jnp.where(first_half, upper, lower)
        return carry

    lax.fori_loop(0, 1 << bits, gather_block, 0)


def sampled_terms(mix, code, me, bits, half):
    rows = mix.shape[0] * mix.shape[2]
    count = half << bits
    return pl.pallas_call(
        functools.partial(terms_kernel, bits, half),
        in_specs=[pl.BlockSpec(memory_space=pltpu.SMEM)] * 2
        + [pl.BlockSpec(memory_space=pltpu.HBM)],
        out_specs=pl.BlockSpec(memory_space=pltpu.VMEM),
        out_shape=jax.ShapeDtypeStruct((count, LANES), jnp.float32),
        scratch_shapes=[
            pltpu.VMEM(mix.shape, jnp.float32),
            pltpu.VMEM((2 * rows, LANES), jnp.float32),
            pltpu.SemaphoreType.DMA((2,)),
        ],
        compiler_params=pltpu.CompilerParams(vmem_limit_bytes=40 << 20),
        cost_estimate=pl.CostEstimate(
            flops=count * LANES * 40, bytes_accessed=24 << 20, transcendentals=0
        ),
    )(code, me, in_hbm(mix))


def two_sum(a, b):
    total = a + b
    part = total - a
    return total, (a - (total - part)) + (b - part)


def quick_sum(a, b):
    total = a + b
    return total, b - (total - a)


def pair_add(a, b):
    total, error = two_sum(a[0], b[0])
    return quick_sum(total, error + (a[1] + b[1]))


def halves(a):
    scaled = a * 4097.0
    high = scaled - (scaled - a)
    return high, a - high


def product(a, b, a_parts, b_parts):
    whole = a * b
    error = (a_parts[0] * b_parts[0] - whole) + a_parts[0] * b_parts[1]
    error = (error + a_parts[1] * b_parts[0]) + a_parts[1] * b_parts[1]
    return whole, error


def gram_kernel(scale, terms_ref, picked_ref, gram_ref):
    cols = picked_ref.shape[0]
    turned = terms_ref[...].T
    picked = jnp.concatenate([turned[:cols], turned[cols:]], axis=1)
    picked_ref[...] = picked
    rest = picked * scale
    shift = jnp.max(jnp.abs(rest), axis=1, keepdims=True) * float(1 << 17)
    parts = []
    for _ in range(SLICES):
        part = (rest + shift) - shift
        rest = rest - part
        shift = shift * (1.0 / 64.0)
        parts.append(part.astype(jnp.bfloat16))
    total = None
    for level in range(SLICES):
        left = jnp.concatenate(parts[: level + 1], axis=1)
        right = jnp.concatenate(parts[: level + 1][::-1], axis=1)
        term = lax.dot_general(
            left, right, (((1,), (1,)), ((), ())), preferred_element_type=jnp.float32
        )
        if total is None:
            total = (term, jnp.zeros_like(term))
        else:
            high, error = two_sum(total[0], term)
            total = (high, total[1] + error)
    high, low = quick_sum(*total)
    gram_ref[...] = jnp.concatenate([high, low], axis=1)


def own_gram(terms, cols, per_device, scale):
    return pl.pallas_call(
        functools.partial(gram_kernel, scale),
        grid=(1,),
        in_specs=[whole(terms)],
        out_specs=(
            pl.BlockSpec((cols, per_device), lambda i: (0, 0)),
            pl.BlockSpec((cols, 2 * cols), lambda i: (0, 0)),
        ),
        out_shape=(
            jax.ShapeDtypeStruct((cols, per_device), jnp.float32),
            jax.ShapeDtypeStruct((cols, 2 * cols), jnp.float32),
        ),
        compiler_params=pltpu.CompilerParams(vmem_limit_bytes=8 << 20),
    )(terms)


def tree_sum(values):
    while len(values) > 1:
        values = [pair_add(values[i], values[i + 1]) for i in range(0, len(values), 2)]
    return values[0]


def split_pair(packed):
    cols = packed.shape[0]
    return packed[:, :cols], packed[:, cols:]


def gram_sum_kernel(count, *refs):
    high, low = tree_sum([split_pair(ref[...]) for ref in refs[:count]])
    refs[-1][...] = jnp.concatenate([high, low], axis=1)


def gram_sum(grams, *through):
    count = len(grams)
    in_place = pl.BlockSpec(memory_space=pltpu.HBM)
    return pl.pallas_call(
        functools.partial(gram_sum_kernel, count),
        grid=(1,),
        in_specs=[whole(gram) for gram in grams] + [in_place] * len(through),
        out_specs=tuple([in_place] * len(through) + [whole(grams[0])]),
        out_shape=tuple(
            [pltpu.HBM(v.shape, v.dtype) for v in through]
            + [jax.ShapeDtypeStruct(grams[0].shape, jnp.float32)]
        ),
        input_output_aliases={count + i: i for i in range(len(through))},
        compiler_params=pltpu.CompilerParams(vmem_limit_bytes=8 << 20),
    )(*grams, *through)


def factor_kernel(picked_ref, *refs):
    gram_refs, (r_ref, white_ref) = refs[:-2], refs[-2:]
    cols = r_ref.shape[0]
    high, low = tree_sum([split_pair(ref[...]) for ref in gram_refs])
    row_id = lax.broadcasted_iota(jnp.int32, (cols, cols), 0)
    lane_id = lax.broadcasted_iota(jnp.int32, (cols, cols), 1)
    unit = (row_id == lane_id).astype(jnp.float32)
    wide_high = jnp.concatenate([high, unit], axis=1)
    wide_low = jnp.concatenate([low, jnp.zeros_like(unit)], axis=1)
    tiles = cols // 8
    shape = (8, 2 * cols)
    rows = [
        (wide_high[t * 8 : (t + 1) * 8], wide_low[t * 8 : (t + 1) * 8])
        for t in range(tiles)
    ]
    sub_id = lax.broadcasted_iota(jnp.int32, shape, 0)
    for j in range(cols - 1):
        tile, sub = divmod(j, 8)
        row = [jnp.broadcast_to(v[sub : sub + 1], shape) for v in rows[tile]]
        pivot = [jnp.broadcast_to(v[sub : sub + 1, j : j + 1], shape) for v in rows[tile]]
        first = 1.0 / pivot[0]
        first_parts = halves(first)
        whole, error = product(pivot[0], first, halves(pivot[0]), first_parts)
        gap = ((1.0 - whole) - error) - pivot[1] * first
        inverse = quick_sum(first, first * gap)
        whole, error = product(row[0], inverse[0], halves(row[0]), halves(inverse[0]))
        scaled = quick_sum(whole, error + (row[0] * inverse[1] + row[1] * inverse[0]))
        scaled_parts = halves(scaled[0])
        for t in range(tile, tiles):
            if t == tile and sub == 7:
                continue
            high, low = rows[t]
            column = [jnp.broadcast_to(v[:, j : j + 1], shape) for v in rows[t]]
            if t == tile:
                column = [jnp.where(sub_id > sub, v, 0.0) for v in column]
            whole, error = product(column[0], scaled[0], halves(column[0]), scaled_parts)
            error = error + (column[0] * scaled[1] + column[1] * scaled[0])
            total, missed = two_sum(high, -whole)
            rows[t] = quick_sum(total, missed + (low - error))
    wide_high = jnp.concatenate([v[0] for v in rows], axis=0)
    wide_low = jnp.concatenate([v[1] for v in rows], axis=0)
    wide_row = lax.broadcasted_iota(jnp.int32, wide_high.shape, 0)
    wide_lane = lax.broadcasted_iota(jnp.int32, wide_high.shape, 1)
    diagonal = jnp.sum(jnp.where(wide_row == wide_lane, wide_high, 0.0), axis=1, keepdims=True)
    root = jnp.sqrt(diagonal)
    wide = (wide_high + wide_low) / root
    r_ref[...] = jnp.where(lane_id >= row_id, wide[:, :cols], 0.0)
    white_ref[...] = jnp.dot(
        wide[:, cols:],
        picked_ref[...],
        precision=lax.Precision.HIGHEST,
        preferred_element_type=jnp.float32,
    )


def factor_and_solve(picked, grams):
    cols = picked.shape[0]
    return pl.pallas_call(
        factor_kernel,
        grid=(1,),
        in_specs=[whole(value) for value in (picked, *grams)],
        out_specs=(pl.BlockSpec((cols, cols), lambda i: (0, 0)), whole(picked)),
        out_shape=(
            jax.ShapeDtypeStruct((cols, cols), jnp.float32),
            jax.ShapeDtypeStruct(picked.shape, jnp.float32),
        ),
        compiler_params=pltpu.CompilerParams(vmem_limit_bytes=8 << 20),
    )(picked, *grams)


def xor_permute(value, mask, device_count):
    return lax.ppermute(value, AXES, [(i, i ^ mask) for i in range(device_count)])


def in_groups(masks, size=2):
    odd = len(masks) % size
    groups = [masks[:odd]] if odd else []
    return groups + [masks[i : i + size] for i in range(odd, len(masks), size)]


def combined(masks, q):
    mask = 0
    for bit, value in enumerate(masks):
        if (q >> bit) & 1:
            mask |= value
    return mask


def local(panel, signs, sample_device, sample_offset):
    device_count = lax.axis_size(AXES)
    me = lax.axis_index(AXES).astype(jnp.int32)
    bits = device_count.bit_length() - 1
    cols, rows = panel.shape
    samples = sample_offset.shape[0]
    per_device = samples // device_count
    half = per_device // 2
    masks = [1 << bit for bit in range(bits)]

    signs_row = signs.reshape(1, rows)
    scale = 1.0 / math.sqrt(rows * device_count)

    mix = local_mix(panel, signs_row, scale, device_count)

    def swap(value):
        return lax.all_to_all(value, AXES, split_axis=0, concat_axis=0, tiled=True)

    received_mix = swap(mix)

    common = me & sample_device[:, 0]
    odd = lax.population_count(common) & 1
    code = sample_offset + odd * rows
    total = sampled_terms(mix, code, me.reshape(1), bits, half)
    for group in in_groups(masks):
        block = total.shape[0] >> len(group)
        mine = total[:block]
        for q in range(1, 1 << len(group)):
            mask = combined(group[::-1], q)
            sent = total[q * block : (q + 1) * block]
            mine = mine + xor_permute(sent, mask, device_count)
        total = mine
    picked, gram = own_gram(total, cols, per_device, 1.0 / math.sqrt(samples))
    across = mix_across(received_mix, gram)
    groups = in_groups(masks)[::-1]
    for number, group in enumerate(groups):
        received = [gram] + [
            xor_permute(gram, combined(group, q), device_count) for q in range(1, 1 << len(group))
        ]
        if number == 0:
            across, gram = gram_sum(received, across)
            mixed = lay_out(swap(across))
        elif number < len(groups) - 1:
            (gram,) = gram_sum(received)
    r_factor, whitened = factor_and_solve(picked, received)
    return (mixed, r_factor, whitened)


def solution(mesh):
    return jax.shard_map(
        local,
        mesh=mesh,
        in_specs=(P(None, AXES), P(AXES), P(), P()),
        out_specs=(P(None, AXES), P(), P(None, AXES)),
        check_vma=False,
    )
```

```python
import functools
import math

import jax
import jax.numpy as jnp
import numpy as np
from jax import lax
from jax.experimental import pallas as pl
from jax.experimental.pallas import tpu as pltpu
from jax.sharding import PartitionSpec as P

AXES = ("rows", "sk")
LANES = 128
GROUP = 8
SLICES = 6


def hadamard_np(order_size):
    table = np.ones((1, 1), np.float32)
    while table.shape[0] < order_size:
        table = np.block([[table, table], [table, -table]])
    return table


def mix_kernel(scale, panel_ref, signs_ref, table_ref, out_ref):
    rows = panel_ref.shape[1]
    inner = rows // LANES
    flipped = panel_ref[...] * (signs_ref[...].astype(jnp.float32) * scale)
    stacked = jnp.concatenate(
        [flipped[:, a * LANES : (a + 1) * LANES] for a in range(inner)], axis=0
    )
    table = table_ref[...]
    total = None
    rest = stacked
    for piece in range(3):
        part = rest.astype(jnp.bfloat16)
        term = jnp.dot(part, table, preferred_element_type=jnp.float32)
        total = term if total is None else total + term
        if piece < 2:
            rest = rest - part.astype(jnp.float32)
    blocks = [total[a * GROUP : (a + 1) * GROUP] for a in range(inner)]
    span = 1
    while span < inner:
        for a in range(inner):
            if a & span == 0:
                left, right = blocks[a], blocks[a + span]
                blocks[a], blocks[a + span] = left + right, left - right
        span *= 2
    for a in range(inner):
        out_ref[:, a * LANES : (a + 1) * LANES] = blocks[a]


def local_mix(panel, signs_row, table, scale, first, count):
    rows = panel.shape[1]
    return pl.pallas_call(
        functools.partial(mix_kernel, scale),
        grid=(count // GROUP,),
        in_specs=[
            pl.BlockSpec((GROUP, rows), lambda i: (first // GROUP + i, 0)),
            pl.BlockSpec((1, rows), lambda i: (0, 0)),
            pl.BlockSpec((LANES, LANES), lambda i: (0, 0)),
        ],
        out_specs=pl.BlockSpec((GROUP, rows), lambda i: (i, 0)),
        out_shape=jax.ShapeDtypeStruct((count, rows), jnp.float32),
        compiler_params=pltpu.CompilerParams(vmem_limit_bytes=32 << 20),
        cost_estimate=pl.CostEstimate(
            flops=count * rows * 800, bytes_accessed=count * rows * 8, transcendentals=0
        ),
    )(panel, signs_row, table)


def terms_kernel(bits, half, code_ref, me_ref, *refs):
    chunk_refs, out_ref, table_ref = refs[:-2], refs[-2], refs[-1]
    rows = chunk_refs[0].shape[1]
    me = me_ref[0]

    def transpose_block(a, carry):
        start = pl.multiple_of(a * LANES, LANES)
        tile = jnp.concatenate([ref[:, pl.ds(start, LANES)] for ref in chunk_refs], axis=0)
        turned = jnp.concatenate([tile, tile], axis=0).T
        table_ref[pl.ds(start, LANES), :] = turned
        table_ref[pl.ds(rows + start, LANES), :] = -turned
        return carry

    lax.fori_loop(0, rows // LANES, transpose_block, 0)
    first_half = lax.broadcasted_iota(jnp.int32, (1, LANES), 1) < LANES // 2

    def gather_block(r, carry):
        mask = jnp.int32(0)
        for bit in range(bits):
            mask = mask | (((r >> bit) & 1) << (bits - 1 - bit))
        source = (me ^ mask) * (2 * half)
        target = pl.multiple_of(r * half, half)
        for j in range(half):
            upper = table_ref[pl.ds(code_ref[source + j], 1), :]
            lower = table_ref[pl.ds(code_ref[source + half + j], 1), :]
            out_ref[pl.ds(target + j, 1), :] = jnp.where(first_half, upper, lower)
        return carry

    lax.fori_loop(0, 1 << bits, gather_block, 0)


def sampled_terms(chunks, code, me, bits, half):
    rows = chunks[0].shape[1]
    count = half << bits
    return pl.pallas_call(
        functools.partial(terms_kernel, bits, half),
        in_specs=[pl.BlockSpec(memory_space=pltpu.SMEM)] * 2
        + [pl.BlockSpec(memory_space=pltpu.VMEM)] * len(chunks),
        out_specs=pl.BlockSpec(memory_space=pltpu.VMEM),
        out_shape=jax.ShapeDtypeStruct((count, LANES), jnp.float32),
        scratch_shapes=[pltpu.VMEM((2 * rows, LANES), jnp.float32)],
        compiler_params=pltpu.CompilerParams(vmem_limit_bytes=24 << 20),
        cost_estimate=pl.CostEstimate(
            flops=count * LANES * 40, bytes_accessed=24 << 20, transcendentals=0
        ),
    )(code, me, *chunks)


def two_sum(a, b):
    total = a + b
    part = total - a
    return total, (a - (total - part)) + (b - part)


def quick_sum(a, b):
    total = a + b
    return total, b - (total - a)


def pair_add(a, b):
    total, error = two_sum(a[0], b[0])
    return quick_sum(total, error + (a[1] + b[1]))


def halves(a):
    scaled = a * 4097.0
    high = scaled - (scaled - a)
    return high, a - high


def product(a, b, a_parts, b_parts):
    whole = a * b
    error = (a_parts[0] * b_parts[0] - whole) + a_parts[0] * b_parts[1]
    error = (error + a_parts[1] * b_parts[0]) + a_parts[1] * b_parts[1]
    return whole, error


def gram_kernel(scale, terms_ref, picked_ref, gram_ref):
    cols = picked_ref.shape[0]
    turned = terms_ref[...].T
    picked = jnp.concatenate([turned[:cols], turned[cols:]], axis=1)
    picked_ref[...] = picked
    rest = picked * scale
    shift = jnp.max(jnp.abs(rest), axis=1, keepdims=True) * float(1 << 17)
    parts = []
    for _ in range(SLICES):
        part = (rest + shift) - shift
        rest = rest - part
        shift = shift * (1.0 / 64.0)
        parts.append(part.astype(jnp.bfloat16))
    total = None
    for level in range(SLICES):
        left = jnp.concatenate(parts[: level + 1], axis=1)
        right = jnp.concatenate(parts[: level + 1][::-1], axis=1)
        term = lax.dot_general(
            left, right, (((1,), (1,)), ((), ())), preferred_element_type=jnp.float32
        )
        if total is None:
            total = (term, jnp.zeros_like(term))
        else:
            high, error = two_sum(total[0], term)
            total = (high, total[1] + error)
    high, low = quick_sum(*total)
    gram_ref[...] = jnp.concatenate([high, low], axis=1)


def own_gram(terms, cols, per_device, scale):
    return pl.pallas_call(
        functools.partial(gram_kernel, scale),
        out_shape=(
            jax.ShapeDtypeStruct((cols, per_device), jnp.float32),
            jax.ShapeDtypeStruct((cols, 2 * cols), jnp.float32),
        ),
        compiler_params=pltpu.CompilerParams(vmem_limit_bytes=8 << 20),
    )(terms)


def tree_sum(values):
    while len(values) > 1:
        values = [pair_add(values[i], values[i + 1]) for i in range(0, len(values), 2)]
    return values[0]


def split_pair(packed):
    cols = packed.shape[0]
    return packed[:, :cols], packed[:, cols:]


def gram_sum_kernel(*refs):
    high, low = tree_sum([split_pair(ref[...]) for ref in refs[:-1]])
    refs[-1][...] = jnp.concatenate([high, low], axis=1)


def gram_sum(grams):
    return pl.pallas_call(
        gram_sum_kernel,
        out_shape=jax.ShapeDtypeStruct(grams[0].shape, jnp.float32),
        compiler_params=pltpu.CompilerParams(vmem_limit_bytes=8 << 20),
    )(*grams)


def factor_kernel(picked_ref, *refs):
    gram_refs, (r_ref, white_ref) = refs[:-2], refs[-2:]
    cols = r_ref.shape[0]
    high, low = tree_sum([split_pair(ref[...]) for ref in gram_refs])
    row_id = lax.broadcasted_iota(jnp.int32, (cols, cols), 0)
    lane_id = lax.broadcasted_iota(jnp.int32, (cols, cols), 1)
    unit = (row_id == lane_id).astype(jnp.float32)
    wide_high = jnp.concatenate([high, unit], axis=1)
    wide_low = jnp.concatenate([low, jnp.zeros_like(unit)], axis=1)
    tiles = cols // 8
    shape = (8, 2 * cols)
    rows = [
        (wide_high[t * 8 : (t + 1) * 8], wide_low[t * 8 : (t + 1) * 8])
        for t in range(tiles)
    ]
    sub_id = lax.broadcasted_iota(jnp.int32, shape, 0)
    for j in range(cols - 1):
        tile, sub = divmod(j, 8)
        row = [jnp.broadcast_to(v[sub : sub + 1], shape) for v in rows[tile]]
        pivot = [jnp.broadcast_to(v[sub : sub + 1, j : j + 1], shape) for v in rows[tile]]
        first = 1.0 / pivot[0]
        first_parts = halves(first)
        whole, error = product(pivot[0], first, halves(pivot[0]), first_parts)
        gap = ((1.0 - whole) - error) - pivot[1] * first
        inverse = quick_sum(first, first * gap)
        whole, error = product(row[0], inverse[0], halves(row[0]), halves(inverse[0]))
        scaled = quick_sum(whole, error + (row[0] * inverse[1] + row[1] * inverse[0]))
        scaled_parts = halves(scaled[0])
        for t in range(tile, tiles):
            if t == tile and sub == 7:
                continue
            high, low = rows[t]
            column = [jnp.broadcast_to(v[:, j : j + 1], shape) for v in rows[t]]
            if t == tile:
                column = [jnp.where(sub_id > sub, v, 0.0) for v in column]
            whole, error = product(column[0], scaled[0], halves(column[0]), scaled_parts)
            error = error + (column[0] * scaled[1] + column[1] * scaled[0])
            total, missed = two_sum(high, -whole)
            rows[t] = quick_sum(total, missed + (low - error))
    wide_high = jnp.concatenate([v[0] for v in rows], axis=0)
    wide_low = jnp.concatenate([v[1] for v in rows], axis=0)
    wide_row = lax.broadcasted_iota(jnp.int32, wide_high.shape, 0)
    wide_lane = lax.broadcasted_iota(jnp.int32, wide_high.shape, 1)
    diagonal = jnp.sum(jnp.where(wide_row == wide_lane, wide_high, 0.0), axis=1, keepdims=True)
    root = jnp.sqrt(diagonal)
    wide = (wide_high + wide_low) / root
    r_ref[...] = jnp.where(lane_id >= row_id, wide[:, :cols], 0.0)
    white_ref[...] = jnp.dot(
        wide[:, cols:],
        picked_ref[...],
        precision=lax.Precision.HIGHEST,
        preferred_element_type=jnp.float32,
    )


def factor_and_solve(picked, grams):
    cols = picked.shape[0]
    return pl.pallas_call(
        factor_kernel,
        out_shape=(
            jax.ShapeDtypeStruct((cols, cols), jnp.float32),
            jax.ShapeDtypeStruct(picked.shape, jnp.float32),
        ),
        compiler_params=pltpu.CompilerParams(vmem_limit_bytes=8 << 20),
    )(picked, *grams)


def xor_permute(value, mask, device_count):
    return lax.ppermute(value, AXES, [(i, i ^ mask) for i in range(device_count)])


def in_groups(masks, size=2):
    odd = len(masks) % size
    groups = [masks[:odd]] if odd else []
    return groups + [masks[i : i + size] for i in range(odd, len(masks), size)]


def idle_kernel(*refs):
    del refs


def gate(values, tokens):
    count = len(values)
    return pl.pallas_call(
        idle_kernel,
        in_specs=[pl.BlockSpec(memory_space=pl.ANY)] * (count + len(tokens)),
        out_specs=tuple([pl.BlockSpec(memory_space=pl.ANY)] * count),
        out_shape=tuple(jax.ShapeDtypeStruct(v.shape, v.dtype) for v in values),
        input_output_aliases={i: i for i in range(count)},
        compiler_params=pltpu.CompilerParams(vmem_limit_bytes=1 << 20),
    )(*values, *tokens)


def combined(masks, q):
    mask = 0
    for bit, value in enumerate(masks):
        if (q >> bit) & 1:
            mask |= value
    return mask


def local(panel, signs, sample_device, sample_offset):
    device_count = lax.axis_size(AXES)
    me = lax.axis_index(AXES).astype(jnp.int32)
    bits = device_count.bit_length() - 1
    cols, rows = panel.shape
    samples = sample_offset.shape[0]
    per_device = samples // device_count
    half = per_device // 2
    masks = [1 << bit for bit in range(bits)]

    table = jnp.asarray(hadamard_np(LANES), jnp.bfloat16)
    signs_row = signs.reshape(1, rows)
    scale = 1.0 / math.sqrt(rows * device_count)

    parts = cols // GROUP
    chunks = [
        local_mix(panel, signs_row, table, scale, part * GROUP, GROUP) for part in range(parts)
    ]

    def own_sign(mask):
        return jnp.where((me & mask) == 0, jnp.float32(1.0), jnp.float32(-1.0))

    def exchange(value, order):
        for mask in order:
            other = xor_permute(value, mask, device_count)
            value = other + own_sign(mask) * value
        return value

    def sampled_path():
        common = me & sample_device[:, 0]
        odd = lax.population_count(common) & 1
        code = sample_offset + odd * rows
        total = yield sampled_terms(chunks, code, me.reshape(1), bits, half)
        for number, group in enumerate(in_groups(masks)):
            block = total.shape[0] >> len(group)
            mine = total[:block]
            for q in range(1, 1 << len(group)):
                mask = combined(group[::-1], q)
                sent = total[q * block : (q + 1) * block]
                mine = mine + xor_permute(sent, mask, device_count)
            if number < len(in_groups(masks)) - 1:
                mine = yield mine
            total = mine
        picked, gram = own_gram(total, cols, per_device, 1.0 / math.sqrt(samples))
        groups = in_groups(masks)[::-1]
        for number, group in enumerate(groups):
            gram = yield gram
            received = [gram] + [
                xor_permute(gram, combined(group, q), device_count)
                for q in range(1, 1 << len(group))
            ]
            gram = gram_sum(received)
        gram = yield gram
        yield factor_and_solve(picked, [gram])

    top, near = masks[-1], masks[:-1]
    sets = [near[i * len(near) // 4 : (i + 1) * len(near) // 4] for i in range(4)]
    after = [sets[2], sets[0], sets[1], sets[3]]
    before = [sets[3], sets[1], sets[0], sets[2]]
    path = sampled_path()
    pending = None
    values = list(chunks)
    late = [[]]
    for phase in range(parts):
        if phase > 0:
            tokens = [values[phase - 1]] + late[phase - 1]
            held = [values[phase]] if pending is None else [values[phase], pending]
            gated = gate(held, tokens)
            values[phase] = gated[0]
            pending = gated[1] if pending is not None else None
        start = values[phase - 1] if phase > 0 else None
        late.append([])
        moved = []
        for part in range(parts):
            if part < parts // 2:
                step, order = phase - part - 1, after
            else:
                step, order = phase - part + parts // 2, before
            if 0 <= step < len(order):
                moved.append((part, order[step]))
        if phase > 0 and moved:
            free = [part for part, _ in moved if part != phase - 1]
            if free:
                for part, value in zip(free, gate([values[part] for part in free], [start])):
                    values[part] = value
        for part, order in moved:
            values[part] = exchange(values[part], order)
            if part < parts // 2:
                late[-1].append(values[part])
        values[phase] = exchange(values[phase], [top])
        pending = next(path) if phase == 0 else path.send(pending)
    while True:
        try:
            pending = path.send(pending)
        except StopIteration:
            break
    r_factor, whitened = pending
    mixed = jnp.concatenate(values, axis=0)
    return (mixed, r_factor, whitened)


def solution(mesh):
    return jax.shard_map(
        local,
        mesh=mesh,
        in_specs=(P(None, AXES), P(AXES), P(), P()),
        out_specs=(P(None, AXES), P(), P(None, AXES)),
        check_vma=False,
    )
```

```python
import functools
import math

import jax
import jax.numpy as jnp
import numpy as np
from jax import lax
from jax.experimental import pallas as pl
from jax.experimental.pallas import tpu as pltpu
from jax.sharding import PartitionSpec as P

AXES = ("rows", "sk")
LANES = 128
GROUP = 16
SLICES = 6


def hadamard_table(order_size):
    shape = (order_size, order_size)
    common = lax.broadcasted_iota(jnp.int32, shape, 0) & lax.broadcasted_iota(jnp.int32, shape, 1)
    for distance in (4, 2, 1):
        common = common ^ (common >> distance)
    return (1 - 2 * (common & 1)).astype(jnp.float32).astype(jnp.bfloat16)


def whole(value):
    return pl.BlockSpec(value.shape, lambda i: (0,) * len(value.shape))


def in_hbm(value):
    return pltpu.with_memory_space_constraint(value, pltpu.HBM)


def mix_kernel(scale, panel_ref, signs_ref, out_ref):
    cols, rows = panel_ref.shape
    inner = rows // LANES
    width = out_ref.shape[2]
    step = min(width, LANES)
    table = hadamard_table(LANES)
    signs = signs_ref[...].astype(jnp.float32) * scale
    for first in range(0, cols, 8):
        flipped = panel_ref[first : first + 8, :] * signs
        stacked = jnp.concatenate(
            [flipped[:, a * LANES : (a + 1) * LANES] for a in range(inner)], axis=0
        )
        total = None
        rest = stacked
        for piece in range(3):
            part = rest.astype(jnp.bfloat16)
            term = jnp.dot(part, table, preferred_element_type=jnp.float32)
            total = term if total is None else total + term
            if piece < 2:
                rest = rest - part.astype(jnp.float32)
        blocks = [total[a * 8 : (a + 1) * 8] for a in range(inner)]
        span = 1
        while span < inner:
            for a in range(inner):
                if a & span == 0:
                    left, right = blocks[a], blocks[a + span]
                    blocks[a], blocks[a + span] = left + right, left - right
            span *= 2
        for start in range(0, rows, step):
            block = blocks[start // LANES][:, start % LANES : start % LANES + step]
            out_ref[start // width, first : first + 8, start % width : start % width + step] = block


def local_mix(panel, signs_row, scale, peers):
    cols, rows = panel.shape
    width = rows // peers
    return pl.pallas_call(
        functools.partial(mix_kernel, scale),
        grid=(cols // GROUP,),
        in_specs=[
            pl.BlockSpec((GROUP, rows), lambda i: (i, 0)),
            pl.BlockSpec((1, rows), lambda i: (0, 0)),
        ],
        out_specs=pl.BlockSpec((peers, GROUP, width), lambda i: (0, i, 0)),
        out_shape=pltpu.HBM((peers, cols, width), jnp.float32),
        compiler_params=pltpu.CompilerParams(vmem_limit_bytes=32 << 20),
    )(in_hbm(panel), in_hbm(signs_row))


def across_kernel(in_ref, token_ref, out_ref):
    del token_ref
    peers = in_ref.shape[0]
    step = min(in_ref.shape[2], LANES)
    for lane in range(0, in_ref.shape[2], step):
        for first in range(0, in_ref.shape[1], 8):
            columns = pl.ds(first, 8)
            blocks = [in_ref[p, columns, lane : lane + step] for p in range(peers)]
            span = 1
            while span < peers:
                for p in range(peers):
                    if p & span == 0:
                        left, right = blocks[p], blocks[p + span]
                        blocks[p], blocks[p + span] = left + right, left - right
                span *= 2
            for p in range(peers):
                out_ref[p, columns, lane : lane + step] = blocks[p]


def mix_across(received, token):
    peers, cols, width = received.shape
    spec = pl.BlockSpec((peers, GROUP, width), lambda i: (0, i, 0))
    return pl.pallas_call(
        across_kernel,
        grid=(cols // GROUP,),
        in_specs=[spec, pl.BlockSpec((8, LANES), lambda i: (0, 0))],
        out_specs=spec,
        out_shape=pltpu.HBM(received.shape, jnp.float32),
        compiler_params=pltpu.CompilerParams(vmem_limit_bytes=32 << 20),
    )(received, token)


def lay_out_kernel(in_ref, out_ref):
    peers, _, width = in_ref.shape
    for p in range(peers):
        out_ref[:, p * width : (p + 1) * width] = in_ref[p]


def lay_out(received):
    peers, cols, width = received.shape
    return pl.pallas_call(
        lay_out_kernel,
        grid=(cols // GROUP,),
        in_specs=[pl.BlockSpec((peers, GROUP, width), lambda i: (0, i, 0))],
        out_specs=pl.BlockSpec((GROUP, peers * width), lambda i: (i, 0)),
        out_shape=jax.ShapeDtypeStruct((cols, peers * width), jnp.float32),
        compiler_params=pltpu.CompilerParams(vmem_limit_bytes=32 << 20),
    )(received)


def terms_kernel(bits, half, code_ref, me_ref, far_ref, out_ref, mix_ref, table_ref, done_sem):
    peers, _, width = mix_ref.shape
    pieces = [
        pltpu.make_async_copy(far_ref.at[part], mix_ref.at[part], done_sem.at[number])
        for number, part in enumerate([pl.ds(0, peers // 2), pl.ds(peers // 2, peers // 2)])
    ]
    for piece in pieces:
        piece.start()
    rows = peers * width
    me = me_ref[0]

    span = max(1, LANES // width)

    def transpose_block(number, carry):
        p = number * span
        for lane in range(0, max(width, LANES), LANES):
            start = pl.multiple_of(p * width + lane, LANES)
            tile = jnp.concatenate(
                [mix_ref[p + i, :, lane : lane + min(width, LANES)] for i in range(span)], axis=1
            )
            turned = jnp.concatenate([tile, tile], axis=0).T
            table_ref[pl.ds(start, LANES), :] = turned
            table_ref[pl.ds(rows + start, LANES), :] = -turned
        return carry

    for number, piece in enumerate(pieces):
        piece.wait()
        count = peers // 2 // span
        lax.fori_loop(number * count, (number + 1) * count, transpose_block, 0)
    first_half = lax.broadcasted_iota(jnp.int32, (1, LANES), 1) < LANES // 2

    def gather_block(r, carry):
        mask = jnp.int32(0)
        for bit in range(bits):
            mask = mask | (((r >> bit) & 1) << (bits - 1 - bit))
        source = (me ^ mask) * (2 * half)
        target = pl.multiple_of(r * half, half)
        for j in range(half):
            upper = table_ref[pl.ds(code_ref[source + j], 1), :]
            lower = table_ref[pl.ds(code_ref[source + half + j], 1), :]
            out_ref[pl.ds(target + j, 1), :] = jnp.where(first_half, upper, lower)
        return carry

    lax.fori_loop(0, 1 << bits, gather_block, 0)


def sampled_terms(mix, code, me, bits, half):
    rows = mix.shape[0] * mix.shape[2]
    count = half << bits
    return pl.pallas_call(
        functools.partial(terms_kernel, bits, half),
        in_specs=[pl.BlockSpec(memory_space=pltpu.SMEM)] * 2
        + [pl.BlockSpec(memory_space=pltpu.HBM)],
        out_specs=pl.BlockSpec(memory_space=pltpu.VMEM),
        out_shape=jax.ShapeDtypeStruct((count, LANES), jnp.float32),
        scratch_shapes=[
            pltpu.VMEM(mix.shape, jnp.float32),
            pltpu.VMEM((2 * rows, LANES), jnp.float32),
            pltpu.SemaphoreType.DMA((2,)),
        ],
        compiler_params=pltpu.CompilerParams(vmem_limit_bytes=40 << 20),
        cost_estimate=pl.CostEstimate(
            flops=count * LANES * 40, bytes_accessed=24 << 20, transcendentals=0
        ),
    )(code, me, in_hbm(mix))


def two_sum(a, b):
    total = a + b
    part = total - a
    return total, (a - (total - part)) + (b - part)


def quick_sum(a, b):
    total = a + b
    return total, b - (total - a)


def pair_add(a, b):
    total, error = two_sum(a[0], b[0])
    return quick_sum(total, error + (a[1] + b[1]))


def halves(a):
    scaled = a * 4097.0
    high = scaled - (scaled - a)
    return high, a - high


def product(a, b, a_parts, b_parts):
    whole = a * b
    error = (a_parts[0] * b_parts[0] - whole) + a_parts[0] * b_parts[1]
    error = (error + a_parts[1] * b_parts[0]) + a_parts[1] * b_parts[1]
    return whole, error


def gram_kernel(scale, terms_ref, token_ref, picked_ref, gram_ref):
    del token_ref
    cols = picked_ref.shape[0]
    turned = terms_ref[...].T
    picked = jnp.concatenate([turned[:cols], turned[cols:]], axis=1)
    picked_ref[...] = picked
    rest = picked * scale
    shift = jnp.max(jnp.abs(rest), axis=1, keepdims=True) * float(1 << 17)
    parts = []
    for _ in range(SLICES):
        part = (rest + shift) - shift
        rest = rest - part
        shift = shift * (1.0 / 64.0)
        parts.append(part.astype(jnp.bfloat16))
    total = None
    for level in range(SLICES):
        left = jnp.concatenate(parts[: level + 1], axis=1)
        right = jnp.concatenate(parts[: level + 1][::-1], axis=1)
        term = lax.dot_general(
            left, right, (((1,), (1,)), ((), ())), preferred_element_type=jnp.float32
        )
        if total is None:
            total = (term, jnp.zeros_like(term))
        else:
            high, error = two_sum(total[0], term)
            total = (high, total[1] + error)
    high, low = quick_sum(*total)
    gram_ref[...] = jnp.concatenate([high, low], axis=1)


def own_gram(terms, cols, per_device, scale, token):
    return pl.pallas_call(
        functools.partial(gram_kernel, scale),
        grid=(1,),
        in_specs=[whole(terms), pl.BlockSpec((1, 8, LANES), lambda i: (0, 0, 0))],
        out_specs=(
            pl.BlockSpec((cols, per_device), lambda i: (0, 0)),
            pl.BlockSpec((cols, 2 * cols), lambda i: (0, 0)),
        ),
        out_shape=(
            jax.ShapeDtypeStruct((cols, per_device), jnp.float32),
            jax.ShapeDtypeStruct((cols, 2 * cols), jnp.float32),
        ),
        compiler_params=pltpu.CompilerParams(vmem_limit_bytes=8 << 20),
    )(terms, in_hbm(token))


def tree_sum(values):
    while len(values) > 1:
        values = [pair_add(values[i], values[i + 1]) for i in range(0, len(values), 2)]
    return values[0]


def split_pair(packed):
    cols = packed.shape[0]
    return packed[:, :cols], packed[:, cols:]


def gram_sum_kernel(count, *refs):
    high, low = tree_sum([split_pair(ref[...]) for ref in refs[:count]])
    refs[-1][...] = jnp.concatenate([high, low], axis=1)


def gram_sum(grams, *through):
    count = len(grams)
    in_place = pl.BlockSpec(memory_space=pltpu.HBM)
    return pl.pallas_call(
        functools.partial(gram_sum_kernel, count),
        grid=(1,),
        in_specs=[whole(gram) for gram in grams] + [in_place] * len(through),
        out_specs=tuple([in_place] * len(through) + [whole(grams[0])]),
        out_shape=tuple(
            [pltpu.HBM(v.shape, v.dtype) for v in through]
            + [jax.ShapeDtypeStruct(grams[0].shape, jnp.float32)]
        ),
        input_output_aliases={count + i: i for i in range(len(through))},
        compiler_params=pltpu.CompilerParams(vmem_limit_bytes=8 << 20),
    )(*grams, *through)


def factor_kernel(picked_ref, *refs):
    gram_refs, (r_ref, white_ref) = refs[:-2], refs[-2:]
    cols = r_ref.shape[0]
    high, low = tree_sum([split_pair(ref[...]) for ref in gram_refs])
    row_id = lax.broadcasted_iota(jnp.int32, (cols, cols), 0)
    lane_id = lax.broadcasted_iota(jnp.int32, (cols, cols), 1)
    unit = (row_id == lane_id).astype(jnp.float32)
    wide_high = jnp.concatenate([high, unit], axis=1)
    wide_low = jnp.concatenate([low, jnp.zeros_like(unit)], axis=1)
    tiles = cols // 8
    shape = (8, 2 * cols)
    rows = [
        (wide_high[t * 8 : (t + 1) * 8], wide_low[t * 8 : (t + 1) * 8])
        for t in range(tiles)
    ]
    sub_id = lax.broadcasted_iota(jnp.int32, shape, 0)
    for j in range(cols - 1):
        tile, sub = divmod(j, 8)
        row = [jnp.broadcast_to(v[sub : sub + 1], shape) for v in rows[tile]]
        pivot = [jnp.broadcast_to(v[sub : sub + 1, j : j + 1], shape) for v in rows[tile]]
        first = 1.0 / pivot[0]
        first_parts = halves(first)
        whole, error = product(pivot[0], first, halves(pivot[0]), first_parts)
        gap = ((1.0 - whole) - error) - pivot[1] * first
        inverse = quick_sum(first, first * gap)
        whole, error = product(row[0], inverse[0], halves(row[0]), halves(inverse[0]))
        scaled = quick_sum(whole, error + (row[0] * inverse[1] + row[1] * inverse[0]))
        scaled_parts = halves(scaled[0])
        for t in range(tile, tiles):
            if t == tile and sub == 7:
                continue
            high, low = rows[t]
            column = [jnp.broadcast_to(v[:, j : j + 1], shape) for v in rows[t]]
            if t == tile:
                column = [jnp.where(sub_id > sub, v, 0.0) for v in column]
            whole, error = product(column[0], scaled[0], halves(column[0]), scaled_parts)
            error = error + (column[0] * scaled[1] + column[1] * scaled[0])
            total, missed = two_sum(high, -whole)
            rows[t] = quick_sum(total, missed + (low - error))
    wide_high = jnp.concatenate([v[0] for v in rows], axis=0)
    wide_low = jnp.concatenate([v[1] for v in rows], axis=0)
    wide_row = lax.broadcasted_iota(jnp.int32, wide_high.shape, 0)
    wide_lane = lax.broadcasted_iota(jnp.int32, wide_high.shape, 1)
    diagonal = jnp.sum(jnp.where(wide_row == wide_lane, wide_high, 0.0), axis=1, keepdims=True)
    root = jnp.sqrt(diagonal)
    wide = (wide_high + wide_low) / root
    r_ref[...] = jnp.where(lane_id >= row_id, wide[:, :cols], 0.0)
    white_ref[...] = jnp.dot(
        wide[:, cols:],
        picked_ref[...],
        precision=lax.Precision.HIGHEST,
        preferred_element_type=jnp.float32,
    )


def factor_and_solve(picked, grams):
    cols = picked.shape[0]
    return pl.pallas_call(
        factor_kernel,
        grid=(1,),
        in_specs=[whole(value) for value in (picked, *grams)],
        out_specs=(pl.BlockSpec((cols, cols), lambda i: (0, 0)), whole(picked)),
        out_shape=(
            jax.ShapeDtypeStruct((cols, cols), jnp.float32),
            jax.ShapeDtypeStruct(picked.shape, jnp.float32),
        ),
        compiler_params=pltpu.CompilerParams(vmem_limit_bytes=8 << 20),
    )(picked, *grams)


def xor_permute(value, mask, device_count):
    return lax.ppermute(value, AXES, [(i, i ^ mask) for i in range(device_count)])


def in_groups(masks, size=2):
    odd = len(masks) % size
    groups = [masks[:odd]] if odd else []
    return groups + [masks[i : i + size] for i in range(odd, len(masks), size)]


def combined(masks, q):
    mask = 0
    for bit, value in enumerate(masks):
        if (q >> bit) & 1:
            mask |= value
    return mask


def local(panel, signs, sample_device, sample_offset):
    device_count = lax.axis_size(AXES)
    me = lax.axis_index(AXES).astype(jnp.int32)
    bits = device_count.bit_length() - 1
    cols, rows = panel.shape
    samples = sample_offset.shape[0]
    per_device = samples // device_count
    half = per_device // 2
    masks = [1 << bit for bit in range(bits)]

    signs_row = signs.reshape(1, rows)
    scale = 1.0 / math.sqrt(rows * device_count)

    mix = local_mix(panel, signs_row, scale, device_count)

    def swap(value):
        return lax.all_to_all(value, AXES, split_axis=0, concat_axis=0, tiled=True)

    received_mix = swap(mix)

    common = me & sample_device[:, 0]
    odd = lax.population_count(common) & 1
    code = sample_offset + odd * rows
    total = sampled_terms(mix, code, me.reshape(1), bits, half)
    for group in in_groups(masks):
        early = total
        block = total.shape[0] >> len(group)
        mine = total[:block]
        for q in range(1, 1 << len(group)):
            mask = combined(group[::-1], q)
            sent = total[q * block : (q + 1) * block]
            mine = mine + xor_permute(sent, mask, device_count)
        total = mine
    across = mix_across(received_mix, early)
    picked, gram = own_gram(total, cols, per_device, 1.0 / math.sqrt(samples), across)
    groups = in_groups(masks)[::-1]
    for number, group in enumerate(groups):
        received = [gram] + [
            xor_permute(gram, combined(group, q), device_count) for q in range(1, 1 << len(group))
        ]
        if number == 0:
            across, gram = gram_sum(received, across)
            mixed = lay_out(swap(across))
        elif number < len(groups) - 1:
            (gram,) = gram_sum(received)
    r_factor, whitened = factor_and_solve(picked, received)
    return (mixed, r_factor, whitened)


def solution(mesh):
    return jax.shard_map(
        local,
        mesh=mesh,
        in_specs=(P(None, AXES), P(AXES), P(), P()),
        out_specs=(P(None, AXES), P(), P(None, AXES)),
        check_vma=False,
    )
```

```python
import functools
import math

import jax
import jax.numpy as jnp
import numpy as np
from jax import lax
from jax.experimental import pallas as pl
from jax.experimental.pallas import tpu as pltpu
from jax.sharding import PartitionSpec as P

AXES = ("rows", "sk")
LANES = 128
GROUP = 32
SLICES = 6


def hadamard_table(order_size):
    shape = (order_size, order_size)
    common = lax.broadcasted_iota(jnp.int32, shape, 0) & lax.broadcasted_iota(jnp.int32, shape, 1)
    for distance in (4, 2, 1):
        common = common ^ (common >> distance)
    return (1 - 2 * (common & 1)).astype(jnp.float32).astype(jnp.bfloat16)


def whole(value):
    return pl.BlockSpec(value.shape, lambda i: (0,) * len(value.shape))


def in_hbm(value):
    return pltpu.with_memory_space_constraint(value, pltpu.HBM)


def mix_kernel(scale, panel_ref, signs_ref, out_ref):
    cols, rows = panel_ref.shape
    inner = rows // LANES
    width = out_ref.shape[2]
    step = min(width, LANES)
    table = hadamard_table(LANES)
    signs = signs_ref[...].astype(jnp.float32) * scale
    for first in range(0, cols, 8):
        flipped = panel_ref[first : first + 8, :] * signs
        stacked = jnp.concatenate(
            [flipped[:, a * LANES : (a + 1) * LANES] for a in range(inner)], axis=0
        )
        total = None
        rest = stacked
        for piece in range(3):
            part = rest.astype(jnp.bfloat16)
            term = jnp.dot(part, table, preferred_element_type=jnp.float32)
            total = term if total is None else total + term
            if piece < 2:
                rest = rest - part.astype(jnp.float32)
        blocks = [total[a * 8 : (a + 1) * 8] for a in range(inner)]
        span = 1
        while span < inner:
            for a in range(inner):
                if a & span == 0:
                    left, right = blocks[a], blocks[a + span]
                    blocks[a], blocks[a + span] = left + right, left - right
            span *= 2
        for start in range(0, rows, step):
            block = blocks[start // LANES][:, start % LANES : start % LANES + step]
            out_ref[start // width, first : first + 8, start % width : start % width + step] = block


def local_mix(panel, signs_row, scale, peers):
    cols, rows = panel.shape
    width = rows // peers
    return pl.pallas_call(
        functools.partial(mix_kernel, scale),
        grid=(cols // GROUP,),
        in_specs=[
            pl.BlockSpec((GROUP, rows), lambda i: (i, 0)),
            pl.BlockSpec((1, rows), lambda i: (0, 0)),
        ],
        out_specs=pl.BlockSpec((peers, GROUP, width), lambda i: (0, i, 0)),
        out_shape=pltpu.HBM((peers, cols, width), jnp.float32),
        compiler_params=pltpu.CompilerParams(vmem_limit_bytes=32 << 20),
    )(in_hbm(panel), in_hbm(signs_row))


def across_kernel(in_ref, token_ref, out_ref):
    del token_ref
    peers = in_ref.shape[0]
    step = min(in_ref.shape[2], LANES)
    for lane in range(0, in_ref.shape[2], step):
        for first in range(0, in_ref.shape[1], 8):
            columns = pl.ds(first, 8)
            blocks = [in_ref[p, columns, lane : lane + step] for p in range(peers)]
            span = 1
            while span < peers:
                for p in range(peers):
                    if p & span == 0:
                        left, right = blocks[p], blocks[p + span]
                        blocks[p], blocks[p + span] = left + right, left - right
                span *= 2
            for p in range(peers):
                out_ref[p, columns, lane : lane + step] = blocks[p]


def mix_across(received, token):
    peers, cols, width = received.shape
    spec = pl.BlockSpec((peers, GROUP, width), lambda i: (0, i, 0))
    return pl.pallas_call(
        across_kernel,
        grid=(cols // GROUP,),
        in_specs=[spec, pl.BlockSpec((8, LANES), lambda i: (0, 0))],
        out_specs=spec,
        out_shape=pltpu.HBM(received.shape, jnp.float32),
        compiler_params=pltpu.CompilerParams(vmem_limit_bytes=32 << 20),
    )(received, token)


def lay_out_kernel(in_ref, out_ref):
    peers, _, width = in_ref.shape
    for p in range(peers):
        out_ref[:, p * width : (p + 1) * width] = in_ref[p]


def lay_out(received):
    peers, cols, width = received.shape
    return pl.pallas_call(
        lay_out_kernel,
        grid=(cols // GROUP,),
        in_specs=[pl.BlockSpec((peers, GROUP, width), lambda i: (0, i, 0))],
        out_specs=pl.BlockSpec((GROUP, peers * width), lambda i: (i, 0)),
        out_shape=jax.ShapeDtypeStruct((cols, peers * width), jnp.float32),
        compiler_params=pltpu.CompilerParams(vmem_limit_bytes=32 << 20),
    )(received)


def terms_kernel(bits, half, code_ref, me_ref, far_ref, out_ref, mix_ref, table_ref, done_sem):
    peers, _, width = mix_ref.shape
    pieces = [
        pltpu.make_async_copy(far_ref.at[part], mix_ref.at[part], done_sem.at[number])
        for number, part in enumerate([pl.ds(0, peers // 2), pl.ds(peers // 2, peers // 2)])
    ]
    for piece in pieces:
        piece.start()
    rows = peers * width
    me = me_ref[0]

    span = max(1, LANES // width)

    def transpose_block(number, carry):
        p = number * span
        for lane in range(0, max(width, LANES), LANES):
            start = pl.multiple_of(p * width + lane, LANES)
            tile = jnp.concatenate(
                [mix_ref[p + i, :, lane : lane + min(width, LANES)] for i in range(span)], axis=1
            )
            turned = jnp.concatenate([tile, tile], axis=0).T
            table_ref[pl.ds(start, LANES), :] = turned
            table_ref[pl.ds(rows + start, LANES), :] = -turned
        return carry

    for number, piece in enumerate(pieces):
        piece.wait()
        count = peers // 2 // span
        lax.fori_loop(number * count, (number + 1) * count, transpose_block, 0)
    first_half = lax.broadcasted_iota(jnp.int32, (1, LANES), 1) < LANES // 2

    def gather_block(r, carry):
        mask = jnp.int32(0)
        for bit in range(bits):
            mask = mask | (((r >> bit) & 1) << (bits - 1 - bit))
        source = (me ^ mask) * (2 * half)
        target = pl.multiple_of(r * half, half)
        for j in range(half):
            upper = table_ref[pl.ds(code_ref[source + j], 1), :]
            lower = table_ref[pl.ds(code_ref[source + half + j], 1), :]
            out_ref[pl.ds(target + j, 1), :] = jnp.where(first_half, upper, lower)
        return carry

    lax.fori_loop(0, 1 << bits, gather_block, 0)


def sampled_terms(mix, code, me, bits, half):
    rows = mix.shape[0] * mix.shape[2]
    count = half << bits
    return pl.pallas_call(
        functools.partial(terms_kernel, bits, half),
        in_specs=[pl.BlockSpec(memory_space=pltpu.SMEM)] * 2
        + [pl.BlockSpec(memory_space=pltpu.HBM)],
        out_specs=pl.BlockSpec(memory_space=pltpu.VMEM),
        out_shape=jax.ShapeDtypeStruct((count, LANES), jnp.float32),
        scratch_shapes=[
            pltpu.VMEM(mix.shape, jnp.float32),
            pltpu.VMEM((2 * rows, LANES), jnp.float32),
            pltpu.SemaphoreType.DMA((2,)),
        ],
        compiler_params=pltpu.CompilerParams(vmem_limit_bytes=40 << 20),
        cost_estimate=pl.CostEstimate(
            flops=count * LANES * 40, bytes_accessed=24 << 20, transcendentals=0
        ),
    )(code, me, in_hbm(mix))


def two_sum(a, b):
    total = a + b
    part = total - a
    return total, (a - (total - part)) + (b - part)


def quick_sum(a, b):
    total = a + b
    return total, b - (total - a)


def pair_add(a, b):
    total, error = two_sum(a[0], b[0])
    return quick_sum(total, error + (a[1] + b[1]))


def halves(a):
    scaled = a * 4097.0
    high = scaled - (scaled - a)
    return high, a - high


def product(a, b, a_parts, b_parts):
    whole = a * b
    error = (a_parts[0] * b_parts[0] - whole) + a_parts[0] * b_parts[1]
    error = (error + a_parts[1] * b_parts[0]) + a_parts[1] * b_parts[1]
    return whole, error


def gram_kernel(scale, terms_ref, picked_ref, gram_ref):
    cols = picked_ref.shape[0]
    turned = terms_ref[...].T
    picked = jnp.concatenate([turned[:cols], turned[cols:]], axis=1)
    picked_ref[...] = picked
    rest = picked * scale
    shift = jnp.max(jnp.abs(rest), axis=1, keepdims=True) * float(1 << 17)
    parts = []
    for _ in range(SLICES):
        part = (rest + shift) - shift
        rest = rest - part
        shift = shift * (1.0 / 64.0)
        parts.append(part.astype(jnp.bfloat16))
    total = None
    for level in range(SLICES):
        left = jnp.concatenate(parts[: level + 1], axis=1)
        right = jnp.concatenate(parts[: level + 1][::-1], axis=1)
        term = lax.dot_general(
            left, right, (((1,), (1,)), ((), ())), preferred_element_type=jnp.float32
        )
        if total is None:
            total = (term, jnp.zeros_like(term))
        else:
            high, error = two_sum(total[0], term)
            total = (high, total[1] + error)
    high, low = quick_sum(*total)
    gram_ref[...] = jnp.concatenate([high, low], axis=1)


def own_gram(terms, cols, per_device, scale):
    return pl.pallas_call(
        functools.partial(gram_kernel, scale),
        grid=(1,),
        in_specs=[whole(terms)],
        out_specs=(
            pl.BlockSpec((cols, per_device), lambda i: (0, 0)),
            pl.BlockSpec((cols, 2 * cols), lambda i: (0, 0)),
        ),
        out_shape=(
            jax.ShapeDtypeStruct((cols, per_device), jnp.float32),
            jax.ShapeDtypeStruct((cols, 2 * cols), jnp.float32),
        ),
        compiler_params=pltpu.CompilerParams(vmem_limit_bytes=8 << 20),
    )(terms)


def tree_sum(values):
    while len(values) > 1:
        values = [pair_add(values[i], values[i + 1]) for i in range(0, len(values), 2)]
    return values[0]


def split_pair(packed):
    cols = packed.shape[0]
    return packed[:, :cols], packed[:, cols:]


def gram_sum_kernel(count, *refs):
    high, low = tree_sum([split_pair(ref[...]) for ref in refs[:count]])
    refs[-1][...] = jnp.concatenate([high, low], axis=1)


def gram_sum(grams, *through):
    count = len(grams)
    in_place = pl.BlockSpec(memory_space=pltpu.HBM)
    return pl.pallas_call(
        functools.partial(gram_sum_kernel, count),
        grid=(1,),
        in_specs=[whole(gram) for gram in grams] + [in_place] * len(through),
        out_specs=tuple([in_place] * len(through) + [whole(grams[0])]),
        out_shape=tuple(
            [pltpu.HBM(v.shape, v.dtype) for v in through]
            + [jax.ShapeDtypeStruct(grams[0].shape, jnp.float32)]
        ),
        input_output_aliases={count + i: i for i in range(len(through))},
        compiler_params=pltpu.CompilerParams(vmem_limit_bytes=8 << 20),
    )(*grams, *through)


def factor_kernel(picked_ref, *refs):
    gram_refs, (r_ref, white_ref) = refs[:-2], refs[-2:]
    cols = r_ref.shape[0]
    high, low = tree_sum([split_pair(ref[...]) for ref in gram_refs])
    row_id = lax.broadcasted_iota(jnp.int32, (cols, cols), 0)
    lane_id = lax.broadcasted_iota(jnp.int32, (cols, cols), 1)
    unit = (row_id == lane_id).astype(jnp.float32)
    wide_high = jnp.concatenate([high, unit], axis=1)
    wide_low = jnp.concatenate([low, jnp.zeros_like(unit)], axis=1)
    tiles = cols // 8
    shape = (8, 2 * cols)
    rows = [
        (wide_high[t * 8 : (t + 1) * 8], wide_low[t * 8 : (t + 1) * 8])
        for t in range(tiles)
    ]
    sub_id = lax.broadcasted_iota(jnp.int32, shape, 0)
    for j in range(cols - 1):
        tile, sub = divmod(j, 8)
        row = [jnp.broadcast_to(v[sub : sub + 1], shape) for v in rows[tile]]
        pivot = [jnp.broadcast_to(v[sub : sub + 1, j : j + 1], shape) for v in rows[tile]]
        first = 1.0 / pivot[0]
        first_parts = halves(first)
        whole, error = product(pivot[0], first, halves(pivot[0]), first_parts)
        gap = ((1.0 - whole) - error) - pivot[1] * first
        inverse = quick_sum(first, first * gap)
        whole, error = product(row[0], inverse[0], halves(row[0]), halves(inverse[0]))
        scaled = quick_sum(whole, error + (row[0] * inverse[1] + row[1] * inverse[0]))
        scaled_parts = halves(scaled[0])
        for t in range(tile, tiles):
            if t == tile and sub == 7:
                continue
            high, low = rows[t]
            column = [jnp.broadcast_to(v[:, j : j + 1], shape) for v in rows[t]]
            if t == tile:
                column = [jnp.where(sub_id > sub, v, 0.0) for v in column]
            whole, error = product(column[0], scaled[0], halves(column[0]), scaled_parts)
            error = error + (column[0] * scaled[1] + column[1] * scaled[0])
            total, missed = two_sum(high, -whole)
            rows[t] = quick_sum(total, missed + (low - error))
    wide_high = jnp.concatenate([v[0] for v in rows], axis=0)
    wide_low = jnp.concatenate([v[1] for v in rows], axis=0)
    wide_row = lax.broadcasted_iota(jnp.int32, wide_high.shape, 0)
    wide_lane = lax.broadcasted_iota(jnp.int32, wide_high.shape, 1)
    diagonal = jnp.sum(jnp.where(wide_row == wide_lane, wide_high, 0.0), axis=1, keepdims=True)
    root = jnp.sqrt(diagonal)
    wide = (wide_high + wide_low) / root
    r_ref[...] = jnp.where(lane_id >= row_id, wide[:, :cols], 0.0)
    white_ref[...] = jnp.dot(
        wide[:, cols:],
        picked_ref[...],
        precision=lax.Precision.HIGHEST,
        preferred_element_type=jnp.float32,
    )


def factor_and_solve(picked, grams):
    cols = picked.shape[0]
    return pl.pallas_call(
        factor_kernel,
        grid=(1,),
        in_specs=[whole(value) for value in (picked, *grams)],
        out_specs=(pl.BlockSpec((cols, cols), lambda i: (0, 0)), whole(picked)),
        out_shape=(
            jax.ShapeDtypeStruct((cols, cols), jnp.float32),
            jax.ShapeDtypeStruct(picked.shape, jnp.float32),
        ),
        compiler_params=pltpu.CompilerParams(vmem_limit_bytes=8 << 20),
    )(picked, *grams)


def xor_permute(value, mask, device_count):
    return lax.ppermute(value, AXES, [(i, i ^ mask) for i in range(device_count)])


def in_groups(masks, size=2):
    odd = len(masks) % size
    groups = [masks[:odd]] if odd else []
    return groups + [masks[i : i + size] for i in range(odd, len(masks), size)]


def combined(masks, q):
    mask = 0
    for bit, value in enumerate(masks):
        if (q >> bit) & 1:
            mask |= value
    return mask


def local(panel, signs, sample_device, sample_offset):
    device_count = lax.axis_size(AXES)
    me = lax.axis_index(AXES).astype(jnp.int32)
    bits = device_count.bit_length() - 1
    cols, rows = panel.shape
    samples = sample_offset.shape[0]
    per_device = samples // device_count
    half = per_device // 2
    masks = [1 << bit for bit in range(bits)]

    signs_row = signs.reshape(1, rows)
    scale = 1.0 / math.sqrt(rows * device_count)

    mix = local_mix(panel, signs_row, scale, device_count)

    def swap(value):
        return lax.all_to_all(value, AXES, split_axis=0, concat_axis=0, tiled=True)

    received_mix = swap(mix)

    common = me & sample_device[:, 0]
    odd = lax.population_count(common) & 1
    code = sample_offset + odd * rows
    total = sampled_terms(mix, code, me.reshape(1), bits, half)
    for group in in_groups(masks):
        block = total.shape[0] >> len(group)
        mine = total[:block]
        for q in range(1, 1 << len(group)):
            mask = combined(group[::-1], q)
            sent = total[q * block : (q + 1) * block]
            mine = mine + xor_permute(sent, mask, device_count)
        total = mine
    picked, gram = own_gram(total, cols, per_device, 1.0 / math.sqrt(samples))
    across = mix_across(received_mix, gram)
    groups = in_groups(masks)[::-1]
    for number, group in enumerate(groups):
        received = [gram] + [
            xor_permute(gram, combined(group, q), device_count) for q in range(1, 1 << len(group))
        ]
        if number == 0:
            across, gram = gram_sum(received, across)
            mixed = lay_out(swap(across))
        elif number < len(groups) - 1:
            (gram,) = gram_sum(received)
    r_factor, whitened = factor_and_solve(picked, received)
    return (mixed, r_factor, whitened)


def solution(mesh):
    return jax.shard_map(
        local,
        mesh=mesh,
        in_specs=(P(None, AXES), P(AXES), P(), P()),
        out_specs=(P(None, AXES), P(), P(None, AXES)),
        check_vma=False,
    )
```

```python
import functools
import math

import jax
import jax.numpy as jnp
import numpy as np
from jax import lax
from jax.experimental import pallas as pl
from jax.experimental.pallas import tpu as pltpu
from jax.sharding import PartitionSpec as P

AXES = ("rows", "sk")
LANES = 128
GROUP = 32
SLICES = 6


def hadamard_table(order_size):
    shape = (order_size, order_size)
    common = lax.broadcasted_iota(jnp.int32, shape, 0) & lax.broadcasted_iota(jnp.int32, shape, 1)
    for distance in (4, 2, 1):
        common = common ^ (common >> distance)
    return (1 - 2 * (common & 1)).astype(jnp.float32).astype(jnp.bfloat16)


def whole(value):
    return pl.BlockSpec(value.shape, lambda i: (0,) * len(value.shape))


def in_hbm(value):
    return pltpu.with_memory_space_constraint(value, pltpu.HBM)


def mix_kernel(scale, panel_ref, signs_ref, out_ref):
    cols, rows = panel_ref.shape
    inner = rows // LANES
    width = out_ref.shape[2]
    step = min(width, LANES)
    table = hadamard_table(LANES)
    signs = signs_ref[...].astype(jnp.float32) * scale
    for first in range(0, cols, 8):
        flipped = panel_ref[first : first + 8, :] * signs
        stacked = jnp.concatenate(
            [flipped[:, a * LANES : (a + 1) * LANES] for a in range(inner)], axis=0
        )
        total = None
        rest = stacked
        for piece in range(3):
            part = rest.astype(jnp.bfloat16)
            term = jnp.dot(part, table, preferred_element_type=jnp.float32)
            total = term if total is None else total + term
            if piece < 2:
                rest = rest - part.astype(jnp.float32)
        blocks = [total[a * 8 : (a + 1) * 8] for a in range(inner)]
        span = 1
        while span < inner:
            for a in range(inner):
                if a & span == 0:
                    left, right = blocks[a], blocks[a + span]
                    blocks[a], blocks[a + span] = left + right, left - right
            span *= 2
        for start in range(0, rows, step):
            block = blocks[start // LANES][:, start % LANES : start % LANES + step]
            out_ref[start // width, first : first + 8, start % width : start % width + step] = block


def local_mix(panel, signs_row, scale, peers):
    cols, rows = panel.shape
    width = rows // peers
    return pl.pallas_call(
        functools.partial(mix_kernel, scale),
        grid=(cols // GROUP,),
        in_specs=[
            pl.BlockSpec((GROUP, rows), lambda i: (i, 0)),
            pl.BlockSpec((1, rows), lambda i: (0, 0)),
        ],
        out_specs=pl.BlockSpec((peers, GROUP, width), lambda i: (0, i, 0)),
        out_shape=pltpu.HBM((peers, cols, width), jnp.float32),
        compiler_params=pltpu.CompilerParams(vmem_limit_bytes=32 << 20),
    )(in_hbm(panel), in_hbm(signs_row))


def across_kernel(in_ref, token_ref, out_ref):
    del token_ref
    peers = in_ref.shape[0]
    step = min(in_ref.shape[2], LANES)
    for lane in range(0, in_ref.shape[2], step):
        for first in range(0, in_ref.shape[1], 8):
            columns = pl.ds(first, 8)
            blocks = [in_ref[p, columns, lane : lane + step] for p in range(peers)]
            span = 1
            while span < peers:
                for p in range(peers):
                    if p & span == 0:
                        left, right = blocks[p], blocks[p + span]
                        blocks[p], blocks[p + span] = left + right, left - right
                span *= 2
            for p in range(peers):
                out_ref[p, columns, lane : lane + step] = blocks[p]


def mix_across(received, token):
    peers, cols, width = received.shape
    spec = pl.BlockSpec((peers, GROUP, width), lambda i: (0, i, 0))
    return pl.pallas_call(
        across_kernel,
        grid=(cols // GROUP,),
        in_specs=[spec, pl.BlockSpec((8, LANES), lambda i: (0, 0))],
        out_specs=spec,
        out_shape=pltpu.HBM(received.shape, jnp.float32),
        compiler_params=pltpu.CompilerParams(vmem_limit_bytes=32 << 20),
    )(received, token)


def lay_out_kernel(in_ref, out_ref):
    peers, _, width = in_ref.shape
    for p in range(peers):
        out_ref[:, p * width : (p + 1) * width] = in_ref[p]


def lay_out(received):
    peers, cols, width = received.shape
    return pl.pallas_call(
        lay_out_kernel,
        grid=(1,),
        in_specs=[pl.BlockSpec((peers, cols, width), lambda i: (0, i, 0))],
        out_specs=pl.BlockSpec((cols, peers * width), lambda i: (i, 0)),
        out_shape=jax.ShapeDtypeStruct((cols, peers * width), jnp.float32),
        compiler_params=pltpu.CompilerParams(vmem_limit_bytes=32 << 20),
    )(received)


def terms_kernel(bits, half, code_ref, me_ref, far_ref, out_ref, mix_ref, table_ref, done_sem):
    peers, _, width = mix_ref.shape
    pieces = [
        pltpu.make_async_copy(far_ref.at[part], mix_ref.at[part], done_sem.at[number])
        for number, part in enumerate([pl.ds(0, peers // 2), pl.ds(peers // 2, peers // 2)])
    ]
    for piece in pieces:
        piece.start()
    rows = peers * width
    me = me_ref[0]

    span = max(1, LANES // width)

    def transpose_block(number, carry):
        p = number * span
        for lane in range(0, max(width, LANES), LANES):
            start = pl.multiple_of(p * width + lane, LANES)
            tile = jnp.concatenate(
                [mix_ref[p + i, :, lane : lane + min(width, LANES)] for i in range(span)], axis=1
            )
            turned = jnp.concatenate([tile, tile], axis=0).T
            table_ref[pl.ds(start, LANES), :] = turned
            table_ref[pl.ds(rows + start, LANES), :] = -turned
        return carry

    for number, piece in enumerate(pieces):
        piece.wait()
        count = peers // 2 // span
        lax.fori_loop(number * count, (number + 1) * count, transpose_block, 0)
    first_half = lax.broadcasted_iota(jnp.int32, (1, LANES), 1) < LANES // 2

    def gather_block(r, carry):
        mask = jnp.int32(0)
        for bit in range(bits):
            mask = mask | (((r >> bit) & 1) << (bits - 1 - bit))
        source = (me ^ mask) * (2 * half)
        target = pl.multiple_of(r * half, half)
        for j in range(half):
            upper = table_ref[pl.ds(code_ref[source + j], 1), :]
            lower = table_ref[pl.ds(code_ref[source + half + j], 1), :]
            out_ref[pl.ds(target + j, 1), :] = jnp.where(first_half, upper, lower)
        return carry

    lax.fori_loop(0, 1 << bits, gather_block, 0)


def sampled_terms(mix, code, me, bits, half):
    rows = mix.shape[0] * mix.shape[2]
    count = half << bits
    return pl.pallas_call(
        functools.partial(terms_kernel, bits, half),
        in_specs=[pl.BlockSpec(memory_space=pltpu.SMEM)] * 2
        + [pl.BlockSpec(memory_space=pltpu.HBM)],
        out_specs=pl.BlockSpec(memory_space=pltpu.VMEM),
        out_shape=jax.ShapeDtypeStruct((count, LANES), jnp.float32),
        scratch_shapes=[
            pltpu.VMEM(mix.shape, jnp.float32),
            pltpu.VMEM((2 * rows, LANES), jnp.float32),
            pltpu.SemaphoreType.DMA((2,)),
        ],
        compiler_params=pltpu.CompilerParams(vmem_limit_bytes=40 << 20),
        cost_estimate=pl.CostEstimate(
            flops=count * LANES * 40, bytes_accessed=24 << 20, transcendentals=0
        ),
    )(code, me, in_hbm(mix))


def two_sum(a, b):
    total = a + b
    part = total - a
    return total, (a - (total - part)) + (b - part)


def quick_sum(a, b):
    total = a + b
    return total, b - (total - a)


def pair_add(a, b):
    total, error = two_sum(a[0], b[0])
    return quick_sum(total, error + (a[1] + b[1]))


def halves(a):
    scaled = a * 4097.0
    high = scaled - (scaled - a)
    return high, a - high


def product(a, b, a_parts, b_parts):
    whole = a * b
    error = (a_parts[0] * b_parts[0] - whole) + a_parts[0] * b_parts[1]
    error = (error + a_parts[1] * b_parts[0]) + a_parts[1] * b_parts[1]
    return whole, error


def gram_kernel(scale, terms_ref, picked_ref, gram_ref):
    cols = picked_ref.shape[0]
    turned = terms_ref[...].T
    picked = jnp.concatenate([turned[:cols], turned[cols:]], axis=1)
    picked_ref[...] = picked
    rest = picked * scale
    shift = jnp.max(jnp.abs(rest), axis=1, keepdims=True) * float(1 << 17)
    parts = []
    for _ in range(SLICES):
        part = (rest + shift) - shift
        rest = rest - part
        shift = shift * (1.0 / 64.0)
        parts.append(part.astype(jnp.bfloat16))
    total = None
    for level in range(SLICES):
        left = jnp.concatenate(parts[: level + 1], axis=1)
        right = jnp.concatenate(parts[: level + 1][::-1], axis=1)
        term = lax.dot_general(
            left, right, (((1,), (1,)), ((), ())), preferred_element_type=jnp.float32
        )
        if total is None:
            total = (term, jnp.zeros_like(term))
        else:
            high, error = two_sum(total[0], term)
            total = (high, total[1] + error)
    high, low = quick_sum(*total)
    gram_ref[...] = jnp.concatenate([high, low], axis=1)


def own_gram(terms, cols, per_device, scale):
    return pl.pallas_call(
        functools.partial(gram_kernel, scale),
        grid=(1,),
        in_specs=[whole(terms)],
        out_specs=(
            pl.BlockSpec((cols, per_device), lambda i: (0, 0)),
            pl.BlockSpec((cols, 2 * cols), lambda i: (0, 0)),
        ),
        out_shape=(
            jax.ShapeDtypeStruct((cols, per_device), jnp.float32),
            jax.ShapeDtypeStruct((cols, 2 * cols), jnp.float32),
        ),
        compiler_params=pltpu.CompilerParams(vmem_limit_bytes=8 << 20),
    )(terms)


def tree_sum(values):
    while len(values) > 1:
        values = [pair_add(values[i], values[i + 1]) for i in range(0, len(values), 2)]
    return values[0]


def split_pair(packed):
    cols = packed.shape[0]
    return packed[:, :cols], packed[:, cols:]


def gram_sum_kernel(count, *refs):
    high, low = tree_sum([split_pair(ref[...]) for ref in refs[:count]])
    refs[-1][...] = jnp.concatenate([high, low], axis=1)


def gram_sum(grams, *through):
    count = len(grams)
    in_place = pl.BlockSpec(memory_space=pltpu.HBM)
    return pl.pallas_call(
        functools.partial(gram_sum_kernel, count),
        grid=(1,),
        in_specs=[whole(gram) for gram in grams] + [in_place] * len(through),
        out_specs=tuple([in_place] * len(through) + [whole(grams[0])]),
        out_shape=tuple(
            [pltpu.HBM(v.shape, v.dtype) for v in through]
            + [jax.ShapeDtypeStruct(grams[0].shape, jnp.float32)]
        ),
        input_output_aliases={count + i: i for i in range(len(through))},
        compiler_params=pltpu.CompilerParams(vmem_limit_bytes=8 << 20),
    )(*grams, *through)


def factor_kernel(picked_ref, *refs):
    gram_refs, (r_ref, white_ref) = refs[:-2], refs[-2:]
    cols = r_ref.shape[0]
    high, low = tree_sum([split_pair(ref[...]) for ref in gram_refs])
    row_id = lax.broadcasted_iota(jnp.int32, (cols, cols), 0)
    lane_id = lax.broadcasted_iota(jnp.int32, (cols, cols), 1)
    unit = (row_id == lane_id).astype(jnp.float32)
    wide_high = jnp.concatenate([high, unit], axis=1)
    wide_low = jnp.concatenate([low, jnp.zeros_like(unit)], axis=1)
    tiles = cols // 8
    shape = (8, 2 * cols)
    rows = [
        (wide_high[t * 8 : (t + 1) * 8], wide_low[t * 8 : (t + 1) * 8])
        for t in range(tiles)
    ]
    sub_id = lax.broadcasted_iota(jnp.int32, shape, 0)
    for j in range(cols - 1):
        tile, sub = divmod(j, 8)
        row = [jnp.broadcast_to(v[sub : sub + 1], shape) for v in rows[tile]]
        pivot = [jnp.broadcast_to(v[sub : sub + 1, j : j + 1], shape) for v in rows[tile]]
        first = 1.0 / pivot[0]
        first_parts = halves(first)
        whole, error = product(pivot[0], first, halves(pivot[0]), first_parts)
        gap = ((1.0 - whole) - error) - pivot[1] * first
        inverse = quick_sum(first, first * gap)
        whole, error = product(row[0], inverse[0], halves(row[0]), halves(inverse[0]))
        scaled = quick_sum(whole, error + (row[0] * inverse[1] + row[1] * inverse[0]))
        scaled_parts = halves(scaled[0])
        for t in range(tile, tiles):
            if t == tile and sub == 7:
                continue
            high, low = rows[t]
            column = [jnp.broadcast_to(v[:, j : j + 1], shape) for v in rows[t]]
            if t == tile:
                column = [jnp.where(sub_id > sub, v, 0.0) for v in column]
            whole, error = product(column[0], scaled[0], halves(column[0]), scaled_parts)
            error = error + (column[0] * scaled[1] + column[1] * scaled[0])
            total, missed = two_sum(high, -whole)
            rows[t] = quick_sum(total, missed + (low - error))
    wide_high = jnp.concatenate([v[0] for v in rows], axis=0)
    wide_low = jnp.concatenate([v[1] for v in rows], axis=0)
    wide_row = lax.broadcasted_iota(jnp.int32, wide_high.shape, 0)
    wide_lane = lax.broadcasted_iota(jnp.int32, wide_high.shape, 1)
    diagonal = jnp.sum(jnp.where(wide_row == wide_lane, wide_high, 0.0), axis=1, keepdims=True)
    root = jnp.sqrt(diagonal)
    wide = (wide_high + wide_low) / root
    r_ref[...] = jnp.where(lane_id >= row_id, wide[:, :cols], 0.0)
    white_ref[...] = jnp.dot(
        wide[:, cols:],
        picked_ref[...],
        precision=lax.Precision.HIGHEST,
        preferred_element_type=jnp.float32,
    )


def factor_and_solve(picked, grams):
    cols = picked.shape[0]
    return pl.pallas_call(
        factor_kernel,
        grid=(1,),
        in_specs=[whole(value) for value in (picked, *grams)],
        out_specs=(pl.BlockSpec((cols, cols), lambda i: (0, 0)), whole(picked)),
        out_shape=(
            jax.ShapeDtypeStruct((cols, cols), jnp.float32),
            jax.ShapeDtypeStruct(picked.shape, jnp.float32),
        ),
        compiler_params=pltpu.CompilerParams(vmem_limit_bytes=8 << 20),
    )(picked, *grams)


def xor_permute(value, mask, device_count):
    return lax.ppermute(value, AXES, [(i, i ^ mask) for i in range(device_count)])


def in_groups(masks, size=2):
    odd = len(masks) % size
    groups = [masks[:odd]] if odd else []
    return groups + [masks[i : i + size] for i in range(odd, len(masks), size)]


def combined(masks, q):
    mask = 0
    for bit, value in enumerate(masks):
        if (q >> bit) & 1:
            mask |= value
    return mask


def local(panel, signs, sample_device, sample_offset):
    device_count = lax.axis_size(AXES)
    me = lax.axis_index(AXES).astype(jnp.int32)
    bits = device_count.bit_length() - 1
    cols, rows = panel.shape
    samples = sample_offset.shape[0]
    per_device = samples // device_count
    half = per_device // 2
    masks = [1 << bit for bit in range(bits)]

    signs_row = signs.reshape(1, rows)
    scale = 1.0 / math.sqrt(rows * device_count)

    mix = local_mix(panel, signs_row, scale, device_count)

    def swap(value):
        return lax.all_to_all(value, AXES, split_axis=0, concat_axis=0, tiled=True)

    received_mix = swap(mix)

    common = me & sample_device[:, 0]
    odd = lax.population_count(common) & 1
    code = sample_offset + odd * rows
    total = sampled_terms(mix, code, me.reshape(1), bits, half)
    for group in in_groups(masks):
        block = total.shape[0] >> len(group)
        mine = total[:block]
        for q in range(1, 1 << len(group)):
            mask = combined(group[::-1], q)
            sent = total[q * block : (q + 1) * block]
            mine = mine + xor_permute(sent, mask, device_count)
        total = mine
    picked, gram = own_gram(total, cols, per_device, 1.0 / math.sqrt(samples))
    across = mix_across(received_mix, gram)
    groups = in_groups(masks)[::-1]
    for number, group in enumerate(groups):
        received = [gram] + [
            xor_permute(gram, combined(group, q), device_count) for q in range(1, 1 << len(group))
        ]
        if number == 0:
            across, gram = gram_sum(received, across)
            mixed = lay_out(swap(across))
        elif number < len(groups) - 1:
            (gram,) = gram_sum(received)
    r_factor, whitened = factor_and_solve(picked, received)
    return (mixed, r_factor, whitened)


def solution(mesh):
    return jax.shard_map(
        local,
        mesh=mesh,
        in_specs=(P(None, AXES), P(AXES), P(), P()),
        out_specs=(P(None, AXES), P(), P(None, AXES)),
        check_vma=False,
    )
```
